32 devices in a mesh: section: 2 (over core), dp: 4 (over y, x), seq: 4 (over z).
Axes of the slice: x: 2, y: 2, z: 4, core: 2. Of those that a mesh axis runs over, the one named last changes fastest.
Arguments:
- block_input: float32 [8, 1024, 768], P('dp', 'seq'), may hold values from -6 to 6
- cotangent: float32 [8, 1024, 768], P('dp', 'seq'), may hold values from -6 to 6
- doc_lengths: int32 [8, 4], P('dp'), may hold values from 1 to 832, 1024 in all within a row
- w_qkv: float32 [2, 768, 2304], P('section', ('dp', 'seq'))
- w_out: float32 [2, 768, 768], P('section', ('dp', 'seq'))
- w_fc1: float32 [2, 768, 3072], P('section', ('dp', 'seq'))
- w_fc2: float32 [2, 3072, 768], P('section', ('dp', 'seq'))
- vectors: float32 [2, 16896], P('section', ('dp', 'seq'))
- vector_sq: float32 [2, 16896], P('section', ('dp', 'seq')), may hold values from 1556 to 6225
- rows_small: float32 [2, 3, 768], P('section', None, ('dp', 'seq')), as said below
- rows_fc2: float32 [2, 3072], P('section', ('dp', 'seq')), as said below
- columns: float32 [2, 6912], P('section'), as said below
Outputs:
- activations: float32 [2, 8, 1024, 768], P('section', 'dp', 'seq')
- input_grads: float32 [2, 8, 1024, 768], P('section', 'dp', 'seq')
- grad_qkv: float32 [2, 768, 2304], P('section', ('dp', 'seq'))
- grad_out: float32 [2, 768, 768], P('section', ('dp', 'seq'))
- grad_fc1: float32 [2, 768, 3072], P('section', ('dp', 'seq'))
- grad_fc2: float32 [2, 3072, 768], P('section', ('dp', 'seq'))
- grad_vectors: float32 [2, 16896], P('section', ('dp', 'seq'))
- new_qkv: float32 [2, 768, 2304], P('section', ('dp', 'seq'))
- new_out: float32 [2, 768, 768], P('section', ('dp', 'seq'))
- new_fc1: float32 [2, 768, 3072], P('section', ('dp', 'seq'))
- new_fc2: float32 [2, 3072, 768], P('section', ('dp', 'seq'))
- new_vectors: float32 [2, 16896], P('section', ('dp', 'seq'))
- new_vector_sq: float32 [2, 16896], P('section', ('dp', 'seq'))
- new_rows_small: float32 [2, 3, 768], P('section', None, ('dp', 'seq'))
- new_rows_fc2: float32 [2, 3072], P('section', ('dp', 'seq'))
- new_columns: float32 [2, 6912], P('section')
The draws below stay inside these ranges and needn't reach their ends.
Inputs may be any that keep to these rules, and one draw needn't show every extreme that they name: `doc_lengths`: the lengths of a row sum to 1024; in every row one document has the largest length. `rows_small`: positive. `rows_fc2`: positive. `columns`: positive.
All inputs are finite; a program needn't handle non-finite values.
Results may differ from the reference program's by a relative error of at most 0.028.
Values may be sent and summed in bfloat16 or wider, within the bound.
A program may use at most 256 MiB of HBM per device.

```python
import math
import jax
import jax.numpy as jnp
import numpy as np
from jax import lax

D = 768
FF = 3072
HEADS = 12
HEAD_DIM = 64
NDOC = 4
STEP = 10
LAYERS = 2
SEQS = 8
LEN = 1024
TOKENS = 8192
NV = 16896


def ramped_weight(key, rows_total, cols_total, fan_in):
    ramp = jnp.exp(jnp.linspace(jnp.log(0.6), jnp.log(1.8), rows_total)).astype(jnp.float32)
    base = jnp.clip(jax.random.normal(key, (LAYERS, rows_total, cols_total), jnp.float32), -4.0, 4.0)
    return base * ramp[None, :, None] * fan_in ** (-0.5)


def state_entries(key, shape, level):
    return level * 0.19 * TOKENS * jax.random.uniform(key, shape, jnp.float32, 1.0, 4.0)


def draw_w_qkv(key, part):
    key = jax.random.fold_in(key, 11)
    return ramped_weight(key, D, 3 * D, D)


def draw_w_out(key, part):
    key = jax.random.fold_in(key, 12)
    return ramped_weight(key, D, D, D)


def draw_w_fc1(key, part):
    key = jax.random.fold_in(key, 13)
    return ramped_weight(key, D, FF, D)


def draw_w_fc2(key, part):
    key = jax.random.fold_in(key, 14)
    return ramped_weight(key, FF, D, FF)


def draw_vectors(key, part):
    key = jax.random.fold_in(key, 15)
    gain_slots = [0, 4, 7, 11]
    widths_list = [D] * 10 + [FF] * 3
    pieces = []
    for slot, span_size in enumerate(widths_list):
        sub_key = jax.random.fold_in(key, slot)
        if slot in gain_slots:
            ramp = jnp.exp(jnp.linspace(jnp.log(0.6), jnp.log(1.8), span_size)).astype(jnp.float32)
            jitter = jax.random.uniform(sub_key, (LAYERS, span_size), jnp.float32, 0.9, 1.1)
            pieces.append(ramp[None, :] * jitter)
        else:
            pieces.append(0.3 * jnp.clip(jax.random.normal(sub_key, (LAYERS, span_size), jnp.float32), -4.0, 4.0))
    return jnp.concatenate(pieces, axis=1)


def draw_rows_small(key, part):
    key = jax.random.fold_in(key, 16)
    levels = jnp.array([0.25, 1.7, 0.36], jnp.float32)
    return state_entries(key, (LAYERS, 3, D), 1.0) * levels[None, :, None]


def draw_rows_fc2(key, part):
    key = jax.random.fold_in(key, 17)
    return state_entries(key, (LAYERS, FF), 1.44)


def draw_columns(key, part):
    key = jax.random.fold_in(key, 18)
    levels = [0.25, 1.7, 0.36, 1.44]
    widths_list = [3 * D, D, FF, D]
    pieces = []
    for slot in range(4):
        sub_key = jax.random.fold_in(key, slot)
        pieces.append(state_entries(sub_key, (LAYERS, widths_list[slot]), levels[slot]))
    return jnp.concatenate(pieces, axis=1)


def shard_levels(own_key, extent, shards, least, top_value):
    def one(axis_at, blocks):
        draws = jax.random.uniform(jax.random.fold_in(jax.random.fold_in(own_key, 6), axis_at), (blocks,), jnp.float32, least / len(shards), top_value / len(shards))
        return jnp.repeat(jnp.exp(draws), extent[axis_at] // blocks).reshape((-1,) + (1,) * (len(extent) - axis_at - 1))

    level = one(*shards[0])
    for cut in shards[1:]:
        level = level * one(*cut)
    return level


def split_up(amount, total, limit, lean):
    loads = [(1 << 20) // math.isqrt(grade ** lean) + 1 for grade in range(2, amount + 1)]
    rest, holding = total - limit - (amount - 1), [1] * (amount - 1)
    while rest > 0:
        movable = [i for i in range(amount - 1) if holding[i] < limit]
        mass, left = sum([loads[i] for i in movable]), rest
        for i in movable:
            more = min(limit - holding[i], max(1, left * loads[i] // mass), rest)
            holding[i] = holding[i] + more
            rest = rest - more
    return np.array([limit] + holding)


def uneven_parts(key, number_of, total, bound, skew):
    if number_of == 2:
        one = jax.random.randint(key, (), max(1, total - bound), min(bound, total - 1) + 1)
        return jnp.stack([one, total - one])
    tallies = jnp.asarray(split_up(number_of, total, bound, skew), jnp.int32)
    couples = (number_of - 1) // 2
    source_of, taker = tallies[1:1 + 2 * couples:2], tallies[2:2 + 2 * couples:2]
    slack = jnp.minimum(source_of - 1, bound - taker)
    moved = jax.random.randint(jax.random.fold_in(key, 1), (couples,), 0, 1 << 20) % (slack + 1)
    tallies = tallies.at[1:1 + 2 * couples:2].set(source_of - moved).at[2:2 + 2 * couples:2].set(taker + moved)
    return tallies[jax.random.permutation(jax.random.fold_in(key, 2), number_of)]


def gaussian(stream_key, shape, spread, reach, cuts=(), kind=jnp.bfloat16):
    level = shard_levels(stream_key, shape, cuts, -0.22, 0.18) if cuts else 1.0
    values = jax.random.normal(stream_key, shape, jnp.float32) * spread * level
    return jnp.minimum(jnp.maximum(values, -reach), reach).astype(kind)


def setup_inputs(seed: int = 0) -> dict:
    streams_of = jax.random.split(jax.random.key(seed), 13)
    block_input = gaussian(streams_of[0], (SEQS, LEN, D), 1.0, 6.0, ((0, 4), (1, 4)), jnp.float32)
    cotangent = gaussian(streams_of[1], (SEQS, LEN, D), 1.0, 6.0, ((0, 4), (1, 4)), jnp.float32)
    doc_lengths = jax.vmap(lambda own: uneven_parts(own, NDOC, LEN, LEN - 3 * LEN // 16, 0))(jax.random.split(streams_of[2], SEQS)).reshape((SEQS, NDOC)).astype(jnp.int32)
    w_qkv = draw_w_qkv(jax.random.fold_in(streams_of[12], 71), 0)
    w_out = draw_w_out(jax.random.fold_in(streams_of[12], 71), 0)
    w_fc1 = draw_w_fc1(jax.random.fold_in(streams_of[12], 71), 0)
    w_fc2 = draw_w_fc2(jax.random.fold_in(streams_of[12], 71), 0)
    vectors = draw_vectors(jax.random.fold_in(streams_of[12], 71), 0)
    vector_sq = jnp.clip(jnp.exp(math.log(6225.0) - 1.386455 * jax.random.uniform(streams_of[8], (LAYERS, NV), jnp.float32) ** shard_levels(streams_of[8], (LAYERS, NV), ((0, 2), (1, 16)), -0.2, 0.2)), 1556.0, 6225.0)
    rows_small = draw_rows_small(jax.random.fold_in(streams_of[12], 71), 0)
    rows_fc2 = draw_rows_fc2(jax.random.fold_in(streams_of[12], 71), 0)
    columns = draw_columns(jax.random.fold_in(streams_of[12], 71), 0)
    return dict(block_input=block_input, cotangent=cotangent, doc_lengths=doc_lengths, w_qkv=w_qkv, w_out=w_out, w_fc1=w_fc1, w_fc2=w_fc2, vectors=vectors, vector_sq=vector_sq, rows_small=rows_small, rows_fc2=rows_fc2, columns=columns)


EPSILON = 1e-05
LEARN_RATE = 0.5
CLIP_LEVEL = 1.0
HIGHEST = lax.Precision.HIGHEST
NEG_LARGE = -1e+30

@jax.custom_vjp
def low(v):
    return lax.optimization_barrier(v.astype(jnp.bfloat16)).astype(jnp.float32)

@jax.custom_vjp
def low_back(v):
    return v

def low_keep(v):
    return (low(v), None)

def low_pass(kept, grad):
    return (grad,)

def back_keep(v):
    return (v, None)

def back_low(kept, grad):
    return (low(grad),)
low.defvjp(low_keep, low_pass)
low_back.defvjp(back_keep, back_low)

def layer_norm(values, ln_gain, ln_bias):
    average = lax.optimization_barrier(jnp.mean(values, axis=-1, keepdims=True))
    centred = values - average
    variance = lax.optimization_barrier(jnp.mean(centred * centred, axis=-1, keepdims=True))
    return centred * lax.rsqrt(variance + EPSILON) * ln_gain + ln_bias

def segment_widths():
    return [D] * 10 + [FF] * 3

def split_vectors(packed):
    pieces = []
    offset = 0
    for span_size in segment_widths():
        pieces.append(packed[offset:offset + span_size])
        offset += span_size
    return pieces

def allowed_mask(lengths_row, positions):
    bounds = jnp.cumsum(lengths_row)
    doc_ids = lax.optimization_barrier(jnp.sum((positions[:, None] >= bounds[None, :]).astype(jnp.int32), axis=1))
    same_doc = doc_ids[:, None] == doc_ids[None, :]
    return same_doc & (positions[None, :] <= positions[:, None])

def heads_of(values):
    return values.reshape(values.shape[0], HEADS, HEAD_DIM)

def block_layer(inputs, params, allowed):
    w_qkv, w_out, w_fc1, w_fc2, packed = params
    w_qkv = low(w_qkv)
    w_out = low(w_out)
    w_fc1 = low(w_fc1)
    w_fc2 = low(w_fc2)
    parts = split_vectors(low(packed))
    normed = low(layer_norm(inputs, parts[0], parts[1]))
    projected = jnp.dot(normed, w_qkv, precision=HIGHEST)
    queries = low_back(low(projected[:, :D] + parts[2]))
    keys_all = low_back(low(projected[:, D:2 * D]))
    values_all = low_back(low(projected[:, 2 * D:] + parts[3]))
    raw = jnp.einsum('qhd,khd->hqk', heads_of(queries), heads_of(keys_all), precision=HIGHEST) * HEAD_DIM ** (-0.5)
    scores = low_back(raw)
    masked = jnp.where(allowed[None], scores, NEG_LARGE)
    top = lax.optimization_barrier(jnp.max(masked, axis=-1, keepdims=True))
    expo = jnp.exp(masked - top)
    probs = low(expo / lax.optimization_barrier(jnp.sum(expo, axis=-1, keepdims=True)))
    attended = jnp.einsum('hqk,khd->qhd', probs, heads_of(values_all), precision=HIGHEST)
    attended = low_back(attended.reshape(inputs.shape[0], D))
    sub_normed = low(layer_norm(attended, parts[4], parts[5]))
    branch = low_back(jnp.dot(sub_normed, w_out, precision=HIGHEST) + parts[6])
    middle = inputs + branch
    normed_two = low(layer_norm(middle, parts[7], parts[8]))
    hidden_pre = low_back(jnp.dot(normed_two, w_fc1, precision=HIGHEST) + parts[10])
    hidden = low(layer_norm(jax.nn.gelu(hidden_pre, approximate=False), parts[11], parts[12]))
    ffn_branch = low_back(jnp.dot(hidden, w_fc2, precision=HIGHEST) + parts[9])
    return middle + ffn_branch

def adafactor_matrix(grad_mat, master, row_old, col_old, decay):
    squares = grad_mat * grad_mat
    row_new = decay * row_old + (1.0 - decay) * lax.optimization_barrier(jnp.mean(squares, axis=1))
    col_new = decay * col_old + (1.0 - decay) * lax.optimization_barrier(jnp.mean(squares, axis=0))
    estimate = row_new[:, None] * col_new[None, :] / jnp.mean(row_new)
    update = grad_mat * lax.rsqrt(estimate)
    rms_update = jnp.sqrt(jnp.mean(update * update))
    rms_master = jnp.sqrt(jnp.mean(master * master))
    new_master = master - LEARN_RATE * rms_master / jnp.maximum(1.0, rms_update / CLIP_LEVEL) * update
    return (new_master, row_new, col_new)

def adafactor_vector(grad_vec, master, sq_old, decay):
    sq_new = decay * sq_old + (1.0 - decay) * grad_vec * grad_vec
    update = grad_vec * lax.rsqrt(sq_new)
    pieces = []
    offset = 0
    for span_size in segment_widths():
        seg_update = update[offset:offset + span_size]
        seg_master = master[offset:offset + span_size]
        rms_update = jnp.sqrt(jnp.mean(seg_update * seg_update))
        rms_master = jnp.sqrt(jnp.mean(seg_master * seg_master))
        pieces.append(seg_master - LEARN_RATE * rms_master / jnp.maximum(1.0, rms_update / CLIP_LEVEL) * seg_update)
        offset += span_size
    return (jnp.concatenate(pieces), sq_new)

def reference(block_input, cotangent, doc_lengths, w_qkv, w_out, w_fc1, w_fc2, vectors, vector_sq, rows_small, rows_fc2, columns):
    positions = jnp.arange(LEN, dtype=jnp.int32)
    params_one = (w_qkv[0], w_out[0], w_fc1[0], w_fc2[0], vectors[0])
    params_two = (w_qkv[1], w_out[1], w_fc1[1], w_fc2[1], vectors[1])
    start_totals = jax.tree.map(lambda leaf_array: jnp.zeros(leaf_array.shape, jnp.float32), (params_one, params_two))

    def per_row(totals, row_items):
        row_input, row_cot, row_lengths = row_items
        allowed = allowed_mask(row_lengths, positions)

        def apply_layer(inputs, params):
            return block_layer(inputs, params, allowed)
        out_one, back_one = jax.vjp(apply_layer, row_input, params_one)
        out_two, back_two = jax.vjp(apply_layer, out_one, params_two)
        grad_mid, grads_two = back_two(row_cot)
        grad_in, grads_one = back_one(grad_mid)
        totals = jax.tree.map(jnp.add, totals, (grads_one, grads_two))
        return (totals, (out_one, out_two, grad_in, grad_mid))
    totals, row_outputs = lax.scan(per_row, start_totals, (block_input, cotangent, doc_lengths))
    out_one, out_two, grad_in, grad_mid = row_outputs
    activations = jnp.stack([out_one, out_two])
    input_grads = jnp.stack([grad_in, grad_mid])
    grads = [jnp.stack([totals[0][index], totals[1][index]]) for index in range(5)]
    decay = 1.0 - STEP ** (-0.8)
    masters = [w_qkv, w_out, w_fc1, w_fc2]
    col_widths = [3 * D, D, FF, D]
    new_mats = [[], [], [], []]
    new_rows = [[], [], [], []]
    new_cols = []
    new_vecs = []
    new_sqs = []
    for layer_pos in range(LAYERS):
        row_olds = [rows_small[layer_pos, 0], rows_small[layer_pos, 1], rows_small[layer_pos, 2], rows_fc2[layer_pos]]
        col_pieces = []
        offset = 0
        for index in range(4):
            col_old = columns[layer_pos, offset:offset + col_widths[index]]
            offset += col_widths[index]
            new_master, row_new, col_new = adafactor_matrix(grads[index][layer_pos], masters[index][layer_pos], row_olds[index], col_old, decay)
            new_mats[index].append(new_master)
            new_rows[index].append(row_new)
            col_pieces.append(col_new)
        new_cols.append(jnp.concatenate(col_pieces))
        new_vec, new_sq = adafactor_vector(grads[4][layer_pos], vectors[layer_pos], vector_sq[layer_pos], decay)
        new_vecs.append(new_vec)
        new_sqs.append(new_sq)
    new_rows_small = jnp.stack([jnp.stack([new_rows[0][layer_pos], new_rows[1][layer_pos], new_rows[2][layer_pos]]) for layer_pos in range(LAYERS)])
    return (activations, input_grads, grads[0], grads[1], grads[2], grads[3], grads[4], jnp.stack(new_mats[0]), jnp.stack(new_mats[1]), jnp.stack(new_mats[2]), jnp.stack(new_mats[3]), jnp.stack(new_vecs), jnp.stack(new_sqs), new_rows_small, jnp.stack(new_rows[3]), jnp.stack(new_cols))
```

```python
import functools

import jax
import jax.numpy as jnp
import numpy as np
from jax import lax
from jax.experimental import pallas as pl
from jax.experimental.pallas import tpu as pltpu
from jax.sharding import PartitionSpec as P

D = 768
FF = 3072
HEADS = 12
HEAD_DIM = 64
STEP = 10
GROUP = 4
GW = D // GROUP
CHUNK_HEADS = HEADS // GROUP

EPSILON = 1e-05
LEARN_RATE = 0.5
CLIP_LEVEL = 1.0
HIGHEST = lax.Precision.HIGHEST
NEG_LARGE = -1e30
MESH = pl.DeviceIdType.MESH
BF = jnp.bfloat16
F32 = jnp.float32


def layer_norm(values, ln_gain, ln_bias):
    average = jnp.mean(values, axis=-1, keepdims=True)
    centred = values - average
    variance = jnp.mean(centred * centred, axis=-1, keepdims=True)
    return centred * lax.rsqrt(variance + EPSILON) * ln_gain + ln_bias


def ffn_inner(hidden_pre, ln_gain, ln_bias):
    return layer_norm(jax.nn.gelu(hidden_pre, approximate=False), ln_gain, ln_bias)


def segment_widths():
    return [D] * 10 + [FF] * 3


def split_vectors(packed):
    pieces = []
    offset = 0
    for span_size in segment_widths():
        pieces.append(packed[offset : offset + span_size])
        offset += span_size
    return pieces


def outer_sum(left, right, kind=F32):
    return lax.dot_general(
        left, right, (((0,), (0,)), ((), ())), preferred_element_type=F32
    ).astype(kind)


def back_project(grads, weight):
    return lax.dot_general(
        grads, weight, (((1,), (1,)), ((), ())), preferred_element_type=F32
    )


def column_total(values_b):
    return jnp.sum(values_b.astype(F32), axis=0)


def dp_bits(count):
    return [1 << i for i in range(count.bit_length() - 1)]


def bit_orders(count):
    bits = dp_bits(count)
    half = len(bits) // 2
    return (bits, bits[half:] + bits[:half])


def subsets(bits):
    found = [0]
    for bit in bits:
        found = found + [m | bit for m in found]
    return sorted(found)


class Copies:
    def __init__(self, send, recv):
        self.send, self.recv, self.used, self.started = send, recv, 0, []

    def go(self, src, dst, device):
        at = self.used
        self.used += 1
        copy = pltpu.make_async_remote_copy(
            src_ref=src,
            dst_ref=dst,
            send_sem=self.send.at[at],
            recv_sem=self.recv.at[at],
            device_id=device,
            device_id_type=MESH,
        )
        copy.start()
        self.started.append(copy)
        return copy

    def finish(self):
        for copy in self.started:
            copy.wait_send()


def greet(peers):
    barrier = pltpu.get_barrier_semaphore()
    for peer in peers:
        pl.semaphore_signal(barrier, inc=1, device_id=peer, device_id_type=MESH)
    pl.semaphore_wait(barrier, len(peers))


def coords():
    return lax.axis_index("section"), lax.axis_index("dp"), lax.axis_index("seq")


def near_peers(c, dp, z, DP, S):
    return (
        [(1 - c, dp, z)]
        + [(c, dp, z ^ k) for k in range(1, S)]
        + [(c, dp ^ b, z) for b in dp_bits(DP)]
    )


def half_lanes(c, width):
    return pl.ds(pl.multiple_of(c * width, 128), width)


def sub_lanes(c, width, a):
    return pl.ds(pl.multiple_of(c * width + a * (width // 2), 128), width // 2)


def gather_kernel(DP, S, *refs):
    ins, (vec,), outs, (ovec, send, recv, local) = refs[:6], refs[6:7], refs[7:13], refs[13:]
    c, dp, z = coords()
    greet(near_peers(c, dp, z, DP, S))
    copies = Copies(send, recv)
    order_a, order_b = bit_orders(DP)

    def cut(ref, lead, kind, part):
        if kind == "row":
            rows = pl.ds(2 * c, 2) if part is None else pl.ds(2 * c + part, 1)
            return ref.at[lead + (rows,)]
        lanes = half_lanes(c, FF // 2) if part is None else sub_lanes(c, FF // 2, part)
        return ref.at[lead + (slice(None), lanes)]

    kinds = ["col", "col", "row"] * 2
    locals_ = []
    for g in range(6):
        own = pltpu.make_async_copy(
            cut(ins[g], (), kinds[g], None), cut(outs[g], (dp, z), kinds[g], None), local.at[g]
        )
        own.start()
        locals_.append(own)
    own_vec = pltpu.make_async_copy(vec, ovec.at[c, dp, z], local.at[6])
    own_vec.start()

    def across(g):
        return [
            copies.go(
                cut(ins[g], (), kinds[g], None),
                cut(outs[g], (dp, z), kinds[g], None),
                (c, dp, z ^ k),
            )
            for k in range(1, S)
        ]

    def beside(g, step):
        found = []
        for part, order in ((0, order_a), (1, order_b)):
            peer = (c, dp ^ order[step], z)
            for m in subsets(order[:step]):
                place = cut(outs[g], (dp ^ m, slice(None)), kinds[g], part)
                found.append(copies.go(place, place, peer))
        return found

    def over_first(g):
        place = cut(outs[g], (dp, slice(None)), kinds[g], None)
        return [copies.go(place, place, (1 - c, dp, z))]

    def over(g, step):
        found = []
        for part, order in ((0, order_a), (1, order_b)):
            for m in subsets(order[:step]):
                place = cut(outs[g], (dp ^ m ^ order[step], slice(None)), kinds[g], part)
                found.append(copies.go(place, place, (1 - c, dp, z)))
        return found

    def arrive(some):
        for copy in some:
            copy.wait_recv()

    steps = len(order_a)
    forwarded = []
    vec_copies = [copies.go(vec, ovec.at[c, dp, z], (c, dp, z ^ k)) for k in range(1, S)]
    cross = [None] * 7
    cross[0] = across(0)
    own_vec.wait()
    arrive(vec_copies)
    for step in range(steps):
        moved = []
        for m in subsets(order_a[:step]):
            place = ovec.at[c, dp ^ m]
            moved.append(copies.go(place, place, (c, dp ^ order_a[step], z)))
        arrive(moved)
    forwarded.append(copies.go(ovec.at[c], ovec.at[c], (1 - c, dp, z)))

    def enter(g):
        locals_[g].wait()
        arrive(cross[g])
        started = beside(g, 0)
        if g + 1 < 6:
            cross[g + 1] = across(g + 1)
        forwarded.extend(over_first(g))
        return started

    flight = [None] * 6
    flight[0] = enter(0)
    last = [None] * 6
    for g in range(6):
        for step in range(1, steps):
            arrive(flight[g])
            flight[g] = beside(g, step)
            forwarded.extend(over(g, step - 1))
        last[g] = flight[g]
        if g + 1 < 6:
            flight[g + 1] = enter(g + 1)
        if g > 0:
            arrive(last[g - 1])
            forwarded.extend(over(g - 1, steps - 1))
    arrive(last[5])
    forwarded.extend(over(5, steps - 1))
    arrive(forwarded)
    copies.finish()


def gather_all(shards, vec, DP, S):
    rows = shards[0].shape[0]
    col = jax.ShapeDtypeStruct((DP, S, rows, FF), BF)
    row = jax.ShapeDtypeStruct((DP, S, 4, rows, D), BF)
    pieces = 2 * (DP - 1)
    amount = 6 * (S - 1 + 1 + 2 * pieces) + (S - 1) + (DP - 1) + 1
    anywhere = pl.BlockSpec(memory_space=pl.ANY)
    return pl.pallas_call(
        functools.partial(gather_kernel, DP, S),
        out_shape=(col, col, row, col, col, row, jax.ShapeDtypeStruct((2, DP, S) + vec.shape, F32)),
        in_specs=[anywhere] * 7,
        out_specs=(anywhere,) * 7,
        scratch_shapes=[
            pltpu.SemaphoreType.DMA((amount,)),
            pltpu.SemaphoreType.DMA((amount,)),
            pltpu.SemaphoreType.DMA((7,)),
        ],
        compiler_params=pltpu.CompilerParams(collective_id=0, has_side_effects=True),
        name="gather_weights",
    )(*shards, vec)


def scatter_kernel(DP, S, counts, *refs):
    g2, g1, gq, go = refs[:4]
    o2, o1, oq, oo = refs[4:8]
    k2, k1, kq, ko, c2, c1, co = refs[8:15]
    rest = refs[15:]
    send, recv, local = rest[-3:]
    bufs = rest[:-3]
    c, dp, z = coords()
    greet(near_peers(c, dp, z, DP, S))
    copies = Copies(send, recv)
    order_a, order_b = bit_orders(DP)
    sibling = (1 - c, dp, z)
    steps = len(order_a)
    everything = slice(None)

    lanes_mine, lanes_other = half_lanes(c, FF // 2), half_lanes(1 - c, FF // 2)
    lo_mine, lo_other = half_lanes(c, D // 2), half_lanes(1 - c, D // 2)
    plan = [
        (
            [(g2.at[:, :, pl.ds(2 * c, 2)], k2)],
            [(g2.at[:, :, pl.ds(2 * (1 - c), 2)], c2)],
        ),
        (
            [(g1.at[:, :, :, lanes_mine], k1)],
            [(g1.at[:, :, :, lanes_other], c1)],
        ),
        (
            [(gq, kq), (go.at[:, :, :, lo_mine], ko)],
            [(go.at[:, :, :, lo_other], co)],
        ),
    ]
    at_local = 0
    mine, theirs = [], []
    for keep, give in plan:
        mine.append([])
        for src, dst in keep:
            own = pltpu.make_async_copy(src, dst, local.at[at_local])
            own.start()
            at_local += 1
            mine[-1].append(own)
        theirs.append([copies.go(src, dst, sibling) for src, dst in give])

    def add(into, lead, cutter, other, other_lead):
        def one(s, carry):
            place = lead + (s,) + cutter
            into[place] = into[place] + other[other_lead + (s,)]
            return carry

        lax.fori_loop(0, S, one, 0)

    parts = [
        [(k2, (pl.ds(0, 1),), order_a), (k2, (pl.ds(1, 1),), order_b)],
        [
            (k1, (everything, pl.ds(0, FF // 4)), order_a),
            (k1, (everything, pl.ds(FF // 4, FF // 4)), order_b),
        ],
        [(kq, (), order_a), (ko, (), order_b)],
    ]
    joins = [(k2, c2), (k1, c1), (ko, co)]

    def join(g):
        for copy in mine[g]:
            copy.wait()
        for copy in theirs[g]:
            copy.wait_recv()
        into, other = joins[g]

        def one(s, carry):
            for d in range(DP):
                into[d, s] = into[d, s] + other[d, s]
            return carry

        lax.fori_loop(0, S, one, 0)

    at_buf = 0
    slots = []
    for g in range(3):
        slots.append([])
        for part in range(2):
            slots[g].append(bufs[at_buf : at_buf + steps + 1])
            at_buf += steps + 1

    def beside(g, step):
        found = []
        for part, (keep, cutter, order) in enumerate(parts[g]):
            bit = order[step]
            remain = subsets(order[step + 1 :])
            for slot, m in enumerate(remain):
                found.append(
                    copies.go(
                        keep.at[(dp ^ m ^ bit, everything) + cutter],
                        slots[g][part][step].at[slot],
                        (c, dp ^ bit, z),
                    )
                )
        return found

    def merge(g, step, some):
        for copy in some:
            copy.wait_recv()
        for part, (keep, cutter, order) in enumerate(parts[g]):
            for slot, m in enumerate(subsets(order[step + 1 :])):
                add(keep, (dp ^ m,), cutter, slots[g][part][step], (slot,))

    def across(g):
        found = []
        for part, (keep, cutter, order) in enumerate(parts[g]):
            for k in range(1, S):
                found.append(
                    copies.go(
                        keep.at[(dp, z ^ k) + cutter],
                        slots[g][part][steps].at[k - 1],
                        (c, dp, z ^ k),
                    )
                )
        return found

    def close(g, some):
        for copy in some:
            copy.wait_recv()
        for part, (keep, cutter, order) in enumerate(parts[g]):
            got = slots[g][part][steps]
            own = keep[(dp, z) + cutter].astype(F32)
            if g == 2 and part == 0:
                oq[0] = own
                for k in range(1, S):
                    oq[k] = got[k - 1].astype(F32)
                continue
            total = own
            for k in range(1, S):
                total = total + got[k - 1].astype(F32)
            if g == 0:
                o2[pl.ds(part, 1)] = total
            elif g == 1:
                o1[:, pl.ds(part * (FF // 4), FF // 4)] = total
            else:
                oo[...] = total

    flight = [None] * 3
    ending = [None] * 3
    join(0)
    flight[0] = beside(0, 0)
    join(1)
    for g in range(3):
        for step in range(steps):
            merge(g, step, flight[g])
            if step + 1 < steps:
                flight[g] = beside(g, step + 1)
            else:
                ending[g] = across(g)
            if step == 0 and g + 1 < 3:
                flight[g + 1] = beside(g + 1, 0)
                if g + 2 < 3:
                    join(g + 2)
        if g > 0:
            close(g - 1, ending[g - 1])
    close(2, ending[2])
    copies.finish()


def scatter_layer(grads, DP, S, collective_id):
    g2, g1, gq, go = grads
    rows = g1.shape[2]
    steps = len(dp_bits(DP))
    cols = [[(1, rows, D)] * 2, [(rows, FF // 4)] * 2, [(rows, 3 * GW), (rows, D // 2)]]
    slots = []
    for pair in cols:
        for tail in pair:
            for step in range(steps):
                slots.append(pltpu.VMEM((DP >> (step + 1), S) + tail, BF))
            slots.append(pltpu.VMEM((S - 1,) + tail, BF))
    amount = 3 + 6 * (DP - 1) + 6 * (S - 1)
    anywhere = pl.BlockSpec(memory_space=pl.ANY)
    vmem = pl.BlockSpec(memory_space=pltpu.VMEM)
    return pl.pallas_call(
        functools.partial(scatter_kernel, DP, S, None),
        out_shape=(
            jax.ShapeDtypeStruct((2, rows, D), F32),
            jax.ShapeDtypeStruct((rows, FF // 2), F32),
            jax.ShapeDtypeStruct((S, rows, 3 * GW), F32),
            jax.ShapeDtypeStruct((rows, D // 2), F32),
        ),
        in_specs=[anywhere] * 4,
        out_specs=(vmem,) * 4,
        scratch_shapes=[
            pltpu.VMEM((DP, S, 2, rows, D), BF),
            pltpu.VMEM((DP, S, rows, FF // 2), BF),
            pltpu.VMEM((DP, S, rows, 3 * GW), BF),
            pltpu.VMEM((DP, S, rows, D // 2), BF),
            pltpu.VMEM((DP, S, 2, rows, D), BF),
            pltpu.VMEM((DP, S, rows, FF // 2), BF),
            pltpu.VMEM((DP, S, rows, D // 2), BF),
        ]
        + slots
        + [
            pltpu.SemaphoreType.DMA((amount,)),
            pltpu.SemaphoreType.DMA((amount,)),
            pltpu.SemaphoreType.DMA((4,)),
        ],
        compiler_params=pltpu.CompilerParams(
            collective_id=collective_id, has_side_effects=True, vmem_limit_bytes=48 << 20
        ),
        name="scatter_grads",
    )(g2, g1, gq, go)


def attend_kernel(start_ref, qkv_ref, o_ref, lse_ref):
    length = qkv_ref.shape[0]
    block = 256
    for h in range(CHUNK_HEADS):
        for at in range(length // block):
            rows = slice(at * block, (at + 1) * block)
            upto = (at + 1) * block
            q = qkv_ref[rows, h * HEAD_DIM : (h + 1) * HEAD_DIM]
            k = qkv_ref[0:upto, GW + h * HEAD_DIM : GW + (h + 1) * HEAD_DIM]
            v = qkv_ref[0:upto, 2 * GW + h * HEAD_DIM : 2 * GW + (h + 1) * HEAD_DIM]
            s = lax.dot_general(
                q, k, (((1,), (1,)), ((), ())), preferred_element_type=F32
            ) * HEAD_DIM ** (-0.5)
            key = lax.broadcasted_iota(jnp.int32, (block, upto), 1)
            query = lax.broadcasted_iota(jnp.int32, (block, upto), 0) + at * block
            ok = (key >= start_ref[rows, :]) & (key <= query)
            s = jnp.where(ok, s, NEG_LARGE)
            top = jnp.max(s, axis=1, keepdims=True)
            e = jnp.exp(s - top)
            total = jnp.sum(e, axis=1, keepdims=True)
            o = lax.dot_general(
                e.astype(BF), v, (((1,), (0,)), ((), ())), preferred_element_type=F32
            )
            o_ref[rows, h * HEAD_DIM : (h + 1) * HEAD_DIM] = (o / total).astype(o_ref.dtype)
            lse_ref[rows, h : h + 1] = top + jnp.log(total)


def attend(start, qkv):
    length = qkv.shape[0]
    return pl.pallas_call(
        attend_kernel,
        out_shape=(
            jax.ShapeDtypeStruct((length, GW), BF),
            jax.ShapeDtypeStruct((length, CHUNK_HEADS), F32),
        ),
        compiler_params=pltpu.CompilerParams(vmem_limit_bytes=48 << 20),
        name="attend",
    )(start, qkv)


def attend_back_kernel(start_ref, qkv_ref, o_ref, do_ref, lse_ref, dqkv_ref, dk_acc, dv_acc):
    length = qkv_ref.shape[0]
    block = 256
    scale = HEAD_DIM ** (-0.5)
    for h in range(CHUNK_HEADS):
        lanes = slice(h * HEAD_DIM, (h + 1) * HEAD_DIM)
        klanes = slice(GW + h * HEAD_DIM, GW + (h + 1) * HEAD_DIM)
        vlanes = slice(2 * GW + h * HEAD_DIM, 2 * GW + (h + 1) * HEAD_DIM)
        for at in reversed(range(length // block)):
            rows = slice(at * block, (at + 1) * block)
            upto = (at + 1) * block
            q = qkv_ref[rows, lanes]
            k = qkv_ref[0:upto, klanes]
            v = qkv_ref[0:upto, vlanes]
            do = do_ref[rows, lanes]
            o = o_ref[rows, lanes]
            delta = jnp.sum(do.astype(F32) * o.astype(F32), axis=1, keepdims=True)
            s = (
                lax.dot_general(q, k, (((1,), (1,)), ((), ())), preferred_element_type=F32)
                * scale
            )
            key = lax.broadcasted_iota(jnp.int32, (block, upto), 1)
            query = lax.broadcasted_iota(jnp.int32, (block, upto), 0) + at * block
            ok = (key >= start_ref[rows, :]) & (key <= query)
            p = jnp.exp(jnp.where(ok, s, NEG_LARGE) - lse_ref[rows, h : h + 1])
            dp = lax.dot_general(do, v, (((1,), (1,)), ((), ())), preferred_element_type=F32)
            ds = (p * (dp - delta)).astype(BF)
            dq = lax.dot_general(ds, k, (((1,), (0,)), ((), ())), preferred_element_type=F32)
            dqkv_ref[rows, lanes] = (dq * scale).astype(BF)
            dk = lax.dot_general(ds, q, (((0,), (0,)), ((), ())), preferred_element_type=F32)
            dv = lax.dot_general(
                p.astype(BF), do, (((0,), (0,)), ((), ())), preferred_element_type=F32
            )
            if at == length // block - 1:
                dk_acc[...] = dk
                dv_acc[...] = dv
            else:
                dk_acc[0:upto, :] += dk
                dv_acc[0:upto, :] += dv
        dqkv_ref[:, klanes] = (dk_acc[...] * scale).astype(BF)
        dqkv_ref[:, vlanes] = dv_acc[...].astype(BF)


def attend_back(start, qkv, o, do, lse):
    length = qkv.shape[0]
    return pl.pallas_call(
        attend_back_kernel,
        out_shape=jax.ShapeDtypeStruct((length, 3 * GW), BF),
        scratch_shapes=[pltpu.VMEM((length, HEAD_DIM), F32)] * 2,
        compiler_params=pltpu.CompilerParams(vmem_limit_bytes=48 << 20),
        name="attend_back",
    )(start, qkv, o, do, lse)


def local(DP, S, *args):
    (
        block_input,
        cotangent,
        doc_lengths,
        w_qkv,
        w_out,
        w_fc1,
        w_fc2,
        vectors,
        vector_sq,
        rows_small,
        rows_fc2,
        columns,
    ) = args
    c, dp, z = coords()
    first = c == 0
    chunk = block_input.shape[1]
    length = chunk * S
    R = w_qkv.shape[1]
    row = z // (S // 2)
    t = jnp.where(first, z, S - 1 - z)

    zs = range(S)

    def swap_core(value):
        return lax.ppermute(value, "section", [(0, 1), (1, 0)])

    def swap_z(value, k):
        return lax.ppermute(value, "seq", [(i, i ^ k) for i in zs])

    def both(value, route):
        return lax.ppermute(
            value, ("section", "seq"), [(a * S + b, e * S + f) for (a, b), (e, f) in route]
        )

    def absolute(rel, me):
        odd = (me & 1) == 1
        high = (me & 2) == 2
        rel = [jnp.where(odd, rel[i ^ 1], rel[i]) for i in range(GROUP)]
        return [jnp.where(high, rel[i ^ 2], rel[i]) for i in range(GROUP)]

    def exchange(stacked):
        def piece(k):
            return lax.dynamic_index_in_dim(stacked, t ^ k, 0, keepdims=False)

        got1 = swap_z(piece(1), 1)
        got3 = swap_core(piece(3))
        got2 = both(piece(2), [((a, b), (1 - a, b ^ 1)) for a in (0, 1) for b in zs])
        return jnp.stack(absolute([piece(0), got1, got2, got3], t))

    def gather_row(own):
        got1 = swap_z(own, 1)
        got3 = swap_core(own)
        got2 = swap_core(got1)
        return jnp.concatenate(absolute([own, got1, got2, got3], t), axis=0)

    def scatter_row(partial):
        four = partial.reshape(GROUP, chunk, D)

        def piece(k):
            return lax.dynamic_index_in_dim(four, t ^ k, 0, keepdims=False)

        sent = jnp.stack([piece(3), piece(2)]).astype(BF)
        got = swap_core(sent)
        mine = piece(0) + got[0].astype(F32)
        other = piece(1) + got[1].astype(F32)
        return mine + swap_z(other.astype(BF), 1).astype(F32)

    x_row_own = lax.dynamic_index_in_dim(block_input, row, 0, keepdims=False)
    x_row_other = lax.dynamic_index_in_dim(block_input, 1 - row, 0, keepdims=False).astype(BF)
    got1 = swap_z(x_row_own.astype(BF), 1)
    far = both(
        x_row_other,
        [((0, b), (0, b ^ 3)) for b in zs] + [((1, b), (1, b ^ 2)) for b in zs],
    )
    far_other = swap_core(far)
    got3 = jnp.where(first, far, far_other)
    got2 = jnp.where(first, far_other, far)
    x_row = jnp.concatenate(
        absolute([x_row_own, got1.astype(F32), got2.astype(F32), got3.astype(F32)], z), axis=0
    )
    x_own = jnp.where(first, x_row_own, got3.astype(F32))
    cot_far = swap_z(
        lax.dynamic_index_in_dim(cotangent, 1 - row, 0, keepdims=False).astype(BF), S - 1
    )
    cot_own = jnp.where(
        first, lax.dynamic_index_in_dim(cotangent, row, 0, keepdims=False), cot_far.astype(F32)
    )
    lengths_row = lax.dynamic_index_in_dim(doc_lengths, row, 0, keepdims=False)
    bounds = jnp.cumsum(lengths_row)
    positions = jnp.arange(length, dtype=jnp.int32)[:, None]
    start = jnp.max(
        jnp.where(positions >= bounds[None, :], bounds[None, :], 0), axis=1, keepdims=True
    )

    own_shards = (
        jnp.concatenate([w_qkv[0], w_out[0]], axis=1).astype(BF),
        w_fc1[0].astype(BF),
        w_fc2[0].astype(BF).reshape(4, R, D),
    )
    other_shards = tuple(swap_core(s) for s in own_shards)
    shards = [jnp.where(first, a, b) for a, b in zip(own_shards, other_shards)] + [
        jnp.where(first, b, a) for a, b in zip(own_shards, other_shards)
    ]
    vec_shard = vectors[0].reshape(8, -1)
    gathered = gather_all(shards, vec_shard, DP, S)
    all_parts = gathered[6].reshape(2, -1).astype(BF).astype(F32)
    weights = []
    for layer in range(2):
        qkvo, w1, w2 = gathered[3 * layer : 3 * layer + 3]
        qkvo = qkvo.reshape(D, 4 * D)
        heads_w = jnp.concatenate(
            [
                lax.dynamic_slice(qkvo, (0, i * D + t * GW), (D, GW))
                for i in range(3)
            ],
            axis=1,
        )
        weights.append((heads_w, qkvo[:, 3 * D :], w1.reshape(D, FF), w2.reshape(FF, D)))

    def forward(layer, x, h_row):
        parts = split_vectors(all_parts[layer])
        heads_w, wo, w1, w2 = weights[layer]
        zero = jnp.zeros((GW,), F32)
        bias = jnp.concatenate(
            [
                lax.dynamic_slice(parts[2], (t * GW,), (GW,)),
                zero,
                lax.dynamic_slice(parts[3], (t * GW,), (GW,)),
            ]
        )
        qkv = (jnp.dot(h_row, heads_w, preferred_element_type=F32) + bias).astype(BF)
        o_heads, lse = attend(start, qkv)
        attended = exchange(o_heads.reshape(GROUP, chunk, GW))
        attended = attended.transpose(1, 0, 2).reshape(chunk, D).astype(F32)
        sub = layer_norm(attended, parts[4], parts[5]).astype(BF)
        middle = x + jnp.dot(sub, wo, preferred_element_type=F32) + parts[6]
        normed_two = layer_norm(middle, parts[7], parts[8]).astype(BF)
        pre = jnp.dot(normed_two, w1, preferred_element_type=F32) + parts[10]
        hidden = ffn_inner(pre, parts[11], parts[12]).astype(BF)
        out = middle + jnp.dot(hidden, w2, preferred_element_type=F32) + parts[9]
        return out, (x, h_row, qkv, o_heads, lse, attended, sub, middle, normed_two, pre, hidden)

    def backward(layer, kept, grad_output):
        x, h_row, qkv, o_heads, lse, attended, sub, middle, normed_two, pre, hidden = kept
        parts = split_vectors(all_parts[layer])
        heads_w, wo, w1, w2 = weights[layer]
        ffn_grad = grad_output.astype(BF)
        grad_fc2 = outer_sum(hidden, ffn_grad, BF)
        grad_hidden = back_project(ffn_grad, w2)
        _, inner_back = jax.vjp(ffn_inner, pre, parts[11], parts[12])
        grad_pre, grad_gain_four, grad_bias_four = inner_back(grad_hidden)
        pre_grad = grad_pre.astype(BF)
        grad_fc1 = outer_sum(normed_two, pre_grad, BF)
        grad_normed_two = back_project(pre_grad, w1)
        _, norm_two_back = jax.vjp(layer_norm, middle, parts[7], parts[8])
        grad_mid_part, grad_gain_three, grad_bias_three = norm_two_back(grad_normed_two)
        grad_middle = grad_output + grad_mid_part
        branch_grad = grad_middle.astype(BF)
        grad_out_proj = outer_sum(sub, branch_grad, BF)
        grad_sub = back_project(branch_grad, wo)
        _, sub_back = jax.vjp(layer_norm, attended, parts[4], parts[5])
        grad_attended, grad_gain_two, grad_bias_two = sub_back(grad_sub)
        do = exchange(
            grad_attended.astype(BF).reshape(chunk, GROUP, GW).transpose(1, 0, 2)
        ).reshape(length, GW)
        dqkv = attend_back(start, qkv, o_heads, do, lse)
        grad_heads = outer_sum(h_row, dqkv, BF)
        totals = column_total(dqkv)
        grad_normed = scatter_row(back_project(dqkv, heads_w))
        _, norm_one_back = jax.vjp(layer_norm, x, parts[0], parts[1])
        grad_in_part, grad_gain_one, grad_bias_one = norm_one_back(grad_normed)
        grad_input = grad_middle + grad_in_part

        def spread(piece):
            return lax.dynamic_update_slice(jnp.zeros((D,), F32), piece, (t * GW,))

        packed = jnp.concatenate(
            [
                grad_gain_one,
                grad_bias_one,
                spread(totals[:GW]),
                spread(totals[2 * GW :]),
                grad_gain_two,
                grad_bias_two,
                column_total(branch_grad),
                grad_gain_three,
                grad_bias_three,
                column_total(ffn_grad),
                column_total(pre_grad),
                grad_gain_four,
                grad_bias_four,
            ]
        )
        grads = (
            grad_fc2.reshape(DP, S, 4, R, D),
            grad_fc1.reshape(DP, S, R, FF),
            grad_heads.reshape(DP, S, R, 3 * GW),
            grad_out_proj.reshape(DP, S, R, D),
        )
        return grad_input, grads, packed

    parts0 = split_vectors(all_parts[0])
    parts1 = split_vectors(all_parts[1])
    h0 = layer_norm(x_row, parts0[0], parts0[1]).astype(BF)
    y0, kept0 = forward(0, x_own, h0)
    h1 = gather_row(layer_norm(y0, parts1[0], parts1[1]).astype(BF))
    y1, kept1 = forward(1, y0, h1)
    dx1, grads1, packed1 = backward(1, kept1, cot_own)
    dx0, grads0, packed0 = backward(0, kept0, dx1)
    red1 = scatter_layer(grads1, DP, S, 1)
    red0 = scatter_layer(grads0, DP, S, 2)

    def place(v0, v1):
        crossed = both(
            jnp.where(first, v1, v0).astype(BF),
            [((0, b), (1, b)) for b in zs] + [((1, b), (0, S - 1 - b)) for b in zs],
        ).astype(F32)
        along = swap_z(v1.astype(BF), S - 1).astype(F32)
        row_own = jnp.where(first, v0, crossed)
        row_other = jnp.where(first, crossed, along)
        low = row == 0
        return jnp.stack([jnp.where(low, row_own, row_other), jnp.where(low, row_other, row_own)])[
            None
        ]

    activations = place(y0, y1)
    input_grads = place(dx0, dx1)

    keep = [jnp.where(first, a, b) for a, b in zip(red0, red1)]
    got = [swap_core(jnp.where(first, b, a)) for a, b in zip(red0, red1)]

    def halves(mine, theirs, axis):
        return jnp.where(
            first,
            jnp.concatenate([mine, theirs], axis=axis),
            jnp.concatenate([theirs, mine], axis=axis),
        )

    reduced_fc2 = halves(keep[0], got[0], 0).reshape(4 * R, D)
    reduced_fc1 = halves(keep[1], got[1], 1)
    reduced_out = halves(keep[3], got[3], 1)
    mine_q = jnp.stack(absolute([keep[2][i] for i in range(GROUP)], t))
    theirs_q = jnp.stack(absolute([got[2][i] for i in range(GROUP)], t ^ 3))
    slots = (mine_q + theirs_q).reshape(GROUP, R, 3, GW)
    reduced_qkv = slots.transpose(1, 2, 0, 3).reshape(R, 3 * D)
    grad_mats = [reduced_qkv, reduced_out, reduced_fc1, reduced_fc2]

    packed_own = jnp.where(first, packed0, packed1) + swap_core(
        jnp.where(first, packed1, packed0)
    )

    def total_over(value):
        for bit in dp_bits(DP):
            value = value + lax.ppermute(value, "dp", [(i, i ^ bit) for i in range(DP)])
        return value + sum(swap_z(value, k) for k in range(1, S))

    decay = 1.0 - STEP ** (-0.8)
    masters = [w_qkv[0], w_out[0], w_fc1[0], w_fc2[0]]
    row_olds = [rows_small[0, 0], rows_small[0, 1], rows_small[0, 2], rows_fc2[0]]
    col_widths = [3 * D, D, FF, D]
    row_counts = [D, D, D, FF]
    row_news = []
    col_parts = []
    weight_terms = []
    row_terms = []
    for index in range(4):
        squares = grad_mats[index] * grad_mats[index]
        row_new = decay * row_olds[index] + (1.0 - decay) * jnp.mean(squares, axis=1)
        row_news.append(row_new)
        col_parts.append(jnp.sum(squares, axis=0))
        weight_terms.append(jnp.sum(masters[index] * masters[index]))
        row_terms.append(jnp.sum(row_new))
    shard_size = vectors.shape[1]
    vec_master = vectors[0]
    ends = np.cumsum(np.array(segment_widths()))
    place_at = (dp * S + z) * shard_size
    global_pos = place_at + jnp.arange(shard_size, dtype=jnp.int32)
    segment_of = jnp.sum(
        (global_pos[:, None] >= jnp.asarray(ends[:-1], jnp.int32)[None, :]).astype(jnp.int32),
        axis=1,
    )
    one_hot = (segment_of[:, None] == jnp.arange(13, dtype=jnp.int32)[None, :]).astype(F32)
    vec_weight_terms = jnp.dot(vec_master * vec_master, one_hot, precision=HIGHEST)
    sizes = np.cumsum([sum(col_widths), 8, 13])
    totals_one = total_over(
        jnp.concatenate(
            col_parts + [jnp.stack(weight_terms + row_terms), vec_weight_terms, packed_own]
        )
    )
    col_sums, scalars, vec_weights, vec_all = jnp.split(totals_one, sizes)
    vec_grad = lax.dynamic_slice(vec_all, (place_at,), (shard_size,))
    vec_sq_new = decay * vector_sq[0] + (1.0 - decay) * vec_grad * vec_grad
    vec_update = vec_grad * lax.rsqrt(vec_sq_new)
    col_news = []
    updates = []
    update_terms = []
    offset = 0
    for index in range(4):
        width = col_widths[index]
        col_new = (
            decay * columns[0, offset : offset + width]
            + (1.0 - decay) * col_sums[offset : offset + width] / row_counts[index]
        )
        offset += width
        col_news.append(col_new)
        mean_row = scalars[4 + index] / row_counts[index]
        estimate = row_news[index][:, None] * col_new[None, :] / mean_row
        update = grad_mats[index] * lax.rsqrt(estimate)
        updates.append(update)
        update_terms.append(jnp.sum(update * update))
    vec_update_terms = jnp.dot(vec_update * vec_update, one_hot, precision=HIGHEST)
    totals_two = total_over(jnp.concatenate([jnp.stack(update_terms), vec_update_terms]))
    new_mats = []
    for index in range(4):
        numel = row_counts[index] * col_widths[index]
        rms_update = jnp.sqrt(totals_two[index] / numel)
        rms_master = jnp.sqrt(scalars[index] / numel)
        new_mats.append(
            masters[index]
            - LEARN_RATE * rms_master / jnp.maximum(1.0, rms_update / CLIP_LEVEL) * updates[index]
        )
    seg_sizes = jnp.asarray(np.array(segment_widths()), F32)
    seg_factor = (
        LEARN_RATE
        * jnp.sqrt(vec_weights / seg_sizes)
        / jnp.maximum(1.0, jnp.sqrt(totals_two[4:] / seg_sizes) / CLIP_LEVEL)
    )
    new_vec = vec_master - jnp.dot(one_hot, seg_factor, precision=HIGHEST) * vec_update
    return (
        activations,
        input_grads,
        grad_mats[0][None],
        grad_mats[1][None],
        grad_mats[2][None],
        grad_mats[3][None],
        vec_grad[None],
        new_mats[0][None],
        new_mats[1][None],
        new_mats[2][None],
        new_mats[3][None],
        new_vec[None],
        vec_sq_new[None],
        jnp.stack(row_news[:3])[None],
        row_news[3][None],
        jnp.concatenate(col_news)[None],
    )


def solution(mesh):
    placed = (
        P("dp", "seq", None),
        P("dp", "seq", None),
        P("dp", None),
        P("section", ("dp", "seq"), None),
        P("section", ("dp", "seq"), None),
        P("section", ("dp", "seq"), None),
        P("section", ("dp", "seq"), None),
        P("section", ("dp", "seq")),
        P("section", ("dp", "seq")),
        P("section", None, ("dp", "seq")),
        P("section", ("dp", "seq")),
        P("section", None),
    )
    return jax.shard_map(
        functools.partial(local, mesh.shape["dp"], mesh.shape["seq"]),
        mesh=mesh,
        in_specs=placed,
        out_specs=(
            P("section", "dp", "seq", None),
            P("section", "dp", "seq", None),
            P("section", ("dp", "seq"), None),
            P("section", ("dp", "seq"), None),
            P("section", ("dp", "seq"), None),
            P("section", ("dp", "seq"), None),
            P("section", ("dp", "seq")),
            P("section", ("dp", "seq"), None),
            P("section", ("dp", "seq"), None),
            P("section", ("dp", "seq"), None),
            P("section", ("dp", "seq"), None),
            P("section", ("dp", "seq")),
            P("section", ("dp", "seq")),
            P("section", None, ("dp", "seq")),
            P("section", ("dp", "seq")),
            P("section", None),
        ),
        check_vma=False,
    )
```

```python
import functools

import jax
import jax.numpy as jnp
import numpy as np
from jax import lax
from jax.experimental import pallas as pl
from jax.experimental.pallas import tpu as pltpu
from jax.sharding import PartitionSpec as P

D = 768
FF = 3072
HEADS = 12
HEAD_DIM = 64
STEP = 10
NDOC = 4
NV = 10 * D + 3 * FF
GROUP = 4
GW = D // GROUP
CHUNK_HEADS = HEADS // GROUP

EPSILON = 1e-05
LEARN_RATE = 0.5
CLIP_LEVEL = 1.0
HIGHEST = lax.Precision.HIGHEST
NEG_LARGE = -1e30
MESH = pl.DeviceIdType.MESH
BF = jnp.bfloat16
F32 = jnp.float32


def layer_norm(values, ln_gain, ln_bias):
    average = jnp.mean(values, axis=-1, keepdims=True)
    centred = values - average
    variance = jnp.mean(centred * centred, axis=-1, keepdims=True)
    return centred * lax.rsqrt(variance + EPSILON) * ln_gain + ln_bias


def ffn_inner(hidden_pre, ln_gain, ln_bias):
    return layer_norm(jax.nn.gelu(hidden_pre, approximate=False), ln_gain, ln_bias)


def segment_widths():
    return [D] * 10 + [FF] * 3


def split_vectors(packed):
    pieces = []
    offset = 0
    for span_size in segment_widths():
        pieces.append(packed[offset : offset + span_size])
        offset += span_size
    return pieces


def outer_sum(left, right, kind=F32):
    return lax.dot_general(
        left, right, (((0,), (0,)), ((), ())), preferred_element_type=F32
    ).astype(kind)


def back_project(grads, weight):
    return lax.dot_general(
        grads, weight, (((1,), (1,)), ((), ())), preferred_element_type=F32
    )


def column_total(values_b):
    return jnp.sum(values_b.astype(F32), axis=0)


def dp_bits(count):
    return [1 << i for i in range(count.bit_length() - 1)]


def bit_orders(count):
    bits = dp_bits(count)
    half = len(bits) // 2
    return (bits, bits[half:] + bits[:half])


def subsets(bits):
    found = [0]
    for bit in bits:
        found = found + [m | bit for m in found]
    return sorted(found)


class Copies:
    def __init__(self, send, recv):
        self.send, self.recv, self.used, self.started = send, recv, 0, []

    def go(self, src, dst, device):
        at = self.used
        self.used += 1
        copy = pltpu.make_async_remote_copy(
            src_ref=src,
            dst_ref=dst,
            send_sem=self.send.at[at],
            recv_sem=self.recv.at[at],
            device_id=device,
            device_id_type=MESH,
        )
        copy.start()
        self.started.append(copy)
        return copy

    def finish(self):
        for copy in self.started:
            copy.wait_send()


def greet(peers):
    barrier = pltpu.get_barrier_semaphore()
    for peer in peers:
        pl.semaphore_signal(barrier, inc=1, device_id=peer, device_id_type=MESH)
    pl.semaphore_wait(barrier, len(peers))


def coords():
    return lax.axis_index("section"), lax.axis_index("dp"), lax.axis_index("seq")


def near_peers(c, dp, z, DP, S):
    return (
        [(1 - c, dp, z)]
        + [(c, dp, z ^ k) for k in range(1, S)]
        + [(c, dp ^ b, z) for b in dp_bits(DP)]
    )


def half_lanes(c, width):
    return pl.ds(pl.multiple_of(c * width, 128), width)


def sub_lanes(c, width, a):
    return pl.ds(pl.multiple_of(c * width + a * (width // 2), 128), width // 2)


class Locals:
    def __init__(self, sems):
        self.sems, self.used, self.open = sems, 0, []

    def go(self, src, dst):
        copy = pltpu.make_async_copy(src, dst, self.sems.at[self.used])
        self.used += 1
        copy.start()
        return copy

    def keep(self, src, dst):
        self.open.append(self.go(src, dst))

    def finish(self):
        for copy in self.open:
            copy.wait()


def arrive(some):
    for copy in some:
        copy.wait_recv()


def norm(values, gain, bias):
    average = jnp.mean(values, axis=1, keepdims=True)
    centred = values - average
    variance = jnp.mean(centred * centred, axis=1, keepdims=True)
    return centred * lax.rsqrt(variance + EPSILON) * gain + bias


def dot(left, right):
    return lax.dot_general(left, right, (((1,), (0,)), ((), ())), preferred_element_type=F32)


def dot_nt(left, right):
    return lax.dot_general(left, right, (((1,), (1,)), ((), ())), preferred_element_type=F32)


def dot_tn(left, right):
    return lax.dot_general(left, right, (((0,), (0,)), ((), ())), preferred_element_type=F32)


def pick(row_vector, t, width):
    total = jnp.where(t == 0, row_vector[:, 0:width], 0.0)
    for k in range(1, GROUP):
        total = total + jnp.where(t == k, row_vector[:, k * width : (k + 1) * width], 0.0)
    return total


def doc_start(lens, row, at, rows):
    pos = lax.broadcasted_iota(jnp.int32, (rows, 1), 0) + at
    bound = jnp.int32(0)
    start = jnp.zeros((rows, 1), jnp.int32)
    for j in range(NDOC):
        size = lens[row, j]
        bound = bound + size
        start = start + jnp.where(pos >= bound, size, 0)
    return start


PARTS = dict(
    g1=(0, D),
    b1=(D, D),
    bq=(2 * D, D),
    bv=(3 * D, D),
    gs1=(4 * D, D),
    bs1=(5 * D, D),
    bo=(6 * D, D),
    g2=(7 * D, D),
    b2=(8 * D, D),
    bo2=(9 * D, D),
    bf1=(10 * D, FF),
    gs2=(10 * D + FF, FF),
    bs2=(10 * D + 2 * FF, FF),
)


def window_rows(size, amount):
    most = max(((i * size) % 128 + size + 127) // 128 for i in range(amount))
    return (most + 7) // 8 * 8


def forward_kernel(DP, S, R, *refs):
    (xb, xf, lens, sh_c, sh_1, sh_2, vwin) = refs[:7]
    outs = refs[7:13]
    s_x, s_h, s_qkv, s_o, s_lse, s_att, s_a, s_mid, s_n2, s_pre, s_u, s_y, s_vec = refs[13:26]
    (both_c, both_r, xr, x_own, hrow, qkv, o, lse, att4, att, a, mid, n2, pre, u, y) = refs[26:42]
    (gbuf, wh, wo, w1, w2, vall, vacc, vrow) = refs[42:50]
    flats = refs[50:-3]
    send, recv, local = refs[-3:]
    c, dp, z = coords()
    t = jnp.where(c == 0, z, S - 1 - z)
    row = z // (S // 2)
    chunk = xb.shape[1]
    order_a, order_b = bit_orders(DP)
    steps = len(order_a)
    copies = Copies(send, recv)
    locs = Locals(local)
    sibling, partner, diagonal = (1 - c, dp, z), (c, dp, z ^ 1), (1 - c, dp, z ^ 1)
    every = slice(None)
    greet(near_peers(c, dp, z, DP, S) + [diagonal])

    own_half = [
        locs.go(sh_c.at[:, half_lanes(c, FF // 2)], both_c.at[c, 0]),
        locs.go(sh_1.at[:, half_lanes(c, FF // 2)], both_c.at[c, 1]),
        locs.go(sh_2.at[pl.ds(2 * c, 2)], both_r.at[c]),
    ]
    give_half = [
        copies.go(sh_c.at[:, half_lanes(1 - c, FF // 2)], both_c.at[c, 0], sibling),
        copies.go(sh_1.at[:, half_lanes(1 - c, FF // 2)], both_c.at[c, 1], sibling),
        copies.go(sh_2.at[pl.ds(2 * (1 - c), 2)], both_r.at[c], sibling),
    ]
    vec_copies = [
        copies.go(vwin, vall.at[c, dp, z], (c, dp, z ^ k)) for k in range(1, S)
    ]
    far = jnp.where(c == 0, 3, 2)
    x_near = copies.go(xb.at[row], xr.at[z], partner)
    x_far = copies.go(xb.at[1 - row], xr.at[z], (c, dp, z ^ far))
    vall[c, dp, z] = vwin[...]
    xr[z] = xb[row]
    for copy in own_half:
        copy.wait()
    arrive(give_half)

    kinds = ["col", "col", "row"] * 2

    def shard(g):
        return both_r.at[g // 3] if kinds[g] == "row" else both_c.at[g // 3, g % 3]

    def cut(g, lead, part):
        if kinds[g] == "row":
            rows = pl.ds(2 * c, 2) if part is None else pl.ds(2 * c + part, 1)
            return outs[g].at[lead + (rows,)]
        lanes = half_lanes(c, FF // 2) if part is None else sub_lanes(c, FF // 2, part)
        return outs[g].at[lead + (every, lanes)]

    def across(g):
        return [copies.go(shard(g), cut(g, (dp, z), None), (c, dp, z ^ k)) for k in range(1, S)]

    def beside(g, step):
        found = []
        for part, order in ((0, order_a), (1, order_b)):
            peer = (c, dp ^ order[step], z)
            for m in subsets(order[:step]):
                place = cut(g, (dp ^ m, every), part)
                found.append(copies.go(place, place, peer))
        return found

    forwarded = [[] for _ in range(6)]

    def over_first(g):
        place = cut(g, (dp, every), None)
        forwarded[g].append(copies.go(place, place, sibling))

    def over(g, step):
        for part, order in ((0, order_a), (1, order_b)):
            for m in subsets(order[:step]):
                place = cut(g, (dp ^ m ^ order[step], every), part)
                forwarded[g].append(copies.go(place, place, sibling))

    own_place = [locs.go(shard(g), cut(g, (dp, z), None)) for g in range(6)]
    cross = [None] * 7
    cross[0] = across(0)

    def enter(g):
        own_place[g].wait()
        arrive(cross[g])
        started = beside(g, 0)
        if g + 1 < 6:
            cross[g + 1] = across(g + 1)
        over_first(g)
        return started

    def vec(layer, name):
        at, size = PARTS[name]
        return vrow[layer, :, at : at + size]

    def vectors_in():
        arrive(vec_copies)
        for step in range(steps):
            arrive(
                [
                    copies.go(
                        vall.at[c, dp ^ m], vall.at[c, dp ^ m], (c, dp ^ order_a[step], z)
                    )
                    for m in subsets(order_a[:step])
                ]
            )
        swapped = copies.go(vall.at[c], vall.at[c], sibling)
        arrive([swapped])
        size = NV // (DP * S)
        for layer in range(2):
            vacc[...] = jnp.zeros_like(vacc)
            for i in range(DP * S):
                first = i * size // 128
                count = vall.shape[3]
                vacc[first : first + count, :] += vall[layer, i // S, i % S]
            for i in range(NV // 128):
                vrow[layer, :, i * 128 : (i + 1) * 128] = (
                    vacc[i : i + 1, :].astype(BF).astype(F32)
                )
            locs.keep(vrow.at[layer], s_vec.at[layer])

    def x_in():
        arrive([x_near, x_far])
        x_over = copies.go(xr.at[z ^ far], xr.at[z ^ far], sibling)
        arrive([x_over])
        x_own[...] = jnp.where(c == 0, xf[row], xr[S - 1 - z].astype(F32))
        locs.keep(x_own, s_x.at[0])

    def to_flat(stage, flat_ref, leads, base=0):
        if flat_ref is None:
            return
        for i, lead in enumerate(leads):
            flat_ref[base + i * R : base + (i + 1) * R, :] = stage[lead]

    shards_at = [(d, e) for d in range(DP) for e in range(S)]
    aligned = R % 16 == 0
    f_wh, f_wo, f_w1, f_w2 = (None,) * 4 if aligned else flats

    def load_qkvo(layer):
        got = [
            locs.go(outs[3 * layer].at[:, :, :, pl.ds(pl.multiple_of(t * D, 128), D)], wh)
        ] + [
            locs.go(outs[3 * layer].at[:, :, :, k * D + 512 : (k + 1) * D], wo.at[k])
            for k in range(GROUP)
        ]
        for copy in got:
            copy.wait()
        to_flat(wh, f_wh, shards_at)
        if not aligned:
            for k in range(GROUP):
                for i, lead in enumerate(shards_at):
                    f_wo[k, i * R : (i + 1) * R, :] = wo[(k,) + lead]

    def load_big(source, stage, flat_ref, tail):
        if aligned:
            locs.go(source, stage).wait()
            return
        some = stage.shape[0]
        leads = [(d, e) + j for d in range(some) for e in range(S) for j in tail]
        for q in range(DP // some):
            locs.go(source.at[q * some : (q + 1) * some], stage).wait()
            to_flat(stage, flat_ref, leads, q * len(leads) * R)

    def load_w1(layer):
        load_big(outs[3 * layer + 1], w1, f_w1, [()])

    def load_w2(layer):
        load_big(outs[3 * layer + 2], w2, f_w2, [(j,) for j in range(4)])

    def heads_w():
        return wh[:, :, :, 0:640].reshape(D, 640) if aligned else f_wh[:, 0:640]

    def wo_piece(k):
        return wo[k].reshape(D, 256) if aligned else f_wo[k]

    def w1_piece(j):
        lanes = slice(j * D, (j + 1) * D)
        return w1[:, :, :, lanes].reshape(D, D) if aligned else f_w1[:, lanes]

    def w2_piece(j):
        if not aligned:
            return f_w2[j * D : (j + 1) * D, :]
        some = DP // 4
        return w2[j * some : (j + 1) * some].reshape(D, D)

    def project(layer):
        biases = (pick(vec(layer, "bq"), t, GW), None, pick(vec(layer, "bv"), t, GW))
        for b in range(GROUP):
            if layer == 0:
                values = jnp.where(z == b, xf[row], xr[b].astype(F32))
                hrow[0, b] = norm(values, vec(0, "g1"), vec(0, "b1")).astype(BF)
            full = dot(hrow[layer, b], heads_w())
            for i in range(3):
                piece = full[:, i * GW : (i + 1) * GW]
                if biases[i] is not None:
                    piece = piece + biases[i]
                qkv[layer, b * chunk : (b + 1) * chunk, i * GW : (i + 1) * GW] = piece.astype(BF)

    def attention(layer):
        for b in range(GROUP):
            rows = slice(b * chunk, (b + 1) * chunk)
            upto = (b + 1) * chunk
            start = doc_start(lens, row, b * chunk, chunk)
            key = lax.broadcasted_iota(jnp.int32, (chunk, upto), 1)
            query = lax.broadcasted_iota(jnp.int32, (chunk, upto), 0) + b * chunk
            ok = (key >= start) & (key <= query)
            for h in range(CHUNK_HEADS):
                at = h * HEAD_DIM
                q = qkv[layer, rows, at : at + HEAD_DIM]
                k = qkv[layer, 0:upto, GW + at : GW + at + HEAD_DIM]
                v = qkv[layer, 0:upto, 2 * GW + at : 2 * GW + at + HEAD_DIM]
                s = jnp.where(ok, dot_nt(q, k) * HEAD_DIM ** (-0.5), NEG_LARGE)
                top = jnp.max(s, axis=1, keepdims=True)
                e = jnp.exp(s - top)
                total = jnp.sum(e, axis=1, keepdims=True)
                o[layer, b, :, at : at + HEAD_DIM] = (dot(e.astype(BF), v) / total).astype(BF)
                lse[layer, rows, h : h + 1] = top + jnp.log(total)

    waiting = {}

    def share(layer):
        waiting["o"] = [
            copies.go(o.at[layer, t ^ 1], att4.at[layer, t], partner),
            copies.go(o.at[layer, t ^ 3], att4.at[layer, t], sibling),
            copies.go(o.at[layer, t ^ 2], att4.at[layer, t], diagonal),
        ]
        att4[layer, t] = o[layer, t]
        locs.keep(qkv.at[layer], s_qkv.at[layer])
        locs.keep(o.at[layer], s_o.at[layer])
        locs.keep(lse.at[layer], s_lse.at[layer])
        locs.keep(hrow.at[layer], s_h.at[layer])

    def branch(layer):
        x = x_own if layer == 0 else y.at[0]
        arrive(waiting["o"])
        for k in range(GROUP):
            att[layer, :, k * GW : (k + 1) * GW] = att4[layer, k]
        a[layer] = norm(
            att[layer].astype(F32), vec(layer, "gs1"), vec(layer, "bs1")
        ).astype(BF)
        bo = vec(layer, "bo")
        for k in range(GROUP):
            lanes = slice(k * GW, (k + 1) * GW)
            piece = dot(a[layer], wo_piece(k))[:, 64:256]
            mid[layer, :, lanes] = x[:, lanes] + piece + bo[:, lanes]
        n2[layer] = norm(mid[layer], vec(layer, "g2"), vec(layer, "b2")).astype(BF)
        locs.keep(att.at[layer], s_att.at[layer])
        locs.keep(a.at[layer], s_a.at[layer])
        locs.keep(mid.at[layer], s_mid.at[layer])
        locs.keep(n2.at[layer], s_n2.at[layer])

    def inner(layer):
        bf1, gs2, bs2 = vec(layer, "bf1"), vec(layer, "gs2"), vec(layer, "bs2")
        total = jnp.zeros((chunk, 1), F32)
        for j in range(FF // D):
            lanes = slice(j * D, (j + 1) * D)
            f = dot(n2[layer], w1_piece(j)) + bf1[:, lanes]
            pre[layer, :, lanes] = f
            g = 0.5 * f * (1.0 + lax.erf(f * np.float32(np.sqrt(0.5))))
            gbuf[:, lanes] = g
            total = total + jnp.sum(g, axis=1, keepdims=True)
        average = total / FF
        square = jnp.zeros((chunk, 1), F32)
        for j in range(FF // D):
            centred = gbuf[:, j * D : (j + 1) * D] - average
            square = square + jnp.sum(centred * centred, axis=1, keepdims=True)
        scale = lax.rsqrt(square / FF + EPSILON)
        for j in range(FF // D):
            lanes = slice(j * D, (j + 1) * D)
            u[layer, :, lanes] = (
                (gbuf[:, lanes] - average) * scale * gs2[:, lanes] + bs2[:, lanes]
            ).astype(BF)
        locs.keep(pre.at[layer], s_pre.at[layer])
        locs.keep(u.at[layer], s_u.at[layer])

    def outer(layer):
        total = mid[layer] + vec(layer, "bo2")
        for j in range(FF // D):
            total = total + dot(u[layer, :, j * D : (j + 1) * D], w2_piece(j))
        y[layer] = total
        locs.keep(y.at[layer], s_y.at[layer])

    def pass_on():
        hrow[1, t] = norm(y[0], vec(1, "g1"), vec(1, "b1")).astype(BF)
        waiting["h"] = [
            copies.go(hrow.at[1, t], hrow.at[1, t], partner),
            copies.go(hrow.at[1, t], hrow.at[1, t], sibling),
        ]
        locs.keep(y.at[0], s_x.at[1])

    def row_in():
        arrive(waiting["h"])
        arrive([copies.go(hrow.at[1, t ^ 1], hrow.at[1, t ^ 1], sibling)])

    def compute(g):
        layer = g // 3
        arrive(forwarded[g])
        if g % 3 == 0:
            load_qkvo(layer)
            if layer == 1:
                row_in()
            project(layer)
            attention(layer)
            share(layer)
        elif g % 3 == 1:
            branch(layer)
            load_w1(layer)
            inner(layer)
        else:
            load_w2(layer)
            outer(layer)
            if layer == 0:
                pass_on()

    flight = [None] * 6
    vectors_in()
    x_in()
    flight[0] = enter(0)
    last = [None] * 6
    for g in range(6):
        for step in range(1, steps):
            arrive(flight[g])
            flight[g] = beside(g, step)
            over(g, step - 1)
        last[g] = flight[g]
        if g + 1 < 6:
            flight[g + 1] = enter(g + 1)
        if g > 0:
            arrive(last[g - 1])
            over(g - 1, steps - 1)
            compute(g - 1)
    arrive(last[5])
    over(5, steps - 1)
    compute(5)
    copies.finish()
    locs.finish()


def forward_all(xb, xf, lens, shards, vwin, DP, S):
    R = shards[0].shape[0]
    chunk = xb.shape[1]
    length = chunk * S
    col = jax.ShapeDtypeStruct((DP, S, R, FF), BF)
    row = jax.ShapeDtypeStruct((DP, S, 4, R, D), BF)
    kept = [
        ((2, chunk, D), F32),
        ((2, GROUP, chunk, D), BF),
        ((2, length, 3 * GW), BF),
        ((2, GROUP, chunk, GW), BF),
        ((2, length, CHUNK_HEADS), F32),
        ((2, chunk, D), BF),
        ((2, chunk, D), BF),
        ((2, chunk, D), F32),
        ((2, chunk, D), BF),
        ((2, chunk, FF), F32),
        ((2, chunk, FF), BF),
        ((2, chunk, D), F32),
        ((2, 1, NV), F32),
    ]
    flats = (
        []
        if R % 16 == 0
        else [
            pltpu.VMEM((D, D), BF),
            pltpu.VMEM((GROUP, D, 256), BF),
            pltpu.VMEM((D, FF), BF),
            pltpu.VMEM((FF, D), BF),
        ]
    )
    staged = DP if R % 16 == 0 else DP // 4
    pieces = 2 * (DP - 1)
    amount = 3 + 6 * (S - 1 + 1 + 2 * pieces) + (S - 1) + (DP - 1) + 1 + 3 + 2 * 3 + 3
    anywhere = pl.BlockSpec(memory_space=pl.ANY)
    vmem = pl.BlockSpec(memory_space=pltpu.VMEM)
    return pl.pallas_call(
        functools.partial(forward_kernel, DP, S, R),
        out_shape=(col, col, row, col, col, row)
        + tuple(jax.ShapeDtypeStruct(shape, kind) for shape, kind in kept),
        in_specs=[vmem, vmem, pl.BlockSpec(memory_space=pltpu.SMEM), vmem, vmem, vmem, vmem],
        out_specs=(anywhere,) * (6 + len(kept)),
        scratch_shapes=[
            pltpu.VMEM((2, 2, R, FF // 2), BF),
            pltpu.VMEM((2, 2, R, D), BF),
            pltpu.VMEM((GROUP, chunk, D), BF),
            pltpu.VMEM((chunk, D), F32),
            pltpu.VMEM((2, GROUP, chunk, D), BF),
            pltpu.VMEM((2, length, 3 * GW), BF),
            pltpu.VMEM((2, GROUP, chunk, GW), BF),
            pltpu.VMEM((2, length, CHUNK_HEADS), F32),
            pltpu.VMEM((2, GROUP, chunk, GW), BF),
            pltpu.VMEM((2, chunk, D), BF),
            pltpu.VMEM((2, chunk, D), BF),
            pltpu.VMEM((2, chunk, D), F32),
            pltpu.VMEM((2, chunk, D), BF),
            pltpu.VMEM((2, chunk, FF), F32),
            pltpu.VMEM((2, chunk, FF), BF),
            pltpu.VMEM((2, chunk, D), F32),
            pltpu.VMEM((chunk, FF), F32),
            pltpu.VMEM((DP, S, R, D), BF),
            pltpu.VMEM((GROUP, DP, S, R, 256), BF),
            pltpu.VMEM((staged, S, R, FF), BF),
            pltpu.VMEM((staged, S, 4, R, D), BF),
            pltpu.VMEM((2, DP, S) + vwin.shape, F32),
            pltpu.VMEM((NV // 128 + 16, 128), F32),
            pltpu.VMEM((2, 1, NV), F32),
        ]
        + flats
        + [
            pltpu.SemaphoreType.DMA((amount,)),
            pltpu.SemaphoreType.DMA((amount,)),
            pltpu.SemaphoreType.DMA((64,)),
        ],
        compiler_params=pltpu.CompilerParams(
            collective_id=0, has_side_effects=True, vmem_limit_bytes=60 << 20
        ),
        name="forward",
    )(xb, xf, lens, *shards, vwin)


def scatter_kernel(DP, S, counts, *refs):
    g2, g1, gq, go = refs[:4]
    o2, o1, oq, oo = refs[4:8]
    k2, k1, kq, ko, c2, c1, co = refs[8:15]
    rest = refs[15:]
    send, recv, local = rest[-3:]
    bufs = rest[:-3]
    c, dp, z = coords()
    greet(near_peers(c, dp, z, DP, S))
    copies = Copies(send, recv)
    order_a, order_b = bit_orders(DP)
    sibling = (1 - c, dp, z)
    steps = len(order_a)
    everything = slice(None)

    lanes_mine, lanes_other = half_lanes(c, FF // 2), half_lanes(1 - c, FF // 2)
    lo_mine, lo_other = half_lanes(c, D // 2), half_lanes(1 - c, D // 2)
    plan = [
        (
            [(g2.at[:, :, pl.ds(2 * c, 2)], k2)],
            [(g2.at[:, :, pl.ds(2 * (1 - c), 2)], c2)],
        ),
        (
            [(g1.at[:, :, :, lanes_mine], k1)],
            [(g1.at[:, :, :, lanes_other], c1)],
        ),
        (
            [(gq, kq), (go.at[:, :, :, lo_mine], ko)],
            [(go.at[:, :, :, lo_other], co)],
        ),
    ]
    at_local = 0
    mine, theirs = [], []
    for keep, give in plan:
        mine.append([])
        for src, dst in keep:
            own = pltpu.make_async_copy(src, dst, local.at[at_local])
            own.start()
            at_local += 1
            mine[-1].append(own)
        theirs.append([copies.go(src, dst, sibling) for src, dst in give])

    def add(into, lead, cutter, other, other_lead):
        def one(s, carry):
            place = lead + (s,) + cutter
            into[place] = into[place] + other[other_lead + (s,)]
            return carry

        lax.fori_loop(0, S, one, 0)

    parts = [
        [(k2, (pl.ds(0, 1),), order_a), (k2, (pl.ds(1, 1),), order_b)],
        [
            (k1, (everything, pl.ds(0, FF // 4)), order_a),
            (k1, (everything, pl.ds(FF // 4, FF // 4)), order_b),
        ],
        [(kq, (), order_a), (ko, (), order_b)],
    ]
    joins = [(k2, c2), (k1, c1), (ko, co)]

    def join(g):
        for copy in mine[g]:
            copy.wait()
        for copy in theirs[g]:
            copy.wait_recv()
        into, other = joins[g]

        def one(s, carry):
            for d in range(DP):
                into[d, s] = into[d, s] + other[d, s]
            return carry

        lax.fori_loop(0, S, one, 0)

    at_buf = 0
    slots = []
    for g in range(3):
        slots.append([])
        for part in range(2):
            slots[g].append(bufs[at_buf : at_buf + steps + 1])
            at_buf += steps + 1

    def beside(g, step):
        found = []
        for part, (keep, cutter, order) in enumerate(parts[g]):
            bit = order[step]
            remain = subsets(order[step + 1 :])
            for slot, m in enumerate(remain):
                found.append(
                    copies.go(
                        keep.at[(dp ^ m ^ bit, everything) + cutter],
                        slots[g][part][step].at[slot],
                        (c, dp ^ bit, z),
                    )
                )
        return found

    def merge(g, step, some):
        for copy in some:
            copy.wait_recv()
        for part, (keep, cutter, order) in enumerate(parts[g]):
            for slot, m in enumerate(subsets(order[step + 1 :])):
                add(keep, (dp ^ m,), cutter, slots[g][part][step], (slot,))

    def across(g):
        found = []
        for part, (keep, cutter, order) in enumerate(parts[g]):
            for k in range(1, S):
                found.append(
                    copies.go(
                        keep.at[(dp, z ^ k) + cutter],
                        slots[g][part][steps].at[k - 1],
                        (c, dp, z ^ k),
                    )
                )
        return found

    def close(g, some):
        for copy in some:
            copy.wait_recv()
        for part, (keep, cutter, order) in enumerate(parts[g]):
            got = slots[g][part][steps]
            own = keep[(dp, z) + cutter].astype(F32)
            if g == 2 and part == 0:
                oq[0] = own
                for k in range(1, S):
                    oq[k] = got[k - 1].astype(F32)
                continue
            total = own
            for k in range(1, S):
                total = total + got[k - 1].astype(F32)
            if g == 0:
                o2[pl.ds(part, 1)] = total
            elif g == 1:
                o1[:, pl.ds(part * (FF // 4), FF // 4)] = total
            else:
                oo[...] = total

    flight = [None] * 3
    ending = [None] * 3
    join(0)
    flight[0] = beside(0, 0)
    join(1)
    for g in range(3):
        for step in range(steps):
            merge(g, step, flight[g])
            if step + 1 < steps:
                flight[g] = beside(g, step + 1)
            else:
                ending[g] = across(g)
            if step == 0 and g + 1 < 3:
                flight[g + 1] = beside(g + 1, 0)
                if g + 2 < 3:
                    join(g + 2)
        if g > 0:
            close(g - 1, ending[g - 1])
    close(2, ending[2])
    copies.finish()


def scatter_layer(grads, DP, S, collective_id):
    g2, g1, gq, go = grads
    rows = g1.shape[2]
    steps = len(dp_bits(DP))
    cols = [[(1, rows, D)] * 2, [(rows, FF // 4)] * 2, [(rows, 3 * GW), (rows, D // 2)]]
    slots = []
    for pair in cols:
        for tail in pair:
            for step in range(steps):
                slots.append(pltpu.VMEM((DP >> (step + 1), S) + tail, BF))
            slots.append(pltpu.VMEM((S - 1,) + tail, BF))
    amount = 3 + 6 * (DP - 1) + 6 * (S - 1)
    anywhere = pl.BlockSpec(memory_space=pl.ANY)
    vmem = pl.BlockSpec(memory_space=pltpu.VMEM)
    return pl.pallas_call(
        functools.partial(scatter_kernel, DP, S, None),
        out_shape=(
            jax.ShapeDtypeStruct((2, rows, D), F32),
            jax.ShapeDtypeStruct((rows, FF // 2), F32),
            jax.ShapeDtypeStruct((S, rows, 3 * GW), F32),
            jax.ShapeDtypeStruct((rows, D // 2), F32),
        ),
        in_specs=[anywhere] * 4,
        out_specs=(vmem,) * 4,
        scratch_shapes=[
            pltpu.VMEM((DP, S, 2, rows, D), BF),
            pltpu.VMEM((DP, S, rows, FF // 2), BF),
            pltpu.VMEM((DP, S, rows, 3 * GW), BF),
            pltpu.VMEM((DP, S, rows, D // 2), BF),
            pltpu.VMEM((DP, S, 2, rows, D), BF),
            pltpu.VMEM((DP, S, rows, FF // 2), BF),
            pltpu.VMEM((DP, S, rows, D // 2), BF),
        ]
        + slots
        + [
            pltpu.SemaphoreType.DMA((amount,)),
            pltpu.SemaphoreType.DMA((amount,)),
            pltpu.SemaphoreType.DMA((4,)),
        ],
        compiler_params=pltpu.CompilerParams(
            collective_id=collective_id, has_side_effects=True, vmem_limit_bytes=48 << 20
        ),
        name="scatter_grads",
    )(g2, g1, gq, go)


def attend_back_kernel(start_ref, qkv_ref, o_ref, do_ref, lse_ref, dqkv_ref, dk_acc, dv_acc):
    length = qkv_ref.shape[0]
    block = 256
    scale = HEAD_DIM ** (-0.5)
    for h in range(CHUNK_HEADS):
        lanes = slice(h * HEAD_DIM, (h + 1) * HEAD_DIM)
        klanes = slice(GW + h * HEAD_DIM, GW + (h + 1) * HEAD_DIM)
        vlanes = slice(2 * GW + h * HEAD_DIM, 2 * GW + (h + 1) * HEAD_DIM)
        for at in reversed(range(length // block)):
            rows = slice(at * block, (at + 1) * block)
            upto = (at + 1) * block
            q = qkv_ref[rows, lanes]
            k = qkv_ref[0:upto, klanes]
            v = qkv_ref[0:upto, vlanes]
            do = do_ref[rows, lanes]
            o = o_ref[rows, lanes]
            delta = jnp.sum(do.astype(F32) * o.astype(F32), axis=1, keepdims=True)
            s = (
                lax.dot_general(q, k, (((1,), (1,)), ((), ())), preferred_element_type=F32)
                * scale
            )
            key = lax.broadcasted_iota(jnp.int32, (block, upto), 1)
            query = lax.broadcasted_iota(jnp.int32, (block, upto), 0) + at * block
            ok = (key >= start_ref[rows, :]) & (key <= query)
            p = jnp.exp(jnp.where(ok, s, NEG_LARGE) - lse_ref[rows, h : h + 1])
            dp = lax.dot_general(do, v, (((1,), (1,)), ((), ())), preferred_element_type=F32)
            ds = (p * (dp - delta)).astype(BF)
            dq = lax.dot_general(ds, k, (((1,), (0,)), ((), ())), preferred_element_type=F32)
            dqkv_ref[rows, lanes] = (dq * scale).astype(BF)
            dk = lax.dot_general(ds, q, (((0,), (0,)), ((), ())), preferred_element_type=F32)
            dv = lax.dot_general(
                p.astype(BF), do, (((0,), (0,)), ((), ())), preferred_element_type=F32
            )
            if at == length // block - 1:
                dk_acc[...] = dk
                dv_acc[...] = dv
            else:
                dk_acc[0:upto, :] += dk
                dv_acc[0:upto, :] += dv
        dqkv_ref[:, klanes] = (dk_acc[...] * scale).astype(BF)
        dqkv_ref[:, vlanes] = dv_acc[...].astype(BF)


def attend_back(start, qkv, o, do, lse):
    length = qkv.shape[0]
    return pl.pallas_call(
        attend_back_kernel,
        out_shape=jax.ShapeDtypeStruct((length, 3 * GW), BF),
        scratch_shapes=[pltpu.VMEM((length, HEAD_DIM), F32)] * 2,
        compiler_params=pltpu.CompilerParams(vmem_limit_bytes=48 << 20),
        name="attend_back",
    )(start, qkv, o, do, lse)


def local(DP, S, *args):
    (
        block_input,
        cotangent,
        doc_lengths,
        w_qkv,
        w_out,
        w_fc1,
        w_fc2,
        vectors,
        vector_sq,
        rows_small,
        rows_fc2,
        columns,
    ) = args
    c, dp, z = coords()
    first = c == 0
    chunk = block_input.shape[1]
    length = chunk * S
    R = w_qkv.shape[1]
    row = z // (S // 2)
    t = jnp.where(first, z, S - 1 - z)

    zs = range(S)

    def swap_core(value):
        return lax.ppermute(value, "section", [(0, 1), (1, 0)])

    def swap_z(value, k):
        return lax.ppermute(value, "seq", [(i, i ^ k) for i in zs])

    def both(value, route):
        return lax.ppermute(
            value, ("section", "seq"), [(a * S + b, e * S + f) for (a, b), (e, f) in route]
        )

    def absolute(rel, me):
        odd = (me & 1) == 1
        high = (me & 2) == 2
        rel = [jnp.where(odd, rel[i ^ 1], rel[i]) for i in range(GROUP)]
        return [jnp.where(high, rel[i ^ 2], rel[i]) for i in range(GROUP)]

    def exchange(stacked):
        def piece(k):
            return lax.dynamic_index_in_dim(stacked, t ^ k, 0, keepdims=False)

        got1 = swap_z(piece(1), 1)
        got3 = swap_core(piece(3))
        got2 = both(piece(2), [((a, b), (1 - a, b ^ 1)) for a in (0, 1) for b in zs])
        return jnp.stack(absolute([piece(0), got1, got2, got3], t))

    def scatter_row(partial):
        four = partial.reshape(GROUP, chunk, D)

        def piece(k):
            return lax.dynamic_index_in_dim(four, t ^ k, 0, keepdims=False)

        sent = jnp.stack([piece(3), piece(2)]).astype(BF)
        got = swap_core(sent)
        mine = piece(0) + got[0].astype(F32)
        other = piece(1) + got[1].astype(F32)
        return mine + swap_z(other.astype(BF), 1).astype(F32)

    cot_far = swap_z(
        lax.dynamic_index_in_dim(cotangent, 1 - row, 0, keepdims=False).astype(BF), S - 1
    )
    cot_own = jnp.where(
        first, lax.dynamic_index_in_dim(cotangent, row, 0, keepdims=False), cot_far.astype(F32)
    )
    lengths_row = lax.dynamic_index_in_dim(doc_lengths, row, 0, keepdims=False)
    bounds = jnp.cumsum(lengths_row)
    positions = jnp.arange(length, dtype=jnp.int32)[:, None]
    start = jnp.max(
        jnp.where(positions >= bounds[None, :], bounds[None, :], 0), axis=1, keepdims=True
    )

    by_head = jnp.concatenate(
        [
            part
            for k in range(GROUP)
            for part in [w_qkv[0][:, i * D + k * GW : i * D + (k + 1) * GW] for i in range(3)]
            + [w_out[0][:, k * GW : (k + 1) * GW]]
        ],
        axis=1,
    ).astype(BF)
    shards = [by_head, w_fc1[0].astype(BF), w_fc2[0].astype(BF).reshape(4, R, D)]
    shard_size = vectors.shape[1]
    place_at = (dp * S + z) * shard_size
    wide = window_rows(shard_size, DP * S)
    vwin = lax.dynamic_update_slice(
        jnp.zeros((wide * 128,), F32), vectors[0], (lax.rem(place_at, 128),)
    ).reshape(wide, 128)
    done = forward_all(
        block_input.astype(BF), block_input, doc_lengths, shards, vwin, DP, S
    )
    kept_all = done[6:]
    all_parts = done[18].reshape(2, NV)
    weights = []
    for layer in range(2):
        qkvo, w1, w2 = done[3 * layer : 3 * layer + 3]
        qkvo = qkvo.reshape(D, 4 * D)
        heads_w = lax.dynamic_slice(qkvo, (0, t * D), (D, 3 * GW))
        wo = jnp.concatenate([qkvo[:, k * D + 3 * GW : (k + 1) * D] for k in range(GROUP)], axis=1)
        weights.append((heads_w, wo, w1.reshape(D, FF), w2.reshape(FF, D)))

    def kept_of(layer):
        x, h_row, qkv, o_heads, lse, att, sub, middle, normed_two, pre, hidden = (
            value[layer] for value in kept_all[:11]
        )
        return (
            x,
            h_row.reshape(length, D),
            qkv,
            o_heads.reshape(length, GW),
            lse,
            att.astype(F32),
            sub,
            middle,
            normed_two,
            pre,
            hidden,
        )

    def backward(layer, kept, grad_output):
        x, h_row, qkv, o_heads, lse, attended, sub, middle, normed_two, pre, hidden = kept
        parts = split_vectors(all_parts[layer])
        heads_w, wo, w1, w2 = weights[layer]
        ffn_grad = grad_output.astype(BF)
        grad_fc2 = outer_sum(hidden, ffn_grad, BF)
        grad_hidden = back_project(ffn_grad, w2)
        _, inner_back = jax.vjp(ffn_inner, pre, parts[11], parts[12])
        grad_pre, grad_gain_four, grad_bias_four = inner_back(grad_hidden)
        pre_grad = grad_pre.astype(BF)
        grad_fc1 = outer_sum(normed_two, pre_grad, BF)
        grad_normed_two = back_project(pre_grad, w1)
        _, norm_two_back = jax.vjp(layer_norm, middle, parts[7], parts[8])
        grad_mid_part, grad_gain_three, grad_bias_three = norm_two_back(grad_normed_two)
        grad_middle = grad_output + grad_mid_part
        branch_grad = grad_middle.astype(BF)
        grad_out_proj = outer_sum(sub, branch_grad, BF)
        grad_sub = back_project(branch_grad, wo)
        _, sub_back = jax.vjp(layer_norm, attended, parts[4], parts[5])
        grad_attended, grad_gain_two, grad_bias_two = sub_back(grad_sub)
        do = exchange(
            grad_attended.astype(BF).reshape(chunk, GROUP, GW).transpose(1, 0, 2)
        ).reshape(length, GW)
        dqkv = attend_back(start, qkv, o_heads, do, lse)
        grad_heads = outer_sum(h_row, dqkv, BF)
        totals = column_total(dqkv)
        grad_normed = scatter_row(back_project(dqkv, heads_w))
        _, norm_one_back = jax.vjp(layer_norm, x, parts[0], parts[1])
        grad_in_part, grad_gain_one, grad_bias_one = norm_one_back(grad_normed)
        grad_input = grad_middle + grad_in_part

        def spread(piece):
            return lax.dynamic_update_slice(jnp.zeros((D,), F32), piece, (t * GW,))

        packed = jnp.concatenate(
            [
                grad_gain_one,
                grad_bias_one,
                spread(totals[:GW]),
                spread(totals[2 * GW :]),
                grad_gain_two,
                grad_bias_two,
                column_total(branch_grad),
                grad_gain_three,
                grad_bias_three,
                column_total(ffn_grad),
                column_total(pre_grad),
                grad_gain_four,
                grad_bias_four,
            ]
        )
        grads = (
            grad_fc2.reshape(DP, S, 4, R, D),
            grad_fc1.reshape(DP, S, R, FF),
            grad_heads.reshape(DP, S, R, 3 * GW),
            grad_out_proj.reshape(DP, S, R, D),
        )
        return grad_input, grads, packed

    kept0, kept1 = kept_of(0), kept_of(1)
    y0, y1 = kept_all[11][0], kept_all[11][1]
    dx1, grads1, packed1 = backward(1, kept1, cot_own)
    dx0, grads0, packed0 = backward(0, kept0, dx1)
    red1 = scatter_layer(grads1, DP, S, 1)
    red0 = scatter_layer(grads0, DP, S, 2)

    def place(v0, v1):
        crossed = both(
            jnp.where(first, v1, v0).astype(BF),
            [((0, b), (1, b)) for b in zs] + [((1, b), (0, S - 1 - b)) for b in zs],
        ).astype(F32)
        along = swap_z(v1.astype(BF), S - 1).astype(F32)
        row_own = jnp.where(first, v0, crossed)
        row_other = jnp.where(first, crossed, along)
        low = row == 0
        return jnp.stack([jnp.where(low, row_own, row_other), jnp.where(low, row_other, row_own)])[
            None
        ]

    activations = place(y0, y1)
    input_grads = place(dx0, dx1)

    keep = [jnp.where(first, a, b) for a, b in zip(red0, red1)]
    got = [swap_core(jnp.where(first, b, a)) for a, b in zip(red0, red1)]

    def halves(mine, theirs, axis):
        return jnp.where(
            first,
            jnp.concatenate([mine, theirs], axis=axis),
            jnp.concatenate([theirs, mine], axis=axis),
        )

    reduced_fc2 = halves(keep[0], got[0], 0).reshape(4 * R, D)
    reduced_fc1 = halves(keep[1], got[1], 1)
    reduced_out = halves(keep[3], got[3], 1)
    mine_q = jnp.stack(absolute([keep[2][i] for i in range(GROUP)], t))
    theirs_q = jnp.stack(absolute([got[2][i] for i in range(GROUP)], t ^ 3))
    slots = (mine_q + theirs_q).reshape(GROUP, R, 3, GW)
    reduced_qkv = slots.transpose(1, 2, 0, 3).reshape(R, 3 * D)
    grad_mats = [reduced_qkv, reduced_out, reduced_fc1, reduced_fc2]

    packed_own = jnp.where(first, packed0, packed1) + swap_core(
        jnp.where(first, packed1, packed0)
    )

    def total_over(value):
        for bit in dp_bits(DP):
            value = value + lax.ppermute(value, "dp", [(i, i ^ bit) for i in range(DP)])
        return value + sum(swap_z(value, k) for k in range(1, S))

    decay = 1.0 - STEP ** (-0.8)
    masters = [w_qkv[0], w_out[0], w_fc1[0], w_fc2[0]]
    row_olds = [rows_small[0, 0], rows_small[0, 1], rows_small[0, 2], rows_fc2[0]]
    col_widths = [3 * D, D, FF, D]
    row_counts = [D, D, D, FF]
    row_news = []
    col_parts = []
    weight_terms = []
    row_terms = []
    for index in range(4):
        squares = grad_mats[index] * grad_mats[index]
        row_new = decay * row_olds[index] + (1.0 - decay) * jnp.mean(squares, axis=1)
        row_news.append(row_new)
        col_parts.append(jnp.sum(squares, axis=0))
        weight_terms.append(jnp.sum(masters[index] * masters[index]))
        row_terms.append(jnp.sum(row_new))
    vec_master = vectors[0]
    ends = np.cumsum(np.array(segment_widths()))
    global_pos = place_at + jnp.arange(shard_size, dtype=jnp.int32)
    segment_of = jnp.sum(
        (global_pos[:, None] >= jnp.asarray(ends[:-1], jnp.int32)[None, :]).astype(jnp.int32),
        axis=1,
    )
    one_hot = (segment_of[:, None] == jnp.arange(13, dtype=jnp.int32)[None, :]).astype(F32)
    vec_weight_terms = jnp.dot(vec_master * vec_master, one_hot, precision=HIGHEST)
    sizes = np.cumsum([sum(col_widths), 8, 13])
    totals_one = total_over(
        jnp.concatenate(
            col_parts + [jnp.stack(weight_terms + row_terms), vec_weight_terms, packed_own]
        )
    )
    col_sums, scalars, vec_weights, vec_all = jnp.split(totals_one, sizes)
    vec_grad = lax.dynamic_slice(vec_all, (place_at,), (shard_size,))
    vec_sq_new = decay * vector_sq[0] + (1.0 - decay) * vec_grad * vec_grad
    vec_update = vec_grad * lax.rsqrt(vec_sq_new)
    col_news = []
    updates = []
    update_terms = []
    offset = 0
    for index in range(4):
        width = col_widths[index]
        col_new = (
            decay * columns[0, offset : offset + width]
            + (1.0 - decay) * col_sums[offset : offset + width] / row_counts[index]
        )
        offset += width
        col_news.append(col_new)
        mean_row = scalars[4 + index] / row_counts[index]
        estimate = row_news[index][:, None] * col_new[None, :] / mean_row
        update = grad_mats[index] * lax.rsqrt(estimate)
        updates.append(update)
        update_terms.append(jnp.sum(update * update))
    vec_update_terms = jnp.dot(vec_update * vec_update, one_hot, precision=HIGHEST)
    totals_two = total_over(jnp.concatenate([jnp.stack(update_terms), vec_update_terms]))
    new_mats = []
    for index in range(4):
        numel = row_counts[index] * col_widths[index]
        rms_update = jnp.sqrt(totals_two[index] / numel)
        rms_master = jnp.sqrt(scalars[index] / numel)
        new_mats.append(
            masters[index]
            - LEARN_RATE * rms_master / jnp.maximum(1.0, rms_update / CLIP_LEVEL) * updates[index]
        )
    seg_sizes = jnp.asarray(np.array(segment_widths()), F32)
    seg_factor = (
        LEARN_RATE
        * jnp.sqrt(vec_weights / seg_sizes)
        / jnp.maximum(1.0, jnp.sqrt(totals_two[4:] / seg_sizes) / CLIP_LEVEL)
    )
    new_vec = vec_master - jnp.dot(one_hot, seg_factor, precision=HIGHEST) * vec_update
    return (
        activations,
        input_grads,
        grad_mats[0][None],
        grad_mats[1][None],
        grad_mats[2][None],
        grad_mats[3][None],
        vec_grad[None],
        new_mats[0][None],
        new_mats[1][None],
        new_mats[2][None],
        new_mats[3][None],
        new_vec[None],
        vec_sq_new[None],
        jnp.stack(row_news[:3])[None],
        row_news[3][None],
        jnp.concatenate(col_news)[None],
    )


def solution(mesh):
    placed = (
        P("dp", "seq", None),
        P("dp", "seq", None),
        P("dp", None),
        P("section", ("dp", "seq"), None),
        P("section", ("dp", "seq"), None),
        P("section", ("dp", "seq"), None),
        P("section", ("dp", "seq"), None),
        P("section", ("dp", "seq")),
        P("section", ("dp", "seq")),
        P("section", None, ("dp", "seq")),
        P("section", ("dp", "seq")),
        P("section", None),
    )
    return jax.shard_map(
        functools.partial(local, mesh.shape["dp"], mesh.shape["seq"]),
        mesh=mesh,
        in_specs=placed,
        out_specs=(
            P("section", "dp", "seq", None),
            P("section", "dp", "seq", None),
            P("section", ("dp", "seq"), None),
            P("section", ("dp", "seq"), None),
            P("section", ("dp", "seq"), None),
            P("section", ("dp", "seq"), None),
            P("section", ("dp", "seq")),
            P("section", ("dp", "seq"), None),
            P("section", ("dp", "seq"), None),
            P("section", ("dp", "seq"), None),
            P("section", ("dp", "seq"), None),
            P("section", ("dp", "seq")),
            P("section", ("dp", "seq")),
            P("section", None, ("dp", "seq")),
            P("section", ("dp", "seq")),
            P("section", None),
        ),
        check_vma=False,
    )
```

```python
import functools

import jax
import jax.numpy as jnp
import numpy as np
from jax import lax
from jax.experimental import pallas as pl
from jax.experimental.pallas import tpu as pltpu
from jax.sharding import PartitionSpec as P

D = 768
FF = 3072
HEADS = 12
HEAD_DIM = 64
STEP = 10
NDOC = 4
NV = 10 * D + 3 * FF
GROUP = 4
GW = D // GROUP
CHUNK_HEADS = HEADS // GROUP

EPSILON = 1e-05
LEARN_RATE = 0.5
CLIP_LEVEL = 1.0
HIGHEST = lax.Precision.HIGHEST
NEG_LARGE = -1e30
MESH = pl.DeviceIdType.MESH
BF = jnp.bfloat16
F32 = jnp.float32


def layer_norm(values, ln_gain, ln_bias):
    average = jnp.mean(values, axis=-1, keepdims=True)
    centred = values - average
    variance = jnp.mean(centred * centred, axis=-1, keepdims=True)
    return centred * lax.rsqrt(variance + EPSILON) * ln_gain + ln_bias


def ffn_inner(hidden_pre, ln_gain, ln_bias):
    return layer_norm(jax.nn.gelu(hidden_pre, approximate=False), ln_gain, ln_bias)


def segment_widths():
    return [D] * 10 + [FF] * 3


def split_vectors(packed):
    pieces = []
    offset = 0
    for span_size in segment_widths():
        pieces.append(packed[offset : offset + span_size])
        offset += span_size
    return pieces


def outer_sum(left, right, kind=F32):
    return lax.dot_general(
        left, right, (((0,), (0,)), ((), ())), preferred_element_type=F32
    ).astype(kind)


def back_project(grads, weight):
    return lax.dot_general(
        grads, weight, (((1,), (1,)), ((), ())), preferred_element_type=F32
    )


def column_total(values_b):
    return jnp.sum(values_b.astype(F32), axis=0)


def dp_bits(count):
    return [1 << i for i in range(count.bit_length() - 1)]


def bit_orders(count):
    bits = dp_bits(count)
    half = len(bits) // 2
    return (bits, bits[half:] + bits[:half])


def subsets(bits):
    found = [0]
    for bit in bits:
        found = found + [m | bit for m in found]
    return sorted(found)


class Copies:
    def __init__(self, send, recv):
        self.send, self.recv, self.used, self.started = send, recv, 0, []

    def go(self, src, dst, device):
        at = self.used
        self.used += 1
        copy = pltpu.make_async_remote_copy(
            src_ref=src,
            dst_ref=dst,
            send_sem=self.send.at[at],
            recv_sem=self.recv.at[at],
            device_id=device,
            device_id_type=MESH,
        )
        copy.start()
        self.started.append(copy)
        return copy

    def settle(self, some):
        for copy in some:
            copy.wait_send()
        gone = [id(copy) for copy in some]
        self.started = [copy for copy in self.started if id(copy) not in gone]

    def finish(self):
        self.settle(self.started)


def greet(peers):
    barrier = pltpu.get_barrier_semaphore()
    for peer in peers:
        pl.semaphore_signal(barrier, inc=1, device_id=peer, device_id_type=MESH)
    pl.semaphore_wait(barrier, len(peers))


def coords():
    return lax.axis_index("section"), lax.axis_index("dp"), lax.axis_index("seq")


def near_peers(c, dp, z, DP, S):
    return (
        [(1 - c, dp, z)]
        + [(c, dp, z ^ k) for k in range(1, S)]
        + [(c, dp ^ b, z) for b in dp_bits(DP)]
    )


def half_lanes(c, width):
    return pl.ds(pl.multiple_of(c * width, 128), width)


def sub_lanes(c, width, a):
    return pl.ds(pl.multiple_of(c * width + a * (width // 2), 128), width // 2)


class Locals:
    def __init__(self, sems):
        self.sems, self.used, self.open = sems, 0, []

    def go(self, src, dst):
        copy = pltpu.make_async_copy(src, dst, self.sems.at[self.used])
        self.used += 1
        copy.start()
        return copy

    def keep(self, src, dst):
        self.open.append(self.go(src, dst))

    def finish(self):
        for copy in self.open:
            copy.wait()


def arrive(some):
    for copy in some:
        copy.wait_recv()


def norm(values, gain, bias):
    average = jnp.mean(values, axis=1, keepdims=True)
    centred = values - average
    variance = jnp.mean(centred * centred, axis=1, keepdims=True)
    return centred * lax.rsqrt(variance + EPSILON) * gain + bias


def dot(left, right):
    return lax.dot_general(left, right, (((1,), (0,)), ((), ())), preferred_element_type=F32)


def dot_nt(left, right):
    return lax.dot_general(left, right, (((1,), (1,)), ((), ())), preferred_element_type=F32)


def dot_tn(left, right):
    return lax.dot_general(left, right, (((0,), (0,)), ((), ())), preferred_element_type=F32)


def pick(row_vector, t, width):
    total = jnp.where(t == 0, row_vector[:, 0:width], 0.0)
    for k in range(1, GROUP):
        total = total + jnp.where(t == k, row_vector[:, k * width : (k + 1) * width], 0.0)
    return total


def doc_start(lens, row, at, rows):
    pos = lax.broadcasted_iota(jnp.int32, (rows, 1), 0) + at
    bound = jnp.int32(0)
    start = jnp.zeros((rows, 1), jnp.int32)
    for j in range(NDOC):
        size = lens[row, j]
        bound = bound + size
        start = start + jnp.where(pos >= bound, size, 0)
    return start


PARTS = dict(
    g1=(0, D),
    b1=(D, D),
    bq=(2 * D, D),
    bv=(3 * D, D),
    gs1=(4 * D, D),
    bs1=(5 * D, D),
    bo=(6 * D, D),
    g2=(7 * D, D),
    b2=(8 * D, D),
    bo2=(9 * D, D),
    bf1=(10 * D, FF),
    gs2=(10 * D + FF, FF),
    bs2=(10 * D + 2 * FF, FF),
)


def window_rows(size, amount):
    most = max(((i * size) % 128 + size + 127) // 128 for i in range(amount))
    return (most + 7) // 8 * 8


def forward_kernel(DP, S, R, *refs):
    (xb, xf, cotb, cotf, lens, sh_c, sh_1, sh_2, vwin) = refs[:9]
    outs = refs[9:15]
    s_x, s_h, s_qkv, s_o, s_lse, s_att, s_a, s_mid, s_n2, s_pre, s_u, s_y, s_vec = refs[15:28]
    s_wo, s_dy = refs[28:30]
    (both_c, both_r, xr, x_own, hrow, qkv, o, lse, att4, att, a, mid, n2, pre, u, y) = refs[30:46]
    (gbuf, wh, wo, w1, w2, vall, vacc, vrow, wo_all, cotr, dy) = refs[46:57]
    flats = refs[57:-3]
    send, recv, local = refs[-3:]
    c, dp, z = coords()
    t = jnp.where(c == 0, z, S - 1 - z)
    row = z // (S // 2)
    chunk = xb.shape[1]
    order_a, order_b = bit_orders(DP)
    steps = len(order_a)
    copies = Copies(send, recv)
    locs = Locals(local)
    sibling, partner, diagonal = (1 - c, dp, z), (c, dp, z ^ 1), (1 - c, dp, z ^ 1)
    every = slice(None)
    greet(near_peers(c, dp, z, DP, S) + [diagonal])

    own_half = [
        locs.go(sh_c.at[:, half_lanes(c, FF // 2)], both_c.at[c, 0]),
        locs.go(sh_1.at[:, half_lanes(c, FF // 2)], both_c.at[c, 1]),
        locs.go(sh_2.at[pl.ds(2 * c, 2)], both_r.at[c]),
    ]
    give_half = [
        copies.go(sh_c.at[:, half_lanes(1 - c, FF // 2)], both_c.at[c, 0], sibling),
        copies.go(sh_1.at[:, half_lanes(1 - c, FF // 2)], both_c.at[c, 1], sibling),
        copies.go(sh_2.at[pl.ds(2 * (1 - c), 2)], both_r.at[c], sibling),
    ]
    vec_copies = [
        copies.go(vwin, vall.at[c, dp, z], (c, dp, z ^ k)) for k in range(1, S)
    ]
    far = jnp.where(c == 0, 3, 2)
    x_near = copies.go(xb.at[row], xr.at[z], partner)
    x_far = copies.go(xb.at[1 - row], xr.at[z], (c, dp, z ^ far))
    vall[c, dp, z] = vwin[...]
    xr[z] = xb[row]
    for copy in own_half:
        copy.wait()
    arrive(give_half)

    kinds = ["col", "col", "row"] * 2

    def shard(g):
        return both_r.at[g // 3] if kinds[g] == "row" else both_c.at[g // 3, g % 3]

    def cut(g, lead, part):
        if kinds[g] == "row":
            rows = pl.ds(2 * c, 2) if part is None else pl.ds(2 * c + part, 1)
            return outs[g].at[lead + (rows,)]
        lanes = half_lanes(c, FF // 2) if part is None else sub_lanes(c, FF // 2, part)
        return outs[g].at[lead + (every, lanes)]

    def across(g):
        return [copies.go(shard(g), cut(g, (dp, z), None), (c, dp, z ^ k)) for k in range(1, S)]

    def beside(g, step):
        found = []
        for part, order in ((0, order_a), (1, order_b)):
            peer = (c, dp ^ order[step], z)
            for m in subsets(order[:step]):
                place = cut(g, (dp ^ m, every), part)
                found.append(copies.go(place, place, peer))
        return found

    forwarded = [[] for _ in range(6)]

    def over_first(g):
        place = cut(g, (dp, every), None)
        forwarded[g].append(copies.go(place, place, sibling))

    def over(g, step):
        for part, order in ((0, order_a), (1, order_b)):
            for m in subsets(order[:step]):
                place = cut(g, (dp ^ m ^ order[step], every), part)
                forwarded[g].append(copies.go(place, place, sibling))

    own_place = [locs.go(shard(g), cut(g, (dp, z), None)) for g in range(6)]
    cross = [None] * 7
    cross[0] = across(0)

    def enter(g):
        own_place[g].wait()
        arrive(cross[g])
        started = beside(g, 0)
        if g + 1 < 6:
            cross[g + 1] = across(g + 1)
        over_first(g)
        return started

    def vec(layer, name):
        at, size = PARTS[name]
        return vrow[layer, :, at : at + size]

    def vectors_in():
        arrive(vec_copies)
        for step in range(steps):
            arrive(
                [
                    copies.go(
                        vall.at[c, dp ^ m], vall.at[c, dp ^ m], (c, dp ^ order_a[step], z)
                    )
                    for m in subsets(order_a[:step])
                ]
            )
        swapped = copies.go(vall.at[c], vall.at[c], sibling)
        arrive([swapped])
        size = NV // (DP * S)
        for layer in range(2):
            vacc[...] = jnp.zeros_like(vacc)
            for i in range(DP * S):
                first = i * size // 128
                count = vall.shape[3]
                vacc[first : first + count, :] += vall[layer, i // S, i % S]
            for i in range(NV // 128):
                vrow[layer, :, i * 128 : (i + 1) * 128] = (
                    vacc[i : i + 1, :].astype(BF).astype(F32)
                )
            locs.keep(vrow.at[layer], s_vec.at[layer])

    def x_in():
        arrive([x_near, x_far])
        x_over = copies.go(xr.at[z ^ far], xr.at[z ^ far], sibling)
        arrive([x_over])
        x_own[...] = jnp.where(c == 0, xf[row], xr[S - 1 - z].astype(F32))
        locs.keep(x_own, s_x.at[0])

    def to_flat(stage, flat_ref, leads, base=0):
        if flat_ref is None:
            return
        for i, lead in enumerate(leads):
            flat_ref[base + i * R : base + (i + 1) * R, :] = stage[lead]

    shards_at = [(d, e) for d in range(DP) for e in range(S)]
    aligned = R % 16 == 0
    f_wh, f_w1, f_w2 = (None,) * 3 if aligned else flats

    def load_qkvo(layer):
        got = [
            locs.go(outs[3 * layer].at[:, :, :, pl.ds(pl.multiple_of(t * D, 128), D)], wh)
        ] + [
            locs.go(outs[3 * layer].at[:, :, :, k * D + 512 : (k + 1) * D], wo.at[k])
            for k in range(GROUP)
        ]
        for copy in got:
            copy.wait()
        to_flat(wh, f_wh, shards_at)
        for k in range(GROUP):
            lanes = slice(k * GW, (k + 1) * GW)
            if aligned:
                wo_all[layer, :, lanes] = wo[k].reshape(D, 256)[:, 64:256]
            else:
                for i, lead in enumerate(shards_at):
                    wo_all[layer, i * R : (i + 1) * R, lanes] = wo[(k,) + lead][:, 64:256]
        locs.keep(wo_all.at[layer], s_wo.at[layer])

    def load_big(source, stage, flat_ref, tail):
        if aligned:
            locs.go(source, stage).wait()
            return
        some = stage.shape[0]
        leads = [(d, e) + j for d in range(some) for e in range(S) for j in tail]
        for q in range(DP // some):
            locs.go(source.at[q * some : (q + 1) * some], stage).wait()
            to_flat(stage, flat_ref, leads, q * len(leads) * R)

    def load_w1(layer):
        load_big(outs[3 * layer + 1], w1, f_w1, [()])

    def load_w2(layer):
        load_big(outs[3 * layer + 2], w2, f_w2, [(j,) for j in range(4)])

    def heads_w():
        return wh[:, :, :, 0:640].reshape(D, 640) if aligned else f_wh[:, 0:640]

    def w1_piece(j):
        lanes = slice(j * D, (j + 1) * D)
        return w1[:, :, :, lanes].reshape(D, D) if aligned else f_w1[:, lanes]

    def w2_piece(j):
        if not aligned:
            return f_w2[j * D : (j + 1) * D, :]
        some = DP // 4
        return w2[j * some : (j + 1) * some].reshape(D, D)

    def project(layer):
        biases = (pick(vec(layer, "bq"), t, GW), None, pick(vec(layer, "bv"), t, GW))
        for b in range(GROUP):
            if layer == 0:
                values = jnp.where(z == b, xf[row], xr[b].astype(F32))
                hrow[0, b] = norm(values, vec(0, "g1"), vec(0, "b1")).astype(BF)
            full = dot(hrow[layer, b], heads_w())
            for i in range(3):
                piece = full[:, i * GW : (i + 1) * GW]
                if biases[i] is not None:
                    piece = piece + biases[i]
                qkv[layer, b * chunk : (b + 1) * chunk, i * GW : (i + 1) * GW] = piece.astype(BF)

    def attention(layer):
        for b in range(GROUP):
            rows = slice(b * chunk, (b + 1) * chunk)
            upto = (b + 1) * chunk
            start = doc_start(lens, row, b * chunk, chunk)
            key = lax.broadcasted_iota(jnp.int32, (chunk, upto), 1)
            query = lax.broadcasted_iota(jnp.int32, (chunk, upto), 0) + b * chunk
            ok = (key >= start) & (key <= query)
            for h in range(CHUNK_HEADS):
                at = h * HEAD_DIM
                q = qkv[layer, rows, at : at + HEAD_DIM]
                k = qkv[layer, 0:upto, GW + at : GW + at + HEAD_DIM]
                v = qkv[layer, 0:upto, 2 * GW + at : 2 * GW + at + HEAD_DIM]
                s = jnp.where(ok, dot_nt(q, k) * HEAD_DIM ** (-0.5), NEG_LARGE)
                top = jnp.max(s, axis=1, keepdims=True)
                e = jnp.exp(s - top)
                total = jnp.sum(e, axis=1, keepdims=True)
                o[layer, b, :, at : at + HEAD_DIM] = (dot(e.astype(BF), v) / total).astype(BF)
                lse[layer, rows, h : h + 1] = top + jnp.log(total)

    waiting = {}

    def share(layer):
        waiting["o"] = [
            copies.go(o.at[layer, t ^ 1], att4.at[layer, t], partner),
            copies.go(o.at[layer, t ^ 3], att4.at[layer, t], sibling),
            copies.go(o.at[layer, t ^ 2], att4.at[layer, t], diagonal),
        ]
        att4[layer, t] = o[layer, t]
        locs.keep(qkv.at[layer], s_qkv.at[layer])
        locs.keep(o.at[layer], s_o.at[layer])
        locs.keep(lse.at[layer], s_lse.at[layer])
        locs.keep(hrow.at[layer], s_h.at[layer])

    def branch(layer):
        x = x_own if layer == 0 else y.at[0]
        arrive(waiting["o"])
        for k in range(GROUP):
            att[layer, :, k * GW : (k + 1) * GW] = att4[layer, k]
        a[layer] = norm(
            att[layer].astype(F32), vec(layer, "gs1"), vec(layer, "bs1")
        ).astype(BF)
        mid[layer] = x[...] + dot(a[layer], wo_all[layer]) + vec(layer, "bo")
        n2[layer] = norm(mid[layer], vec(layer, "g2"), vec(layer, "b2")).astype(BF)
        locs.keep(att.at[layer], s_att.at[layer])
        locs.keep(a.at[layer], s_a.at[layer])
        locs.keep(mid.at[layer], s_mid.at[layer])
        locs.keep(n2.at[layer], s_n2.at[layer])

    def inner(layer):
        bf1, gs2, bs2 = vec(layer, "bf1"), vec(layer, "gs2"), vec(layer, "bs2")
        total = jnp.zeros((chunk, 1), F32)
        for j in range(FF // D):
            lanes = slice(j * D, (j + 1) * D)
            f = dot(n2[layer], w1_piece(j)) + bf1[:, lanes]
            pre[layer, :, lanes] = f
            g = 0.5 * f * (1.0 + lax.erf(f * np.float32(np.sqrt(0.5))))
            gbuf[:, lanes] = g
            total = total + jnp.sum(g, axis=1, keepdims=True)
        average = total / FF
        square = jnp.zeros((chunk, 1), F32)
        for j in range(FF // D):
            centred = gbuf[:, j * D : (j + 1) * D] - average
            square = square + jnp.sum(centred * centred, axis=1, keepdims=True)
        scale = lax.rsqrt(square / FF + EPSILON)
        for j in range(FF // D):
            lanes = slice(j * D, (j + 1) * D)
            u[layer, :, lanes] = (
                (gbuf[:, lanes] - average) * scale * gs2[:, lanes] + bs2[:, lanes]
            ).astype(BF)
        locs.keep(pre.at[layer], s_pre.at[layer])
        locs.keep(u.at[layer], s_u.at[layer])

    def outer(layer):
        total = mid[layer] + vec(layer, "bo2")
        for j in range(FF // D):
            total = total + dot(u[layer, :, j * D : (j + 1) * D], w2_piece(j))
        y[layer] = total
        locs.keep(y.at[layer], s_y.at[layer])

    def pass_on():
        hrow[1, t] = norm(y[0], vec(1, "g1"), vec(1, "b1")).astype(BF)
        waiting["h"] = [
            copies.go(hrow.at[1, t], hrow.at[1, t], partner),
            copies.go(hrow.at[1, t], hrow.at[1, t], sibling),
        ]
        locs.keep(y.at[0], s_x.at[1])

    def row_in():
        arrive(waiting["h"])
        arrive([copies.go(hrow.at[1, t ^ 1], hrow.at[1, t ^ 1], sibling)])

    def compute(g):
        layer = g // 3
        arrive(forwarded[g])
        if g % 3 == 0:
            load_qkvo(layer)
            if layer == 1:
                row_in()
            project(layer)
            attention(layer)
            share(layer)
        elif g % 3 == 1:
            branch(layer)
            load_w1(layer)
            inner(layer)
        else:
            load_w2(layer)
            outer(layer)
            if layer == 0:
                pass_on()
                cotangent_in()

    def cotangent_in():
        copy = copies.go(cotb.at[1 - row], cotr, (c, dp, S - 1 - z))
        arrive([copy])
        dy[...] = jnp.where(c == 0, cotf[row], cotr[...].astype(F32))
        locs.keep(dy, s_dy)

    flight = [None] * 6
    vectors_in()
    x_in()
    flight[0] = enter(0)
    last = [None] * 6
    for g in range(6):
        for step in range(1, steps):
            arrive(flight[g])
            flight[g] = beside(g, step)
            over(g, step - 1)
        last[g] = flight[g]
        if g + 1 < 6:
            flight[g + 1] = enter(g + 1)
        if g > 0:
            arrive(last[g - 1])
            over(g - 1, steps - 1)
            compute(g - 1)
    arrive(last[5])
    over(5, steps - 1)
    compute(5)
    copies.finish()
    locs.finish()


def forward_all(xb, xf, cotb, cotf, lens, shards, vwin, DP, S):
    R = shards[0].shape[0]
    chunk = xb.shape[1]
    length = chunk * S
    col = jax.ShapeDtypeStruct((DP, S, R, FF), BF)
    row = jax.ShapeDtypeStruct((DP, S, 4, R, D), BF)
    kept = [
        ((2, chunk, D), F32),
        ((2, GROUP, chunk, D), BF),
        ((2, length, 3 * GW), BF),
        ((2, GROUP, chunk, GW), BF),
        ((2, length, CHUNK_HEADS), F32),
        ((2, chunk, D), BF),
        ((2, chunk, D), BF),
        ((2, chunk, D), F32),
        ((2, chunk, D), BF),
        ((2, chunk, FF), F32),
        ((2, chunk, FF), BF),
        ((2, chunk, D), F32),
        ((2, 1, NV), F32),
        ((2, D, D), BF),
        ((chunk, D), F32),
    ]
    flats = (
        []
        if R % 16 == 0
        else [
            pltpu.VMEM((D, D), BF),
            pltpu.VMEM((D, FF), BF),
            pltpu.VMEM((FF, D), BF),
        ]
    )
    staged = DP if R % 16 == 0 else DP // 4
    pieces = 2 * (DP - 1)
    amount = 3 + 6 * (S - 1 + 1 + 2 * pieces) + (S - 1) + (DP - 1) + 1 + 3 + 2 * 3 + 3 + 1
    anywhere = pl.BlockSpec(memory_space=pl.ANY)
    vmem = pl.BlockSpec(memory_space=pltpu.VMEM)
    return pl.pallas_call(
        functools.partial(forward_kernel, DP, S, R),
        out_shape=(col, col, row, col, col, row)
        + tuple(jax.ShapeDtypeStruct(shape, kind) for shape, kind in kept),
        in_specs=[vmem] * 4 + [pl.BlockSpec(memory_space=pltpu.SMEM)] + [vmem] * 4,
        out_specs=(anywhere,) * (6 + len(kept)),
        scratch_shapes=[
            pltpu.VMEM((2, 2, R, FF // 2), BF),
            pltpu.VMEM((2, 2, R, D), BF),
            pltpu.VMEM((GROUP, chunk, D), BF),
            pltpu.VMEM((chunk, D), F32),
            pltpu.VMEM((2, GROUP, chunk, D), BF),
            pltpu.VMEM((2, length, 3 * GW), BF),
            pltpu.VMEM((2, GROUP, chunk, GW), BF),
            pltpu.VMEM((2, length, CHUNK_HEADS), F32),
            pltpu.VMEM((2, GROUP, chunk, GW), BF),
            pltpu.VMEM((2, chunk, D), BF),
            pltpu.VMEM((2, chunk, D), BF),
            pltpu.VMEM((2, chunk, D), F32),
            pltpu.VMEM((2, chunk, D), BF),
            pltpu.VMEM((2, chunk, FF), F32),
            pltpu.VMEM((2, chunk, FF), BF),
            pltpu.VMEM((2, chunk, D), F32),
            pltpu.VMEM((chunk, FF), F32),
            pltpu.VMEM((DP, S, R, D), BF),
            pltpu.VMEM((GROUP, DP, S, R, 256), BF),
            pltpu.VMEM((staged, S, R, FF), BF),
            pltpu.VMEM((staged, S, 4, R, D), BF),
            pltpu.VMEM((2, DP, S) + vwin.shape, F32),
            pltpu.VMEM((NV // 128 + 16, 128), F32),
            pltpu.VMEM((2, 1, NV), F32),
            pltpu.VMEM((2, D, D), BF),
            pltpu.VMEM((chunk, D), BF),
            pltpu.VMEM((chunk, D), F32),
        ]
        + flats
        + [
            pltpu.SemaphoreType.DMA((amount,)),
            pltpu.SemaphoreType.DMA((amount,)),
            pltpu.SemaphoreType.DMA((80,)),
        ],
        compiler_params=pltpu.CompilerParams(
            collective_id=0, has_side_effects=True, vmem_limit_bytes=62 << 20
        ),
        name="forward",
    )(xb, xf, cotb, cotf, lens, *shards, vwin)


def norm_back(values, gain, grads):
    average = jnp.mean(values, axis=1, keepdims=True)
    centred = values - average
    scale = lax.rsqrt(jnp.mean(centred * centred, axis=1, keepdims=True) + EPSILON)
    unit = centred * scale
    by_gain = jnp.sum(grads * unit, axis=0, keepdims=True)
    by_bias = jnp.sum(grads, axis=0, keepdims=True)
    by_unit = grads * gain
    first = jnp.mean(by_unit, axis=1, keepdims=True)
    second = jnp.mean(by_unit * unit, axis=1, keepdims=True)
    return scale * (by_unit - first - unit * second), by_gain, by_bias


def backward_kernel(DP, S, R, *refs):
    (wq0, w10, w20, wq1, w11, w21) = refs[:6]
    s_x, s_h, s_qkv, s_o, s_lse, s_att, s_a, s_mid, s_n2, s_pre, s_u, s_y, s_vec = refs[6:19]
    s_wo, s_dy, lens = refs[19:22]
    x_u, x_n2, x_a, igr, r2, r1, rq, ro, gv = refs[22:31]
    (ub, nb, ab, preb, midb, attb, xb, hb, qkvb, ob, lseb) = refs[31:42]
    (wbig, wob, whb, vrow, dyb, dx1b, dub, dfb, sums) = refs[42:51]
    (dyc, dy_sib, df_sib, db_c, db_sib, do_out, do_in, dqkv, dk_acc, dv_acc) = refs[51:61]
    (dh_out, dh_in, dh2_out, dh2_in, ys, yb, cross_in, along_in) = refs[61:69]
    keeps = refs[69:73]
    slot_refs = refs[73:-3]
    send, recv, local = refs[-3:]
    c, dp, z = coords()
    t = jnp.where(c == 0, z, S - 1 - z)
    row = z // (S // 2)
    chunk = s_mid.shape[1]
    order_a, order_b = bit_orders(DP)
    steps = len(order_a)
    copies = Copies(send, recv)
    locs = Locals(local)
    sibling, partner, diagonal = (1 - c, dp, z), (c, dp, z ^ 1), (1 - c, dp, z ^ 1)
    crossing = (1 - c, dp, jnp.where(c == 0, z, S - 1 - z))
    greet(near_peers(c, dp, z, DP, S) + [diagonal, (1 - c, dp, S - 1 - z)])
    hold = {}

    def fetch(name, src, dst):
        hold[name] = locs.go(src, dst)

    def need(*names):
        for name in names:
            hold.pop(name).wait()

    sib = {}
    for layer in (1, 0):
        sib[layer, "u"] = copies.go(s_u.at[layer], x_u.at[layer], sibling)
        sib[layer, "n2"] = copies.go(s_n2.at[layer], x_n2.at[layer], sibling)
        sib[layer, "a"] = copies.go(s_a.at[layer], x_a.at[layer], sibling)

    half = S // 2
    groups = [[0], [1], [2], [3]]
    slots = {}
    at = 0
    for i in range(4):
        for step in range(steps + 2):
            for layer in range(2) if step < steps else [step - steps]:
                slots[layer, i, min(step, steps)] = slot_refs[at]
            at += 1
    results = [r2, r1, ro, rq]
    flights = {}
    sending = {}

    def sides():
        return ((0, order_a), (1, order_b))

    def beside(layer, g, step):
        found = []
        for i in groups[g]:
            for part, order in sides():
                bit = order[step]
                remain = subsets(order[step + 1 :])
                for at_, m in enumerate(remain):
                    found.append(
                        copies.go(
                            keeps[i].at[dp ^ m ^ bit, pl.ds(part * half, half)],
                            slots[layer, i, step].at[part * len(remain) + at_],
                            (c, dp ^ bit, z),
                        )
                    )
        flights[layer, g] = found
        sending.setdefault((layer, g), []).extend(found)

    def merge(layer, g, step):
        arrive(flights[layer, g])
        for i in groups[g]:
            for part, order in sides():
                remain = subsets(order[step + 1 :])
                for at_, m in enumerate(remain):
                    for e in range(half):
                        got = slots[layer, i, step][part * len(remain) + at_, e]
                        place = (dp ^ m, part * half + e)
                        keeps[i][place] = keeps[i][place] + got

    def across(layer, g):
        found = []
        for i in groups[g]:
            for k in range(1, S):
                found.append(
                    copies.go(
                        keeps[i].at[dp, z ^ k],
                        slots[layer, i, steps].at[k - 1],
                        (c, dp, z ^ k),
                    )
                )
        flights[layer, g] = found
        sending[layer, g].extend(found)

    def close(layer, g):
        arrive(flights[layer, g])
        for i in groups[g]:
            got = slots[layer, i, steps]
            own = keeps[i][dp, z].astype(F32)
            if i == 3:
                rq[layer, 0] = own
                for k in range(1, S):
                    rq[layer, k] = got[k - 1].astype(F32)
            else:
                for k in range(1, S):
                    own = own + got[k - 1].astype(F32)
                results[i][layer] = own
        copies.settle(sending.pop((layer, g)))

    def store(i, first, rows, value, lanes=slice(None)):
        value = value.astype(BF)
        size = keeps[i].shape[2]
        if size % 16 == 0:
            d, e = divmod(first // size, S)
            some = rows // size
            if some < S:
                keeps[i][d, e : e + some, :, lanes] = value.reshape(some, size, value.shape[1])
            else:
                keeps[i][d : d + some // S, :, :, lanes] = value.reshape(
                    some // S, S, size, value.shape[1]
                )
            return
        for n in range(rows // size):
            d, e = divmod(first // size + n, S)
            keeps[i][d, e, :, lanes] = value[n * size : (n + 1) * size]

    w_in = {0: (wq0, w10, w20), 1: (wq1, w11, w21)}

    def fetch_w2(layer):
        fetch("w2", w_in[layer][2], wbig)

    def fetch_w1(layer):
        for j in range(4):
            fetch(("w1", j), w_in[layer][1].at[:, j * D : (j + 1) * D], wbig.at[j])

    def fetch_u(layer, part):
        lanes = slice(part * (FF // 2), (part + 1) * (FF // 2))
        if part == 0:
            arrive([sib[layer, "u"]])
        fetch("u", s_u.at[layer, :, lanes], ub.at[0])
        fetch("u_sib", x_u.at[layer, :, lanes], ub.at[1])

    def fetch_pre(layer):
        fetch("pre", s_pre.at[layer], preb)

    def fetch_n2(layer):
        arrive([sib[layer, "n2"]])
        fetch("n2", s_n2.at[layer], nb.at[0])
        fetch("n2_sib", x_n2.at[layer], nb.at[1])

    def fetch_a(layer):
        arrive([sib[layer, "a"]])
        fetch("a", s_a.at[layer], ab.at[0])
        fetch("a_sib", x_a.at[layer], ab.at[1])

    def fetch_mid(layer):
        fetch("mid", s_mid.at[layer], midb)

    def fetch_att(layer):
        fetch("att", s_att.at[layer], attb)
        fetch("wo", s_wo.at[layer], wob)

    def fetch_heads(layer):
        fetch("qkv", s_qkv.at[layer], qkvb)
        fetch("o", s_o.at[layer], ob)
        fetch("lse", s_lse.at[layer], lseb)

    def fetch_h(layer):
        fetch("h", s_h.at[layer], hb)
        lanes = pl.ds(pl.multiple_of(t * D, 128), D)
        fetch("wh", w_in[layer][0].at[:, lanes], whb)
        fetch("x", s_x.at[layer], xb)

    def vec(layer, name):
        at_, size = PARTS[name]
        return vrow[layer, :, at_ : at_ + size]

    def put(layer, name, value, offset=0):
        at_ = PARTS[name][0] + offset
        gv[layer, :, at_ : at_ + value.shape[1]] = value

    def columns_of(value):
        return jnp.sum(value.astype(F32), axis=0, keepdims=True)

    def mine(ref, width, core):
        return ref[:, pl.ds(pl.multiple_of(core * width, 128), width)]

    def attention_back(layer):
        scale = HEAD_DIM ** (-0.5)
        for h in range(CHUNK_HEADS):
            low = h * HEAD_DIM
            lanes = slice(low, low + HEAD_DIM)
            klanes = slice(GW + low, GW + low + HEAD_DIM)
            vlanes = slice(2 * GW + low, 2 * GW + low + HEAD_DIM)
            for b in reversed(range(GROUP)):
                rows = slice(b * chunk, (b + 1) * chunk)
                upto = (b + 1) * chunk
                start = doc_start(lens, row, b * chunk, chunk)
                key = lax.broadcasted_iota(jnp.int32, (chunk, upto), 1)
                query = lax.broadcasted_iota(jnp.int32, (chunk, upto), 0) + b * chunk
                ok = (key >= start) & (key <= query)
                q = qkvb[rows, lanes]
                k = qkvb[0:upto, klanes]
                v = qkvb[0:upto, vlanes]
                do = do_in[layer, b, :, lanes]
                delta = jnp.sum(
                    do.astype(F32) * ob[b, :, lanes].astype(F32), axis=1, keepdims=True
                )
                s = jnp.where(ok, dot_nt(q, k) * scale, NEG_LARGE)
                p = jnp.exp(s - lseb[rows, h : h + 1])
                ds = (p * (dot_nt(do, v) - delta)).astype(BF)
                dqkv[rows, lanes] = (dot(ds, k) * scale).astype(BF)
                dk, dv = dot_tn(ds, q), dot_tn(p.astype(BF), do)
                if b == GROUP - 1:
                    dk_acc[...] = dk
                    dv_acc[...] = dv
                else:
                    dk_acc[0:upto, :] += dk
                    dv_acc[0:upto, :] += dv
            dqkv[:, klanes] = (dk_acc[...] * scale).astype(BF)
            dqkv[:, vlanes] = dv_acc[...].astype(BF)

    def inner_back(layer, part):
        block = 32
        if part == 0:
            sums[...] = jnp.zeros_like(sums)
        gs2 = vec(layer, "gs2")

        def fold(value):
            return jnp.sum(value.reshape(block // 8, 8, FF), axis=0)

        def one(i, carry):
            rows = pl.ds(pl.multiple_of(i * block + part * (chunk // 2), block), block)
            f = preb[rows, :]
            bell = 0.5 * (1.0 + lax.erf(f * np.float32(np.sqrt(0.5))))
            g = f * bell
            average = jnp.mean(g, axis=1, keepdims=True)
            centred = g - average
            scale = lax.rsqrt(jnp.mean(centred * centred, axis=1, keepdims=True) + EPSILON)
            unit = centred * scale
            du = dub[pl.ds(pl.multiple_of(i * block, block), block), :]
            sums[0] += fold(du * unit)
            sums[1] += fold(du)
            by_unit = du * gs2
            first = jnp.mean(by_unit, axis=1, keepdims=True)
            second = jnp.mean(by_unit * unit, axis=1, keepdims=True)
            dg = scale * (by_unit - first - unit * second)
            slope = bell + f * jnp.exp(-0.5 * f * f) * np.float32(1.0 / np.sqrt(2.0 * np.pi))
            df = (dg * slope).astype(BF)
            dfb[rows, :] = df
            sums[2] += fold(df.astype(F32))
            return carry

        lax.fori_loop(0, chunk // 2 // block, one, 0)
        if part == 0:
            return
        put(layer, "gs2", jnp.sum(sums[0], axis=0, keepdims=True))
        put(layer, "bs2", jnp.sum(sums[1], axis=0, keepdims=True))
        put(layer, "bf1", jnp.sum(sums[2], axis=0, keepdims=True))

    def layer_back(layer, hooks):
        dyc[...] = dyb[...].astype(BF)
        dy_copy = copies.go(
            dyc.at[:, half_lanes(1 - c, D // 2)], dy_sib.at[layer], sibling
        )
        put(layer, "bo2", columns_of(dyc[...]))
        hooks[0]()
        arrive([dy_copy])
        for part in range(2):
            need("u", "u_sib")
            for j in range(4):
                lanes = slice(j * (D // 2), (j + 1) * (D // 2))
                value = dot_tn(ub[0, :, lanes], mine(dyc, D // 2, c)) + dot_tn(
                    ub[1, :, lanes], dy_sib[layer]
                )
                store(0, part * (FF // 2) + j * (D // 2), D // 2, value)
            if part == 0:
                fetch_u(layer, 1)
        beside(layer, 0, 0)
        if layer == 1:
            fetch_u(0, 0)
        need("w2", "pre")
        for part in range(2):
            rows = slice(part * (chunk // 2), (part + 1) * (chunk // 2))
            for j in range(4):
                dub[:, j * D : (j + 1) * D] = dot_nt(dyc[rows, :], wbig[j])
            if part == 1:
                fetch_w1(layer)
            inner_back(layer, part)
        df_copy = copies.go(
            dfb.at[:, half_lanes(1 - c, FF // 2)], df_sib.at[layer], sibling
        )
        if layer == 1:
            fetch_pre(0)
        hooks[1]()
        total = jnp.zeros((chunk, D), F32)
        for j in range(4):
            need(("w1", j))
            total = total + dot_nt(dfb[:, j * D : (j + 1) * D], wbig[j])
        if layer == 1:
            fetch_w2(0)
        need("mid")
        part, by_gain, by_bias = norm_back(midb[...], vec(layer, "g2"), total)
        put(layer, "g2", by_gain)
        put(layer, "b2", by_bias)
        dx1b[...] = dyb[...] + part
        db_c[...] = dx1b[...].astype(BF)
        db_copy = copies.go(
            db_c.at[:, half_lanes(1 - c, D // 2)], db_sib.at[layer], sibling
        )
        put(layer, "bo", columns_of(db_c[...]))
        if layer == 1:
            fetch_mid(0)
        need("att", "wo")
        da = dot_nt(db_c[...], wob[...])
        part, by_gain, by_bias = norm_back(attb[...].astype(F32), vec(layer, "gs1"), da)
        put(layer, "gs1", by_gain)
        put(layer, "bs1", by_bias)
        do = part.astype(BF)
        for k in range(GROUP):
            do_out[k] = do[:, k * GW : (k + 1) * GW]
        do_copies = [
            copies.go(do_out.at[t ^ 1], do_in.at[layer, t], partner),
            copies.go(do_out.at[t ^ 3], do_in.at[layer, t], sibling),
            copies.go(do_out.at[t ^ 2], do_in.at[layer, t], diagonal),
        ]
        do_in[layer, t] = do_out[t]
        if layer == 1:
            fetch_att(0)
        need("n2", "n2_sib")
        arrive([df_copy])
        for j in range(2):
            lanes = slice(j * (D // 2), (j + 1) * (D // 2))
            for k in range(2):
                there = pl.ds(pl.multiple_of(c * (FF // 2) + k * D, 128), D)
                value = dot_tn(nb[0, :, lanes], dfb[:, there]) + dot_tn(
                    nb[1, :, lanes], df_sib[layer, :, k * D : (k + 1) * D]
                )
                store(1, j * (D // 2), D // 2, value, slice(k * D, (k + 1) * D))
        beside(layer, 1, 0)
        if layer == 1:
            fetch_n2(0)
        hooks[2]()
        need("a", "a_sib")
        arrive([db_copy])
        for j in range(2):
            lanes = slice(j * (D // 2), (j + 1) * (D // 2))
            value = dot_tn(ab[0, :, lanes], mine(db_c, D // 2, c)) + dot_tn(
                ab[1, :, lanes], db_sib[layer]
            )
            store(2, j * (D // 2), D // 2, value)
        beside(layer, 2, 0)
        if layer == 1:
            fetch_a(0)
        need("qkv", "o", "lse")
        arrive(do_copies)
        copies.settle(do_copies + [dy_copy, df_copy, db_copy])
        attention_back(layer)
        if layer == 1:
            fetch_heads(0)
        hooks[3]()
        need("h", "wh", "x")
        wq = whb[:, 0 : 3 * GW]

        def partial(k):
            rows = pl.ds(pl.multiple_of((t ^ k) * chunk, chunk), chunk)
            return dot_nt(dqkv[rows, :], wq)

        dh_out[0] = partial(3).astype(BF)
        dh_out[1] = partial(2).astype(BF)
        dh_copy = copies.go(dh_out, dh_in.at[layer], sibling)
        own, other = partial(0), partial(1)
        arrive([dh_copy])
        dh2_out[...] = (other + dh_in[layer, 1].astype(F32)).astype(BF)
        dh2_copy = copies.go(dh2_out, dh2_in.at[layer], partner)
        own = own + dh_in[layer, 0].astype(F32)
        for j in range(2):
            lanes = slice(j * (D // 2), (j + 1) * (D // 2))
            value = dot_tn(hb[:, lanes], dqkv[...])
            store(3, j * (D // 2), D // 2, value)
        beside(layer, 3, 0)
        sums_q = columns_of(dqkv[...])
        for k in range(GROUP):
            here = t == k
            put(layer, "bq", jnp.where(here, sums_q[:, 0:GW], 0.0), k * GW)
            put(layer, "bv", jnp.where(here, sums_q[:, 2 * GW : 3 * GW], 0.0), k * GW)
        arrive([dh2_copy])
        dh = own + dh2_in[layer].astype(F32)
        part, by_gain, by_bias = norm_back(xb[...], vec(layer, "g1"), dh)
        put(layer, "g1", by_gain)
        put(layer, "b1", by_bias)
        dyb[...] = dx1b[...] + part
        copies.settle([dh_copy, dh2_copy])
        if layer == 1:
            fetch_h(0)

    fetch("dy", s_dy, dyb)
    fetch("vec", s_vec, vrow)
    fetch_u(1, 0)
    fetch_w2(1)
    fetch_pre(1)
    fetch_mid(1)
    fetch_att(1)
    fetch_n2(1)
    fetch_a(1)
    fetch_heads(1)
    fetch_h(1)
    need("dy", "vec")

    def middle(layer, g):
        for step in range(steps - 1):
            merge(layer, g, step)
            beside(layer, g, step + 1)

    def final(layer, g):
        merge(layer, g, steps - 1)
        across(layer, g)

    def chain(*calls):
        def run():
            for call, layer, g in calls:
                call(layer, g)

        return run

    layer_back(
        1,
        [
            chain(),
            chain((middle, 1, 0)),
            chain((final, 1, 0)),
            chain((close, 1, 0), (middle, 1, 1), (middle, 1, 2)),
        ],
    )
    yb[...] = dyb[...].astype(BF)
    along = copies.go(yb, along_in, (c, dp, S - 1 - z))
    layer_back(
        0,
        [
            chain((final, 1, 1), (final, 1, 2)),
            chain((middle, 1, 3), (middle, 0, 0), (close, 1, 1), (close, 1, 2)),
            chain((final, 1, 3), (final, 0, 0)),
            chain((close, 1, 3), (close, 0, 0), (middle, 0, 1), (middle, 0, 2)),
        ],
    )
    ys[...] = jnp.where(c == 0, yb[...], dyb[...].astype(BF))
    crossed = copies.go(ys, cross_in, crossing)
    chain((final, 0, 1), (final, 0, 2), (middle, 0, 3), (close, 0, 1), (close, 0, 2))()
    chain((final, 0, 3))()
    arrive([crossed, along])
    got = cross_in[...].astype(F32)
    preb[:, 0:D] = jnp.where(c == 0, dyb[...], got)
    preb[:, D : 2 * D] = jnp.where(c == 0, got, along_in[...].astype(F32))
    out_copies = [
        locs.go(preb.at[:, 0:D], igr.at[row]),
        locs.go(preb.at[:, D : 2 * D], igr.at[1 - row]),
    ]
    close(0, 3)
    for copy in out_copies:
        copy.wait()
    copies.finish()
    locs.finish()


def backward_all(weights, saved, lens, DP, S, R):
    chunk = saved[7].shape[1]
    length = chunk * S
    steps = len(dp_bits(DP))
    tails = [(4 * R, D // 2), (R, FF // 2), (R, D // 2), (R, 3 * GW)]
    slots = []
    for tail in tails:
        for step in range(steps):
            slots.append(pltpu.VMEM((2 * (DP >> (step + 1)), S // 2) + tail, BF))
        slots.extend([pltpu.VMEM((S - 1,) + tail, BF)] * 2)
    anywhere = pl.BlockSpec(memory_space=pl.ANY)
    vmem = pl.BlockSpec(memory_space=pltpu.VMEM)
    outs = [
        ((2, chunk, FF), BF, anywhere),
        ((2, chunk, D), BF, anywhere),
        ((2, chunk, D), BF, anywhere),
        ((2, chunk, D), F32, anywhere),
        ((2,) + tails[0], F32, vmem),
        ((2,) + tails[1], F32, vmem),
        ((2, S) + tails[3], F32, vmem),
        ((2,) + tails[2], F32, vmem),
        ((2, 1, NV), F32, vmem),
    ]
    amount = 6 + 2 * (4 * (2 * (DP - 1) + S - 1) + 3 + 3 + 2) + 4
    return pl.pallas_call(
        functools.partial(backward_kernel, DP, S, R),
        out_shape=tuple(jax.ShapeDtypeStruct(shape, kind) for shape, kind, _ in outs),
        in_specs=[anywhere] * (6 + len(saved)) + [pl.BlockSpec(memory_space=pltpu.SMEM)],
        out_specs=tuple(spec for _, _, spec in outs),
        scratch_shapes=[
            pltpu.VMEM((2, chunk, FF // 2), BF),
            pltpu.VMEM((2, chunk, D), BF),
            pltpu.VMEM((2, chunk, D), BF),
            pltpu.VMEM((chunk, FF), F32),
            pltpu.VMEM((chunk, D), F32),
            pltpu.VMEM((chunk, D), BF),
            pltpu.VMEM((chunk, D), F32),
            pltpu.VMEM((length, D), BF),
            pltpu.VMEM((length, 3 * GW), BF),
            pltpu.VMEM((GROUP, chunk, GW), BF),
            pltpu.VMEM((length, CHUNK_HEADS), F32),
            pltpu.VMEM((4, D, D), BF),
            pltpu.VMEM((D, D), BF),
            pltpu.VMEM((D, D), BF),
            pltpu.VMEM((2, 1, NV), F32),
            pltpu.VMEM((chunk, D), F32),
            pltpu.VMEM((chunk, D), F32),
            pltpu.VMEM((chunk // 2, FF), F32),
            pltpu.VMEM((chunk, FF), BF),
            pltpu.VMEM((3, 8, FF), F32),
            pltpu.VMEM((chunk, D), BF),
            pltpu.VMEM((2, chunk, D // 2), BF),
            pltpu.VMEM((2, chunk, FF // 2), BF),
            pltpu.VMEM((chunk, D), BF),
            pltpu.VMEM((2, chunk, D // 2), BF),
            pltpu.VMEM((GROUP, chunk, GW), BF),
            pltpu.VMEM((2, GROUP, chunk, GW), BF),
            pltpu.VMEM((length, 3 * GW), BF),
            pltpu.VMEM((length, HEAD_DIM), F32),
            pltpu.VMEM((length, HEAD_DIM), F32),
            pltpu.VMEM((2, chunk, D), BF),
            pltpu.VMEM((2, 2, chunk, D), BF),
            pltpu.VMEM((chunk, D), BF),
            pltpu.VMEM((2, chunk, D), BF),
            pltpu.VMEM((chunk, D), BF),
            pltpu.VMEM((chunk, D), BF),
            pltpu.VMEM((chunk, D), BF),
            pltpu.VMEM((chunk, D), BF),
        ]
        + [pltpu.VMEM((DP, S) + tail, BF) for tail in tails]
        + slots
        + [
            pltpu.SemaphoreType.DMA((amount,)),
            pltpu.SemaphoreType.DMA((amount,)),
            pltpu.SemaphoreType.DMA((80,)),
        ],
        compiler_params=pltpu.CompilerParams(
            collective_id=1, has_side_effects=True, vmem_limit_bytes=63 << 20
        ),
        name="backward",
    )(*weights, *saved, lens)


def local(DP, S, *args):
    (
        block_input,
        cotangent,
        doc_lengths,
        w_qkv,
        w_out,
        w_fc1,
        w_fc2,
        vectors,
        vector_sq,
        rows_small,
        rows_fc2,
        columns,
    ) = args
    c, dp, z = coords()
    first = c == 0
    chunk = block_input.shape[1]
    length = chunk * S
    R = w_qkv.shape[1]
    row = z // (S // 2)
    t = jnp.where(first, z, S - 1 - z)

    zs = range(S)

    def swap_core(value):
        return lax.ppermute(value, "section", [(0, 1), (1, 0)])

    def swap_z(value, k):
        return lax.ppermute(value, "seq", [(i, i ^ k) for i in zs])

    def both(value, route):
        return lax.ppermute(
            value, ("section", "seq"), [(a * S + b, e * S + f) for (a, b), (e, f) in route]
        )

    def absolute(rel, me):
        odd = (me & 1) == 1
        high = (me & 2) == 2
        rel = [jnp.where(odd, rel[i ^ 1], rel[i]) for i in range(GROUP)]
        return [jnp.where(high, rel[i ^ 2], rel[i]) for i in range(GROUP)]

    by_head = jnp.concatenate(
        [
            part
            for k in range(GROUP)
            for part in [w_qkv[0][:, i * D + k * GW : i * D + (k + 1) * GW] for i in range(3)]
            + [w_out[0][:, k * GW : (k + 1) * GW]]
        ],
        axis=1,
    ).astype(BF)
    shards = [by_head, w_fc1[0].astype(BF), w_fc2[0].astype(BF).reshape(4, R, D)]
    shard_size = vectors.shape[1]
    place_at = (dp * S + z) * shard_size
    wide = window_rows(shard_size, DP * S)
    vwin = lax.dynamic_update_slice(
        jnp.zeros((wide * 128,), F32), vectors[0], (lax.rem(place_at, 128),)
    ).reshape(wide, 128)
    done = forward_all(
        block_input.astype(BF),
        block_input,
        cotangent.astype(BF),
        cotangent,
        doc_lengths,
        shards,
        vwin,
        DP,
        S,
    )
    kept_all = done[6:]
    weights = []
    for layer in range(2):
        qkvo, w1, w2 = done[3 * layer : 3 * layer + 3]
        weights += [qkvo.reshape(D, 4 * D), w1.reshape(D, FF), w2.reshape(4, D, D)]
    saved = list(kept_all)
    saved[1] = saved[1].reshape(2, length, D)
    back = backward_all(weights, saved, doc_lengths, DP, S, R)
    input_grads, r2, r1, rq, ro, packed = back[3:]
    input_grads = input_grads[None]
    red0, red1 = ([value[layer] for value in (r2, r1, rq, ro)] for layer in range(2))
    packed0, packed1 = packed[0, 0], packed[1, 0]
    y0, y1 = kept_all[11][0], kept_all[11][1]

    def place(v0, v1):
        crossed = both(
            jnp.where(first, v1, v0).astype(BF),
            [((0, b), (1, b)) for b in zs] + [((1, b), (0, S - 1 - b)) for b in zs],
        ).astype(F32)
        along = swap_z(v1.astype(BF), S - 1).astype(F32)
        row_own = jnp.where(first, v0, crossed)
        row_other = jnp.where(first, crossed, along)
        low = row == 0
        return jnp.stack([jnp.where(low, row_own, row_other), jnp.where(low, row_other, row_own)])[
            None
        ]

    activations = place(y0, y1)

    keep = [jnp.where(first, a, b) for a, b in zip(red0, red1)]
    got = [swap_core(jnp.where(first, b, a)) for a, b in zip(red0, red1)]

    def halves(mine, theirs, axis):
        return jnp.where(
            first,
            jnp.concatenate([mine, theirs], axis=axis),
            jnp.concatenate([theirs, mine], axis=axis),
        )

    reduced_fc2 = halves(keep[0], got[0], 1)
    reduced_fc1 = halves(keep[1], got[1], 1)
    reduced_out = halves(keep[3], got[3], 1)
    mine_q = jnp.stack(absolute([keep[2][i] for i in range(GROUP)], t))
    theirs_q = jnp.stack(absolute([got[2][i] for i in range(GROUP)], t ^ 3))
    slots = (mine_q + theirs_q).reshape(GROUP, R, 3, GW)
    reduced_qkv = slots.transpose(1, 2, 0, 3).reshape(R, 3 * D)
    grad_mats = [reduced_qkv, reduced_out, reduced_fc1, reduced_fc2]

    packed_own = jnp.where(first, packed0, packed1) + swap_core(
        jnp.where(first, packed1, packed0)
    )

    def total_over(value):
        for bit in dp_bits(DP):
            value = value + lax.ppermute(value, "dp", [(i, i ^ bit) for i in range(DP)])
        return value + sum(swap_z(value, k) for k in range(1, S))

    decay = 1.0 - STEP ** (-0.8)
    masters = [w_qkv[0], w_out[0], w_fc1[0], w_fc2[0]]
    row_olds = [rows_small[0, 0], rows_small[0, 1], rows_small[0, 2], rows_fc2[0]]
    col_widths = [3 * D, D, FF, D]
    row_counts = [D, D, D, FF]
    row_news = []
    col_parts = []
    weight_terms = []
    row_terms = []
    for index in range(4):
        squares = grad_mats[index] * grad_mats[index]
        row_new = decay * row_olds[index] + (1.0 - decay) * jnp.mean(squares, axis=1)
        row_news.append(row_new)
        col_parts.append(jnp.sum(squares, axis=0))
        weight_terms.append(jnp.sum(masters[index] * masters[index]))
        row_terms.append(jnp.sum(row_new))
    vec_master = vectors[0]
    ends = np.cumsum(np.array(segment_widths()))
    global_pos = place_at + jnp.arange(shard_size, dtype=jnp.int32)
    segment_of = jnp.sum(
        (global_pos[:, None] >= jnp.asarray(ends[:-1], jnp.int32)[None, :]).astype(jnp.int32),
        axis=1,
    )
    one_hot = (segment_of[:, None] == jnp.arange(13, dtype=jnp.int32)[None, :]).astype(F32)
    vec_weight_terms = jnp.dot(vec_master * vec_master, one_hot, precision=HIGHEST)
    sizes = np.cumsum([sum(col_widths), 8, 13])
    totals_one = total_over(
        jnp.concatenate(
            col_parts + [jnp.stack(weight_terms + row_terms), vec_weight_terms, packed_own]
        )
    )
    col_sums, scalars, vec_weights, vec_all = jnp.split(totals_one, sizes)
    vec_grad = lax.dynamic_slice(vec_all, (place_at,), (shard_size,))
    vec_sq_new = decay * vector_sq[0] + (1.0 - decay) * vec_grad * vec_grad
    vec_update = vec_grad * lax.rsqrt(vec_sq_new)
    col_news = []
    updates = []
    update_terms = []
    offset = 0
    for index in range(4):
        width = col_widths[index]
        col_new = (
            decay * columns[0, offset : offset + width]
            + (1.0 - decay) * col_sums[offset : offset + width] / row_counts[index]
        )
        offset += width
        col_news.append(col_new)
        mean_row = scalars[4 + index] / row_counts[index]
        estimate = row_news[index][:, None] * col_new[None, :] / mean_row
        update = grad_mats[index] * lax.rsqrt(estimate)
        updates.append(update)
        update_terms.append(jnp.sum(update * update))
    vec_update_terms = jnp.dot(vec_update * vec_update, one_hot, precision=HIGHEST)
    totals_two = total_over(jnp.concatenate([jnp.stack(update_terms), vec_update_terms]))
    new_mats = []
    for index in range(4):
        numel = row_counts[index] * col_widths[index]
        rms_update = jnp.sqrt(totals_two[index] / numel)
        rms_master = jnp.sqrt(scalars[index] / numel)
        new_mats.append(
            masters[index]
            - LEARN_RATE * rms_master / jnp.maximum(1.0, rms_update / CLIP_LEVEL) * updates[index]
        )
    seg_sizes = jnp.asarray(np.array(segment_widths()), F32)
    seg_factor = (
        LEARN_RATE
        * jnp.sqrt(vec_weights / seg_sizes)
        / jnp.maximum(1.0, jnp.sqrt(totals_two[4:] / seg_sizes) / CLIP_LEVEL)
    )
    new_vec = vec_master - jnp.dot(one_hot, seg_factor, precision=HIGHEST) * vec_update
    return (
        activations,
        input_grads,
        grad_mats[0][None],
        grad_mats[1][None],
        grad_mats[2][None],
        grad_mats[3][None],
        vec_grad[None],
        new_mats[0][None],
        new_mats[1][None],
        new_mats[2][None],
        new_mats[3][None],
        new_vec[None],
        vec_sq_new[None],
        jnp.stack(row_news[:3])[None],
        row_news[3][None],
        jnp.concatenate(col_news)[None],
    )


def solution(mesh):
    placed = (
        P("dp", "seq", None),
        P("dp", "seq", None),
        P("dp", None),
        P("section", ("dp", "seq"), None),
        P("section", ("dp", "seq"), None),
        P("section", ("dp", "seq"), None),
        P("section", ("dp", "seq"), None),
        P("section", ("dp", "seq")),
        P("section", ("dp", "seq")),
        P("section", None, ("dp", "seq")),
        P("section", ("dp", "seq")),
        P("section", None),
    )
    return jax.shard_map(
        functools.partial(local, mesh.shape["dp"], mesh.shape["seq"]),
        mesh=mesh,
        in_specs=placed,
        out_specs=(
            P("section", "dp", "seq", None),
            P("section", "dp", "seq", None),
            P("section", ("dp", "seq"), None),
            P("section", ("dp", "seq"), None),
            P("section", ("dp", "seq"), None),
            P("section", ("dp", "seq"), None),
            P("section", ("dp", "seq")),
            P("section", ("dp", "seq"), None),
            P("section", ("dp", "seq"), None),
            P("section", ("dp", "seq"), None),
            P("section", ("dp", "seq"), None),
            P("section", ("dp", "seq")),
            P("section", ("dp", "seq")),
            P("section", None, ("dp", "seq")),
            P("section", ("dp", "seq")),
            P("section", None),
        ),
        check_vma=False,
    )
```

```python
import functools

import jax
import jax.numpy as jnp
import numpy as np
from jax import lax
from jax.experimental import pallas as pl
from jax.experimental.pallas import tpu as pltpu
from jax.sharding import PartitionSpec as P

D = 768
FF = 3072
HEADS = 12
HEAD_DIM = 64
STEP = 10
NDOC = 4
NV = 10 * D + 3 * FF
GROUP = 4
GW = D // GROUP
CHUNK_HEADS = HEADS // GROUP

EPSILON = 1e-05
LEARN_RATE = 0.5
CLIP_LEVEL = 1.0
NEG_LARGE = -1e30
MESH = pl.DeviceIdType.MESH
BF = jnp.bfloat16
F32 = jnp.float32


def dp_bits(count):
    return [1 << i for i in range(count.bit_length() - 1)]


def bit_orders(count):
    bits = dp_bits(count)
    half = len(bits) // 2
    return (bits, bits[half:] + bits[:half])


def subsets(bits):
    found = [0]
    for bit in bits:
        found = found + [m | bit for m in found]
    return sorted(found)


class Copies:
    def __init__(self, send, recv):
        self.send, self.recv, self.used, self.started = send, recv, 0, []

    def go(self, src, dst, device):
        at = self.used
        self.used += 1
        copy = pltpu.make_async_remote_copy(
            src_ref=src,
            dst_ref=dst,
            send_sem=self.send.at[at],
            recv_sem=self.recv.at[at],
            device_id=device,
            device_id_type=MESH,
        )
        copy.start()
        self.started.append(copy)
        return copy

    def settle(self, some):
        for copy in some:
            copy.wait_send()
        gone = [id(copy) for copy in some]
        self.started = [copy for copy in self.started if id(copy) not in gone]

    def finish(self):
        self.settle(self.started)


def greet(peers):
    barrier = pltpu.get_barrier_semaphore()
    for peer in peers:
        pl.semaphore_signal(barrier, inc=1, device_id=peer, device_id_type=MESH)
    pl.semaphore_wait(barrier, len(peers))


def coords():
    return lax.axis_index("section"), lax.axis_index("dp"), lax.axis_index("seq")


def near_peers(c, dp, z, DP, S):
    return (
        [(1 - c, dp, z)]
        + [(c, dp, z ^ k) for k in range(1, S)]
        + [(c, dp ^ b, z) for b in dp_bits(DP)]
    )


def half_lanes(c, width):
    return pl.ds(pl.multiple_of(c * width, 128), width)


def sub_lanes(c, width, a):
    return pl.ds(pl.multiple_of(c * width + a * (width // 2), 128), width // 2)


class Locals:
    def __init__(self, sems):
        self.sems, self.used, self.open = sems, 0, []

    def go(self, src, dst):
        copy = pltpu.make_async_copy(src, dst, self.sems.at[self.used])
        self.used += 1
        copy.start()
        return copy

    def keep(self, src, dst):
        self.open.append(self.go(src, dst))

    def finish(self):
        for copy in self.open:
            copy.wait()


def arrive(some):
    for copy in some:
        copy.wait_recv()


def norm(values, gain, bias):
    average = jnp.mean(values, axis=1, keepdims=True)
    centred = values - average
    variance = jnp.mean(centred * centred, axis=1, keepdims=True)
    return centred * lax.rsqrt(variance + EPSILON) * gain + bias


def dot(left, right):
    return lax.dot_general(left, right, (((1,), (0,)), ((), ())), preferred_element_type=F32)


def dot_nt(left, right):
    return lax.dot_general(left, right, (((1,), (1,)), ((), ())), preferred_element_type=F32)


def dot_tn(left, right):
    return lax.dot_general(left, right, (((0,), (0,)), ((), ())), preferred_element_type=F32)


def pick(row_vector, t, width):
    total = jnp.where(t == 0, row_vector[:, 0:width], 0.0)
    for k in range(1, GROUP):
        total = total + jnp.where(t == k, row_vector[:, k * width : (k + 1) * width], 0.0)
    return total


def doc_start(lens, row, at, rows):
    pos = lax.broadcasted_iota(jnp.int32, (rows, 1), 0) + at
    bound = jnp.int32(0)
    start = jnp.zeros((rows, 1), jnp.int32)
    for j in range(NDOC):
        size = lens[row, j]
        bound = bound + size
        start = start + jnp.where(pos >= bound, size, 0)
    return start


PARTS = dict(
    g1=(0, D),
    b1=(D, D),
    bq=(2 * D, D),
    bv=(3 * D, D),
    gs1=(4 * D, D),
    bs1=(5 * D, D),
    bo=(6 * D, D),
    g2=(7 * D, D),
    b2=(8 * D, D),
    bo2=(9 * D, D),
    bf1=(10 * D, FF),
    gs2=(10 * D + FF, FF),
    bs2=(10 * D + 2 * FF, FF),
)


def window_rows(size, amount):
    most = max(((i * size) % 128 + size + 127) // 128 for i in range(amount))
    return (most + 7) // 8 * 8


def forward_kernel(DP, S, R, *refs):
    (xb, xf, cotb, cotf, lens, sh_c, sh_1, sh_2, vwin) = refs[:9]
    outs = refs[9:15]
    s_x, s_h, s_qkv, s_o, s_lse, s_att, s_a, s_mid, s_n2, s_pre, s_u, s_y, s_vec = refs[15:28]
    s_wo, s_dy = refs[28:30]
    (both_c, both_r, xr, x_own, hrow, qkv, o, lse, att4, att, a, mid, n2, pre, u, y) = refs[30:46]
    (gbuf, wh, wo, w1, w2, vall, vacc, vrow, wo_all, cotr, dy) = refs[46:57]
    flats = refs[57:-3]
    send, recv, local = refs[-3:]
    c, dp, z = coords()
    t = jnp.where(c == 0, z, S - 1 - z)
    row = z // (S // 2)
    chunk = xb.shape[1]
    order_a, order_b = bit_orders(DP)
    steps = len(order_a)
    copies = Copies(send, recv)
    locs = Locals(local)
    sibling, partner, diagonal = (1 - c, dp, z), (c, dp, z ^ 1), (1 - c, dp, z ^ 1)
    every = slice(None)
    greet(near_peers(c, dp, z, DP, S) + [diagonal])

    own_half = [
        locs.go(sh_c.at[:, half_lanes(c, FF // 2)], both_c.at[c, 0]),
        locs.go(sh_1.at[:, half_lanes(c, FF // 2)], both_c.at[c, 1]),
        locs.go(sh_2.at[pl.ds(2 * c, 2)], both_r.at[c]),
    ]
    give_half = [
        copies.go(sh_c.at[:, half_lanes(1 - c, FF // 2)], both_c.at[c, 0], sibling),
        copies.go(sh_1.at[:, half_lanes(1 - c, FF // 2)], both_c.at[c, 1], sibling),
        copies.go(sh_2.at[pl.ds(2 * (1 - c), 2)], both_r.at[c], sibling),
    ]
    vec_copies = [
        copies.go(vwin, vall.at[c, dp, z], (c, dp, z ^ k)) for k in range(1, S)
    ]
    far = jnp.where(c == 0, 3, 2)
    x_near = copies.go(xb.at[row], xr.at[z], partner)
    x_far = copies.go(xb.at[1 - row], xr.at[z], (c, dp, z ^ far))
    vall[c, dp, z] = vwin[...]
    xr[z] = xb[row]
    for copy in own_half:
        copy.wait()
    arrive(give_half)

    kinds = ["col", "col", "row"] * 2

    def shard(g):
        return both_r.at[g // 3] if kinds[g] == "row" else both_c.at[g // 3, g % 3]

    def cut(g, lead, part):
        if kinds[g] == "row":
            rows = pl.ds(2 * c, 2) if part is None else pl.ds(2 * c + part, 1)
            return outs[g].at[lead + (rows,)]
        lanes = half_lanes(c, FF // 2) if part is None else sub_lanes(c, FF // 2, part)
        return outs[g].at[lead + (every, lanes)]

    def across(g):
        return [copies.go(shard(g), cut(g, (dp, z), None), (c, dp, z ^ k)) for k in range(1, S)]

    def beside(g, step):
        found = []
        for part, order in ((0, order_a), (1, order_b)):
            peer = (c, dp ^ order[step], z)
            for m in subsets(order[:step]):
                place = cut(g, (dp ^ m, every), part)
                found.append(copies.go(place, place, peer))
        return found

    forwarded = [[] for _ in range(6)]

    def over_first(g):
        place = cut(g, (dp, every), None)
        forwarded[g].append(copies.go(place, place, sibling))

    def over(g, step):
        for part, order in ((0, order_a), (1, order_b)):
            for m in subsets(order[:step]):
                place = cut(g, (dp ^ m ^ order[step], every), part)
                forwarded[g].append(copies.go(place, place, sibling))

    own_place = [locs.go(shard(g), cut(g, (dp, z), None)) for g in range(6)]
    cross = [None] * 7
    cross[0] = across(0)

    def enter(g):
        own_place[g].wait()
        arrive(cross[g])
        started = beside(g, 0)
        if g + 1 < 6:
            cross[g + 1] = across(g + 1)
        over_first(g)
        return started

    def vec(layer, name):
        at, size = PARTS[name]
        return vrow[layer, :, at : at + size]

    def vectors_in():
        arrive(vec_copies)
        for step in range(steps):
            arrive(
                [
                    copies.go(
                        vall.at[c, dp ^ m], vall.at[c, dp ^ m], (c, dp ^ order_a[step], z)
                    )
                    for m in subsets(order_a[:step])
                ]
            )
        swapped = copies.go(vall.at[c], vall.at[c], sibling)
        arrive([swapped])
        size = NV // (DP * S)
        for layer in range(2):
            vacc[...] = jnp.zeros_like(vacc)
            for i in range(DP * S):
                first = i * size // 128
                count = vall.shape[3]
                vacc[first : first + count, :] += vall[layer, i // S, i % S]
            for i in range(NV // 128):
                vrow[layer, :, i * 128 : (i + 1) * 128] = (
                    vacc[i : i + 1, :].astype(BF).astype(F32)
                )
            locs.keep(vrow.at[layer], s_vec.at[layer])

    def x_in():
        arrive([x_near, x_far])
        x_over = copies.go(xr.at[z ^ far], xr.at[z ^ far], sibling)
        arrive([x_over])
        x_own[...] = jnp.where(c == 0, xf[row], xr[S - 1 - z].astype(F32))
        locs.keep(x_own, s_x.at[0])

    def to_flat(stage, flat_ref, leads, base=0):
        if flat_ref is None:
            return
        for i, lead in enumerate(leads):
            flat_ref[base + i * R : base + (i + 1) * R, :] = stage[lead]

    shards_at = [(d, e) for d in range(DP) for e in range(S)]
    aligned = R % 16 == 0
    f_wh, f_w1, f_w2 = (None,) * 3 if aligned else flats

    def load_qkvo(layer):
        got = [
            locs.go(outs[3 * layer].at[:, :, :, pl.ds(pl.multiple_of(t * D, 128), D)], wh)
        ] + [
            locs.go(outs[3 * layer].at[:, :, :, k * D + 512 : (k + 1) * D], wo.at[k])
            for k in range(GROUP)
        ]
        for copy in got:
            copy.wait()
        to_flat(wh, f_wh, shards_at)
        for k in range(GROUP):
            lanes = slice(k * GW, (k + 1) * GW)
            if aligned:
                wo_all[layer, :, lanes] = wo[k].reshape(D, 256)[:, 64:256]
            else:
                for i, lead in enumerate(shards_at):
                    wo_all[layer, i * R : (i + 1) * R, lanes] = wo[(k,) + lead][:, 64:256]
        locs.keep(wo_all.at[layer], s_wo.at[layer])

    def load_big(source, stage, flat_ref, tail):
        if aligned:
            locs.go(source, stage).wait()
            return
        some = stage.shape[0]
        leads = [(d, e) + j for d in range(some) for e in range(S) for j in tail]
        for q in range(DP // some):
            locs.go(source.at[q * some : (q + 1) * some], stage).wait()
            to_flat(stage, flat_ref, leads, q * len(leads) * R)

    def load_w1(layer):
        load_big(outs[3 * layer + 1], w1, f_w1, [()])

    def load_w2(layer):
        load_big(outs[3 * layer + 2], w2, f_w2, [(j,) for j in range(4)])

    def heads_w():
        return wh[:, :, :, 0:640].reshape(D, 640) if aligned else f_wh[:, 0:640]

    def w1_piece(j):
        lanes = slice(j * D, (j + 1) * D)
        return w1[:, :, :, lanes].reshape(D, D) if aligned else f_w1[:, lanes]

    def w2_piece(j):
        if not aligned:
            return f_w2[j * D : (j + 1) * D, :]
        some = DP // 4
        return w2[j * some : (j + 1) * some].reshape(D, D)

    def project(layer):
        biases = (pick(vec(layer, "bq"), t, GW), None, pick(vec(layer, "bv"), t, GW))
        for b in range(GROUP):
            if layer == 0:
                values = jnp.where(z == b, xf[row], xr[b].astype(F32))
                hrow[0, b] = norm(values, vec(0, "g1"), vec(0, "b1")).astype(BF)
            full = dot(hrow[layer, b], heads_w())
            for i in range(3):
                piece = full[:, i * GW : (i + 1) * GW]
                if biases[i] is not None:
                    piece = piece + biases[i]
                qkv[layer, b * chunk : (b + 1) * chunk, i * GW : (i + 1) * GW] = piece.astype(BF)

    def attention(layer):
        for b in range(GROUP):
            rows = slice(b * chunk, (b + 1) * chunk)
            upto = (b + 1) * chunk
            start = doc_start(lens, row, b * chunk, chunk)
            key = lax.broadcasted_iota(jnp.int32, (chunk, upto), 1)
            query = lax.broadcasted_iota(jnp.int32, (chunk, upto), 0) + b * chunk
            ok = (key >= start) & (key <= query)
            for h in range(CHUNK_HEADS):
                at = h * HEAD_DIM
                q = qkv[layer, rows, at : at + HEAD_DIM]
                k = qkv[layer, 0:upto, GW + at : GW + at + HEAD_DIM]
                v = qkv[layer, 0:upto, 2 * GW + at : 2 * GW + at + HEAD_DIM]
                s = jnp.where(ok, dot_nt(q, k) * HEAD_DIM ** (-0.5), NEG_LARGE)
                top = jnp.max(s, axis=1, keepdims=True)
                e = jnp.exp(s - top)
                total = jnp.sum(e, axis=1, keepdims=True)
                o[layer, b, :, at : at + HEAD_DIM] = (dot(e.astype(BF), v) / total).astype(BF)
                lse[layer, rows, h : h + 1] = top + jnp.log(total)

    waiting = {}

    def share(layer):
        waiting["o"] = [
            copies.go(o.at[layer, t ^ 1], att4.at[layer, t], partner),
            copies.go(o.at[layer, t ^ 3], att4.at[layer, t], sibling),
            copies.go(o.at[layer, t ^ 2], att4.at[layer, t], diagonal),
        ]
        att4[layer, t] = o[layer, t]
        locs.keep(qkv.at[layer], s_qkv.at[layer])
        locs.keep(o.at[layer], s_o.at[layer])
        locs.keep(lse.at[layer], s_lse.at[layer])
        locs.keep(hrow.at[layer], s_h.at[layer])

    def branch(layer):
        x = x_own if layer == 0 else y.at[0]
        arrive(waiting["o"])
        for k in range(GROUP):
            att[layer, :, k * GW : (k + 1) * GW] = att4[layer, k]
        a[layer] = norm(
            att[layer].astype(F32), vec(layer, "gs1"), vec(layer, "bs1")
        ).astype(BF)
        mid[layer] = x[...] + dot(a[layer], wo_all[layer]) + vec(layer, "bo")
        n2[layer] = norm(mid[layer], vec(layer, "g2"), vec(layer, "b2")).astype(BF)
        locs.keep(att.at[layer], s_att.at[layer])
        locs.keep(a.at[layer], s_a.at[layer])
        locs.keep(mid.at[layer], s_mid.at[layer])
        locs.keep(n2.at[layer], s_n2.at[layer])

    def inner(layer):
        bf1, gs2, bs2 = vec(layer, "bf1"), vec(layer, "gs2"), vec(layer, "bs2")
        total = jnp.zeros((chunk, 1), F32)
        for j in range(FF // D):
            lanes = slice(j * D, (j + 1) * D)
            f = dot(n2[layer], w1_piece(j)) + bf1[:, lanes]
            pre[layer, :, lanes] = f
            g = 0.5 * f * (1.0 + lax.erf(f * np.float32(np.sqrt(0.5))))
            gbuf[:, lanes] = g
            total = total + jnp.sum(g, axis=1, keepdims=True)
        average = total / FF
        square = jnp.zeros((chunk, 1), F32)
        for j in range(FF // D):
            centred = gbuf[:, j * D : (j + 1) * D] - average
            square = square + jnp.sum(centred * centred, axis=1, keepdims=True)
        scale = lax.rsqrt(square / FF + EPSILON)
        for j in range(FF // D):
            lanes = slice(j * D, (j + 1) * D)
            u[layer, :, lanes] = (
                (gbuf[:, lanes] - average) * scale * gs2[:, lanes] + bs2[:, lanes]
            ).astype(BF)
        locs.keep(pre.at[layer], s_pre.at[layer])
        locs.keep(u.at[layer], s_u.at[layer])

    def outer(layer):
        total = mid[layer] + vec(layer, "bo2")
        for j in range(FF // D):
            total = total + dot(u[layer, :, j * D : (j + 1) * D], w2_piece(j))
        y[layer] = total
        locs.keep(y.at[layer], s_y.at[layer])

    def pass_on():
        hrow[1, t] = norm(y[0], vec(1, "g1"), vec(1, "b1")).astype(BF)
        waiting["h"] = [
            copies.go(hrow.at[1, t], hrow.at[1, t], partner),
            copies.go(hrow.at[1, t], hrow.at[1, t], sibling),
        ]
        locs.keep(y.at[0], s_x.at[1])

    def row_in():
        arrive(waiting["h"])
        arrive([copies.go(hrow.at[1, t ^ 1], hrow.at[1, t ^ 1], sibling)])

    def compute(g):
        layer = g // 3
        arrive(forwarded[g])
        if g % 3 == 0:
            load_qkvo(layer)
            if layer == 1:
                row_in()
            project(layer)
            attention(layer)
            share(layer)
        elif g % 3 == 1:
            branch(layer)
            load_w1(layer)
            inner(layer)
        else:
            load_w2(layer)
            outer(layer)
            if layer == 0:
                pass_on()
                cotangent_in()

    def cotangent_in():
        copy = copies.go(cotb.at[1 - row], cotr, (c, dp, S - 1 - z))
        arrive([copy])
        dy[...] = jnp.where(c == 0, cotf[row], cotr[...].astype(F32))
        locs.keep(dy, s_dy)

    flight = [None] * 6
    vectors_in()
    x_in()
    flight[0] = enter(0)
    last = [None] * 6
    for g in range(6):
        for step in range(1, steps):
            arrive(flight[g])
            flight[g] = beside(g, step)
            over(g, step - 1)
        last[g] = flight[g]
        if g + 1 < 6:
            flight[g + 1] = enter(g + 1)
        if g > 0:
            arrive(last[g - 1])
            over(g - 1, steps - 1)
            compute(g - 1)
    arrive(last[5])
    over(5, steps - 1)
    compute(5)
    copies.finish()
    locs.finish()


def forward_all(xb, xf, cotb, cotf, lens, shards, vwin, DP, S):
    R = shards[0].shape[0]
    chunk = xb.shape[1]
    length = chunk * S
    col = jax.ShapeDtypeStruct((DP, S, R, FF), BF)
    row = jax.ShapeDtypeStruct((DP, S, 4, R, D), BF)
    kept = [
        ((2, chunk, D), F32),
        ((2, GROUP, chunk, D), BF),
        ((2, length, 3 * GW), BF),
        ((2, GROUP, chunk, GW), BF),
        ((2, length, CHUNK_HEADS), F32),
        ((2, chunk, D), BF),
        ((2, chunk, D), BF),
        ((2, chunk, D), F32),
        ((2, chunk, D), BF),
        ((2, chunk, FF), F32),
        ((2, chunk, FF), BF),
        ((2, chunk, D), F32),
        ((2, 1, NV), F32),
        ((2, D, D), BF),
        ((chunk, D), F32),
    ]
    flats = (
        []
        if R % 16 == 0
        else [
            pltpu.VMEM((D, D), BF),
            pltpu.VMEM((D, FF), BF),
            pltpu.VMEM((FF, D), BF),
        ]
    )
    staged = DP if R % 16 == 0 else DP // 4
    pieces = 2 * (DP - 1)
    amount = 3 + 6 * (S - 1 + 1 + 2 * pieces) + (S - 1) + (DP - 1) + 1 + 3 + 2 * 3 + 3 + 1
    anywhere = pl.BlockSpec(memory_space=pl.ANY)
    vmem = pl.BlockSpec(memory_space=pltpu.VMEM)
    return pl.pallas_call(
        functools.partial(forward_kernel, DP, S, R),
        out_shape=(col, col, row, col, col, row)
        + tuple(jax.ShapeDtypeStruct(shape, kind) for shape, kind in kept),
        in_specs=[vmem] * 4 + [pl.BlockSpec(memory_space=pltpu.SMEM)] + [vmem] * 4,
        out_specs=(anywhere,) * (6 + len(kept)),
        scratch_shapes=[
            pltpu.VMEM((2, 2, R, FF // 2), BF),
            pltpu.VMEM((2, 2, R, D), BF),
            pltpu.VMEM((GROUP, chunk, D), BF),
            pltpu.VMEM((chunk, D), F32),
            pltpu.VMEM((2, GROUP, chunk, D), BF),
            pltpu.VMEM((2, length, 3 * GW), BF),
            pltpu.VMEM((2, GROUP, chunk, GW), BF),
            pltpu.VMEM((2, length, CHUNK_HEADS), F32),
            pltpu.VMEM((2, GROUP, chunk, GW), BF),
            pltpu.VMEM((2, chunk, D), BF),
            pltpu.VMEM((2, chunk, D), BF),
            pltpu.VMEM((2, chunk, D), F32),
            pltpu.VMEM((2, chunk, D), BF),
            pltpu.VMEM((2, chunk, FF), F32),
            pltpu.VMEM((2, chunk, FF), BF),
            pltpu.VMEM((2, chunk, D), F32),
            pltpu.VMEM((chunk, FF), F32),
            pltpu.VMEM((DP, S, R, D), BF),
            pltpu.VMEM((GROUP, DP, S, R, 256), BF),
            pltpu.VMEM((staged, S, R, FF), BF),
            pltpu.VMEM((staged, S, 4, R, D), BF),
            pltpu.VMEM((2, DP, S) + vwin.shape, F32),
            pltpu.VMEM((NV // 128 + 16, 128), F32),
            pltpu.VMEM((2, 1, NV), F32),
            pltpu.VMEM((2, D, D), BF),
            pltpu.VMEM((chunk, D), BF),
            pltpu.VMEM((chunk, D), F32),
        ]
        + flats
        + [
            pltpu.SemaphoreType.DMA((amount,)),
            pltpu.SemaphoreType.DMA((amount,)),
            pltpu.SemaphoreType.DMA((80,)),
        ],
        compiler_params=pltpu.CompilerParams(
            collective_id=0, has_side_effects=True, vmem_limit_bytes=62 << 20
        ),
        name="forward",
    )(xb, xf, cotb, cotf, lens, *shards, vwin)


def norm_back(values, gain, grads):
    average = jnp.mean(values, axis=1, keepdims=True)
    centred = values - average
    scale = lax.rsqrt(jnp.mean(centred * centred, axis=1, keepdims=True) + EPSILON)
    unit = centred * scale
    by_gain = jnp.sum(grads * unit, axis=0, keepdims=True)
    by_bias = jnp.sum(grads, axis=0, keepdims=True)
    by_unit = grads * gain
    first = jnp.mean(by_unit, axis=1, keepdims=True)
    second = jnp.mean(by_unit * unit, axis=1, keepdims=True)
    return scale * (by_unit - first - unit * second), by_gain, by_bias


def backward_kernel(DP, S, R, *refs):
    (wq0, w10, w20, wq1, w11, w21) = refs[:6]
    s_x, s_h, s_qkv, s_o, s_lse, s_att, s_a, s_mid, s_n2, s_pre, s_u, s_y, s_vec = refs[6:19]
    s_wo, s_dy, lens = refs[19:22]
    x_u, x_n2, x_a, act, igr, r2, r1, rq, ro, gv = refs[22:32]
    (ub, nb, ab, preb, midb, attb, xb, hb, qkvb, ob, lseb) = refs[32:43]
    (wbig, wob, whb, vrow, dyb, dx1b, dub, dfb, sums) = refs[43:52]
    (dyc, dy_sib, df_sib, db_c, db_sib, do_out, do_in, dqkv, dk_acc, dv_acc) = refs[52:62]
    (dh_out, dh_in, dh2_out, dh2_in, ys, yb, cross_in, along_in) = refs[62:70]
    keeps = refs[70:74]
    slot_refs = refs[74:-3]
    send, recv, local = refs[-3:]
    c, dp, z = coords()
    t = jnp.where(c == 0, z, S - 1 - z)
    row = z // (S // 2)
    chunk = s_mid.shape[1]
    order_a, order_b = bit_orders(DP)
    steps = len(order_a)
    copies = Copies(send, recv)
    locs = Locals(local)
    sibling, partner, diagonal = (1 - c, dp, z), (c, dp, z ^ 1), (1 - c, dp, z ^ 1)
    crossing = (1 - c, dp, jnp.where(c == 0, z, S - 1 - z))
    greet(near_peers(c, dp, z, DP, S) + [diagonal, (1 - c, dp, S - 1 - z)])
    hold = {}

    def fetch(name, src, dst):
        hold[name] = locs.go(src, dst)

    def need(*names):
        for name in names:
            hold.pop(name).wait()

    sib = {}
    for layer in (1, 0):
        sib[layer, "u"] = copies.go(s_u.at[layer], x_u.at[layer], sibling)
        sib[layer, "n2"] = copies.go(s_n2.at[layer], x_n2.at[layer], sibling)
        sib[layer, "a"] = copies.go(s_a.at[layer], x_a.at[layer], sibling)

    half = S // 2
    groups = [[0], [1], [2], [3]]
    slots = {}
    at = 0
    for i in range(4):
        for step in range(steps + 2):
            for layer in range(2) if step < steps else [step - steps]:
                slots[layer, i, min(step, steps)] = slot_refs[at]
            at += 1
    results = [r2, r1, ro, rq]
    flights = {}
    sending = {}

    def sides():
        return ((0, order_a), (1, order_b))

    def beside(layer, g, step):
        found = []
        for i in groups[g]:
            for part, order in sides():
                bit = order[step]
                remain = subsets(order[step + 1 :])
                for at_, m in enumerate(remain):
                    found.append(
                        copies.go(
                            keeps[i].at[dp ^ m ^ bit, pl.ds(part * half, half)],
                            slots[layer, i, step].at[part * len(remain) + at_],
                            (c, dp ^ bit, z),
                        )
                    )
        flights[layer, g] = found
        sending.setdefault((layer, g), []).extend(found)

    def merge(layer, g, step):
        arrive(flights[layer, g])
        for i in groups[g]:
            for part, order in sides():
                remain = subsets(order[step + 1 :])
                for at_, m in enumerate(remain):
                    for e in range(half):
                        got = slots[layer, i, step][part * len(remain) + at_, e]
                        place = (dp ^ m, part * half + e)
                        keeps[i][place] = keeps[i][place] + got

    def across(layer, g):
        found = []
        for i in groups[g]:
            for k in range(1, S):
                found.append(
                    copies.go(
                        keeps[i].at[dp, z ^ k],
                        slots[layer, i, steps].at[k - 1],
                        (c, dp, z ^ k),
                    )
                )
        flights[layer, g] = found
        sending[layer, g].extend(found)

    def close(layer, g):
        arrive(flights[layer, g])
        for i in groups[g]:
            got = slots[layer, i, steps]
            own = keeps[i][dp, z].astype(F32)
            if i == 3:
                rq[layer, 0] = own
                for k in range(1, S):
                    rq[layer, k] = got[k - 1].astype(F32)
            else:
                for k in range(1, S):
                    own = own + got[k - 1].astype(F32)
                results[i][layer] = own
        copies.settle(sending.pop((layer, g)))

    def store(i, first, rows, value, lanes=slice(None)):
        value = value.astype(BF)
        size = keeps[i].shape[2]
        if size % 16 == 0:
            d, e = divmod(first // size, S)
            some = rows // size
            if some < S:
                keeps[i][d, e : e + some, :, lanes] = value.reshape(some, size, value.shape[1])
            else:
                keeps[i][d : d + some // S, :, :, lanes] = value.reshape(
                    some // S, S, size, value.shape[1]
                )
            return
        for n in range(rows // size):
            d, e = divmod(first // size + n, S)
            keeps[i][d, e, :, lanes] = value[n * size : (n + 1) * size]

    w_in = {0: (wq0, w10, w20), 1: (wq1, w11, w21)}

    def fetch_w2(layer):
        fetch("w2", w_in[layer][2], wbig)

    def fetch_w1(layer):
        for j in range(4):
            fetch(("w1", j), w_in[layer][1].at[:, j * D : (j + 1) * D], wbig.at[j])

    def fetch_u(layer, part):
        lanes = slice(part * (FF // 2), (part + 1) * (FF // 2))
        if part == 0:
            arrive([sib[layer, "u"]])
        fetch("u", s_u.at[layer, :, lanes], ub.at[0])
        fetch("u_sib", x_u.at[layer, :, lanes], ub.at[1])

    def fetch_pre(layer):
        fetch("pre", s_pre.at[layer], preb)

    def fetch_n2(layer):
        arrive([sib[layer, "n2"]])
        fetch("n2", s_n2.at[layer], nb.at[0])
        fetch("n2_sib", x_n2.at[layer], nb.at[1])

    def fetch_a(layer):
        arrive([sib[layer, "a"]])
        fetch("a", s_a.at[layer], ab.at[0])
        fetch("a_sib", x_a.at[layer], ab.at[1])

    def fetch_mid(layer):
        fetch("mid", s_mid.at[layer], midb)

    def fetch_att(layer):
        fetch("att", s_att.at[layer], attb)
        fetch("wo", s_wo.at[layer], wob)

    def fetch_heads(layer):
        fetch("qkv", s_qkv.at[layer], qkvb)
        fetch("o", s_o.at[layer], ob)
        fetch("lse", s_lse.at[layer], lseb)

    def fetch_h(layer):
        fetch("h", s_h.at[layer], hb)
        lanes = pl.ds(pl.multiple_of(t * D, 128), D)
        fetch("wh", w_in[layer][0].at[:, lanes], whb)
        fetch("x", s_x.at[layer], xb)

    def vec(layer, name):
        at_, size = PARTS[name]
        return vrow[layer, :, at_ : at_ + size]

    def put(layer, name, value, offset=0):
        at_ = PARTS[name][0] + offset
        gv[layer, :, at_ : at_ + value.shape[1]] = value

    def columns_of(value):
        return jnp.sum(value.astype(F32), axis=0, keepdims=True)

    def mine(ref, width, core):
        return ref[:, pl.ds(pl.multiple_of(core * width, 128), width)]

    def attention_back(layer):
        scale = HEAD_DIM ** (-0.5)
        for h in range(CHUNK_HEADS):
            low = h * HEAD_DIM
            lanes = slice(low, low + HEAD_DIM)
            klanes = slice(GW + low, GW + low + HEAD_DIM)
            vlanes = slice(2 * GW + low, 2 * GW + low + HEAD_DIM)
            for b in reversed(range(GROUP)):
                rows = slice(b * chunk, (b + 1) * chunk)
                upto = (b + 1) * chunk
                start = doc_start(lens, row, b * chunk, chunk)
                key = lax.broadcasted_iota(jnp.int32, (chunk, upto), 1)
                query = lax.broadcasted_iota(jnp.int32, (chunk, upto), 0) + b * chunk
                ok = (key >= start) & (key <= query)
                q = qkvb[rows, lanes]
                k = qkvb[0:upto, klanes]
                v = qkvb[0:upto, vlanes]
                do = do_in[layer, b, :, lanes]
                delta = jnp.sum(
                    do.astype(F32) * ob[b, :, lanes].astype(F32), axis=1, keepdims=True
                )
                s = jnp.where(ok, dot_nt(q, k) * scale, NEG_LARGE)
                p = jnp.exp(s - lseb[rows, h : h + 1])
                ds = (p * (dot_nt(do, v) - delta)).astype(BF)
                dqkv[rows, lanes] = (dot(ds, k) * scale).astype(BF)
                dk, dv = dot_tn(ds, q), dot_tn(p.astype(BF), do)
                if b == GROUP - 1:
                    dk_acc[...] = dk
                    dv_acc[...] = dv
                else:
                    dk_acc[0:upto, :] += dk
                    dv_acc[0:upto, :] += dv
            dqkv[:, klanes] = (dk_acc[...] * scale).astype(BF)
            dqkv[:, vlanes] = dv_acc[...].astype(BF)

    def inner_back(layer, part):
        block = 32
        if part == 0:
            sums[...] = jnp.zeros_like(sums)
        gs2 = vec(layer, "gs2")

        def fold(value):
            return jnp.sum(value.reshape(block // 8, 8, FF), axis=0)

        def one(i, carry):
            rows = pl.ds(pl.multiple_of(i * block + part * (chunk // 2), block), block)
            f = preb[rows, :]
            bell = 0.5 * (1.0 + lax.erf(f * np.float32(np.sqrt(0.5))))
            g = f * bell
            average = jnp.mean(g, axis=1, keepdims=True)
            centred = g - average
            scale = lax.rsqrt(jnp.mean(centred * centred, axis=1, keepdims=True) + EPSILON)
            unit = centred * scale
            du = dub[pl.ds(pl.multiple_of(i * block, block), block), :]
            sums[0] += fold(du * unit)
            sums[1] += fold(du)
            by_unit = du * gs2
            first = jnp.mean(by_unit, axis=1, keepdims=True)
            second = jnp.mean(by_unit * unit, axis=1, keepdims=True)
            dg = scale * (by_unit - first - unit * second)
            slope = bell + f * jnp.exp(-0.5 * f * f) * np.float32(1.0 / np.sqrt(2.0 * np.pi))
            df = (dg * slope).astype(BF)
            dfb[rows, :] = df
            sums[2] += fold(df.astype(F32))
            return carry

        lax.fori_loop(0, chunk // 2 // block, one, 0)
        if part == 0:
            return
        put(layer, "gs2", jnp.sum(sums[0], axis=0, keepdims=True))
        put(layer, "bs2", jnp.sum(sums[1], axis=0, keepdims=True))
        put(layer, "bf1", jnp.sum(sums[2], axis=0, keepdims=True))

    def layer_back(layer, hooks):
        dyc[...] = dyb[...].astype(BF)
        dy_copy = copies.go(
            dyc.at[:, half_lanes(1 - c, D // 2)], dy_sib.at[layer], sibling
        )
        put(layer, "bo2", columns_of(dyc[...]))
        hooks[0]()
        arrive([dy_copy])
        for part in range(2):
            need("u", "u_sib")
            for j in range(4):
                lanes = slice(j * (D // 2), (j + 1) * (D // 2))
                value = dot_tn(ub[0, :, lanes], mine(dyc, D // 2, c)) + dot_tn(
                    ub[1, :, lanes], dy_sib[layer]
                )
                store(0, part * (FF // 2) + j * (D // 2), D // 2, value)
            if part == 0:
                fetch_u(layer, 1)
        beside(layer, 0, 0)
        if layer == 1:
            fetch_u(0, 0)
        need("w2", "pre")
        for part in range(2):
            rows = slice(part * (chunk // 2), (part + 1) * (chunk // 2))
            for j in range(4):
                dub[:, j * D : (j + 1) * D] = dot_nt(dyc[rows, :], wbig[j])
            if part == 1:
                fetch_w1(layer)
            inner_back(layer, part)
        df_copy = copies.go(
            dfb.at[:, half_lanes(1 - c, FF // 2)], df_sib.at[layer], sibling
        )
        if layer == 1:
            fetch_pre(0)
        hooks[1]()
        total = jnp.zeros((chunk, D), F32)
        for j in range(4):
            need(("w1", j))
            total = total + dot_nt(dfb[:, j * D : (j + 1) * D], wbig[j])
        if layer == 1:
            fetch_w2(0)
        need("mid")
        part, by_gain, by_bias = norm_back(midb[...], vec(layer, "g2"), total)
        put(layer, "g2", by_gain)
        put(layer, "b2", by_bias)
        dx1b[...] = dyb[...] + part
        db_c[...] = dx1b[...].astype(BF)
        db_copy = copies.go(
            db_c.at[:, half_lanes(1 - c, D // 2)], db_sib.at[layer], sibling
        )
        put(layer, "bo", columns_of(db_c[...]))
        if layer == 1:
            fetch_mid(0)
        need("att", "wo")
        da = dot_nt(db_c[...], wob[...])
        part, by_gain, by_bias = norm_back(attb[...].astype(F32), vec(layer, "gs1"), da)
        put(layer, "gs1", by_gain)
        put(layer, "bs1", by_bias)
        do = part.astype(BF)
        for k in range(GROUP):
            do_out[k] = do[:, k * GW : (k + 1) * GW]
        do_copies = [
            copies.go(do_out.at[t ^ 1], do_in.at[layer, t], partner),
            copies.go(do_out.at[t ^ 3], do_in.at[layer, t], sibling),
            copies.go(do_out.at[t ^ 2], do_in.at[layer, t], diagonal),
        ]
        do_in[layer, t] = do_out[t]
        if layer == 1:
            fetch_att(0)
        need("n2", "n2_sib")
        arrive([df_copy])
        for j in range(2):
            lanes = slice(j * (D // 2), (j + 1) * (D // 2))
            for k in range(2):
                there = pl.ds(pl.multiple_of(c * (FF // 2) + k * D, 128), D)
                value = dot_tn(nb[0, :, lanes], dfb[:, there]) + dot_tn(
                    nb[1, :, lanes], df_sib[layer, :, k * D : (k + 1) * D]
                )
                store(1, j * (D // 2), D // 2, value, slice(k * D, (k + 1) * D))
        beside(layer, 1, 0)
        if layer == 1:
            fetch_n2(0)
        hooks[2]()
        need("a", "a_sib")
        arrive([db_copy])
        for j in range(2):
            lanes = slice(j * (D // 2), (j + 1) * (D // 2))
            value = dot_tn(ab[0, :, lanes], mine(db_c, D // 2, c)) + dot_tn(
                ab[1, :, lanes], db_sib[layer]
            )
            store(2, j * (D // 2), D // 2, value)
        beside(layer, 2, 0)
        if layer == 1:
            fetch_a(0)
        need("qkv", "o", "lse")
        arrive(do_copies)
        copies.settle(do_copies + [dy_copy, df_copy, db_copy])
        attention_back(layer)
        if layer == 1:
            fetch_heads(0)
        hooks[3]()
        need("h", "wh", "x")
        wq = whb[:, 0 : 3 * GW]

        def partial(k):
            rows = pl.ds(pl.multiple_of((t ^ k) * chunk, chunk), chunk)
            return dot_nt(dqkv[rows, :], wq)

        dh_out[0] = partial(3).astype(BF)
        dh_out[1] = partial(2).astype(BF)
        dh_copy = copies.go(dh_out, dh_in.at[layer], sibling)
        own, other = partial(0), partial(1)
        arrive([dh_copy])
        dh2_out[...] = (other + dh_in[layer, 1].astype(F32)).astype(BF)
        dh2_copy = copies.go(dh2_out, dh2_in.at[layer], partner)
        own = own + dh_in[layer, 0].astype(F32)
        for j in range(2):
            lanes = slice(j * (D // 2), (j + 1) * (D // 2))
            value = dot_tn(hb[:, lanes], dqkv[...])
            store(3, j * (D // 2), D // 2, value)
        beside(layer, 3, 0)
        sums_q = columns_of(dqkv[...])
        for k in range(GROUP):
            here = t == k
            put(layer, "bq", jnp.where(here, sums_q[:, 0:GW], 0.0), k * GW)
            put(layer, "bv", jnp.where(here, sums_q[:, 2 * GW : 3 * GW], 0.0), k * GW)
        arrive([dh2_copy])
        dh = own + dh2_in[layer].astype(F32)
        part, by_gain, by_bias = norm_back(xb[...], vec(layer, "g1"), dh)
        put(layer, "g1", by_gain)
        put(layer, "b1", by_bias)
        dyb[...] = dx1b[...] + part
        copies.settle([dh_copy, dh2_copy])
        if layer == 1:
            fetch_h(0)

    act_cross = copies.go(s_y.at[1 - c], act.at[row], crossing)
    act_along = pltpu.make_async_remote_copy(
        src_ref=s_y.at[1],
        dst_ref=act.at[row],
        send_sem=send.at[copies.used],
        recv_sem=recv.at[copies.used],
        device_id=(c, dp, S - 1 - z),
        device_id_type=MESH,
    )
    copies.used += 1
    act_own = pltpu.make_async_copy(s_y.at[0], act.at[row], local.at[79])

    @pl.when(c == 0)
    def _():
        act_own.start()

    @pl.when(c == 1)
    def _():
        act_along.start()

    fetch("dy", s_dy, dyb)
    fetch("vec", s_vec, vrow)
    fetch_u(1, 0)
    fetch_w2(1)
    fetch_pre(1)
    fetch_mid(1)
    fetch_att(1)
    fetch_n2(1)
    fetch_a(1)
    fetch_heads(1)
    fetch_h(1)
    need("dy", "vec")

    def middle(layer, g):
        for step in range(steps - 1):
            merge(layer, g, step)
            beside(layer, g, step + 1)

    def final(layer, g):
        merge(layer, g, steps - 1)
        across(layer, g)

    def chain(*calls):
        def run():
            for call, layer, g in calls:
                call(layer, g)

        return run

    layer_back(
        1,
        [
            chain(),
            chain((middle, 1, 0)),
            chain((final, 1, 0)),
            chain((close, 1, 0), (middle, 1, 1), (middle, 1, 2)),
        ],
    )
    yb[...] = dyb[...].astype(BF)
    along = copies.go(yb, along_in, (c, dp, S - 1 - z))
    layer_back(
        0,
        [
            chain((final, 1, 1), (final, 1, 2)),
            chain((middle, 1, 3), (middle, 0, 0), (close, 1, 1), (close, 1, 2)),
            chain((final, 1, 3), (final, 0, 0)),
            chain((close, 1, 3), (close, 0, 0), (middle, 0, 1), (middle, 0, 2)),
        ],
    )
    ys[...] = jnp.where(c == 0, yb[...], dyb[...].astype(BF))
    crossed = copies.go(ys, cross_in, crossing)
    chain((final, 0, 1), (final, 0, 2), (middle, 0, 3), (close, 0, 1), (close, 0, 2))()
    chain((final, 0, 3))()
    arrive([crossed, along])
    got = cross_in[...].astype(F32)
    preb[:, 0:D] = jnp.where(c == 0, dyb[...], got)
    preb[:, D : 2 * D] = jnp.where(c == 0, got, along_in[...].astype(F32))
    out_copies = [
        locs.go(preb.at[:, 0:D], igr.at[row]),
        locs.go(preb.at[:, D : 2 * D], igr.at[1 - row]),
    ]
    close(0, 3)
    for copy in out_copies:
        copy.wait()
    arrive([act_cross])

    @pl.when(c == 0)
    def _():
        act_own.wait()

    @pl.when(c == 1)
    def _():
        act_along.wait()

    copies.finish()
    locs.finish()


def backward_all(weights, saved, lens, DP, S, R):
    chunk = saved[7].shape[1]
    length = chunk * S
    steps = len(dp_bits(DP))
    tails = [(4 * R, D // 2), (R, FF // 2), (R, D // 2), (R, 3 * GW)]
    slots = []
    for tail in tails:
        for step in range(steps):
            slots.append(pltpu.VMEM((2 * (DP >> (step + 1)), S // 2) + tail, BF))
        slots.extend([pltpu.VMEM((S - 1,) + tail, BF)] * 2)
    anywhere = pl.BlockSpec(memory_space=pl.ANY)
    vmem = pl.BlockSpec(memory_space=pltpu.VMEM)
    outs = [
        ((2, chunk, FF), BF, anywhere),
        ((2, chunk, D), BF, anywhere),
        ((2, chunk, D), BF, anywhere),
        ((2, chunk, D), F32, anywhere),
        ((2, chunk, D), F32, anywhere),
        ((2,) + tails[0], F32, vmem),
        ((2,) + tails[1], F32, vmem),
        ((2, S) + tails[3], F32, vmem),
        ((2,) + tails[2], F32, vmem),
        ((2, 1, NV), F32, vmem),
    ]
    amount = 6 + 2 * (4 * (2 * (DP - 1) + S - 1) + 3 + 3 + 2) + 4
    return pl.pallas_call(
        functools.partial(backward_kernel, DP, S, R),
        out_shape=tuple(jax.ShapeDtypeStruct(shape, kind) for shape, kind, _ in outs),
        in_specs=[anywhere] * (6 + len(saved)) + [pl.BlockSpec(memory_space=pltpu.SMEM)],
        out_specs=tuple(spec for _, _, spec in outs),
        scratch_shapes=[
            pltpu.VMEM((2, chunk, FF // 2), BF),
            pltpu.VMEM((2, chunk, D), BF),
            pltpu.VMEM((2, chunk, D), BF),
            pltpu.VMEM((chunk, FF), F32),
            pltpu.VMEM((chunk, D), F32),
            pltpu.VMEM((chunk, D), BF),
            pltpu.VMEM((chunk, D), F32),
            pltpu.VMEM((length, D), BF),
            pltpu.VMEM((length, 3 * GW), BF),
            pltpu.VMEM((GROUP, chunk, GW), BF),
            pltpu.VMEM((length, CHUNK_HEADS), F32),
            pltpu.VMEM((4, D, D), BF),
            pltpu.VMEM((D, D), BF),
            pltpu.VMEM((D, D), BF),
            pltpu.VMEM((2, 1, NV), F32),
            pltpu.VMEM((chunk, D), F32),
            pltpu.VMEM((chunk, D), F32),
            pltpu.VMEM((chunk // 2, FF), F32),
            pltpu.VMEM((chunk, FF), BF),
            pltpu.VMEM((3, 8, FF), F32),
            pltpu.VMEM((chunk, D), BF),
            pltpu.VMEM((2, chunk, D // 2), BF),
            pltpu.VMEM((2, chunk, FF // 2), BF),
            pltpu.VMEM((chunk, D), BF),
            pltpu.VMEM((2, chunk, D // 2), BF),
            pltpu.VMEM((GROUP, chunk, GW), BF),
            pltpu.VMEM((2, GROUP, chunk, GW), BF),
            pltpu.VMEM((length, 3 * GW), BF),
            pltpu.VMEM((length, HEAD_DIM), F32),
            pltpu.VMEM((length, HEAD_DIM), F32),
            pltpu.VMEM((2, chunk, D), BF),
            pltpu.VMEM((2, 2, chunk, D), BF),
            pltpu.VMEM((chunk, D), BF),
            pltpu.VMEM((2, chunk, D), BF),
            pltpu.VMEM((chunk, D), BF),
            pltpu.VMEM((chunk, D), BF),
            pltpu.VMEM((chunk, D), BF),
            pltpu.VMEM((chunk, D), BF),
        ]
        + [pltpu.VMEM((DP, S) + tail, BF) for tail in tails]
        + slots
        + [
            pltpu.SemaphoreType.DMA((amount,)),
            pltpu.SemaphoreType.DMA((amount,)),
            pltpu.SemaphoreType.DMA((80,)),
        ],
        compiler_params=pltpu.CompilerParams(
            collective_id=1, has_side_effects=True, vmem_limit_bytes=63 << 20
        ),
        name="backward",
    )(*weights, *saved, lens)


MATS = [("q", 3 * D, D), ("o", D, D), ("1", FF, D), ("2", D, FF)]
COLS = 3 * D + D + FF + D
DECAY = 1.0 - STEP ** (-0.8)


def total_of(value):
    return jnp.sum(jnp.sum(value, axis=1, keepdims=True), axis=0, keepdims=True)


def lanes_of(values, width=128):
    lane = lax.broadcasted_iota(jnp.int32, (1, width), 1)
    row = jnp.zeros((1, width), F32)
    for i, value in enumerate(values):
        row = row + jnp.where(lane == i, value, 0.0)
    return row


def square_mask(size):
    shape = (size, size)
    return lax.broadcasted_iota(jnp.int32, shape, 0) == lax.broadcasted_iota(jnp.int32, shape, 1)


def upright(row_vector):
    size = row_vector.shape[1]
    return jnp.sum(jnp.where(square_mask(size), row_vector, 0.0), axis=1, keepdims=True)


def level(column):
    size = column.shape[0]
    return jnp.sum(jnp.where(square_mask(size), column, 0.0), axis=0, keepdims=True)


def sums_kernel(DP, S, R, n, *refs):
    r2, r1, rq, ro, gv, wq, wo, w1, w2, vec, vsq, rows_small, rows_fc2, columns = refs[:14]
    gq, go, g1, g2, acol, acol2, bcol, scal, rowv, rowf, coln, vout = refs[14:26]
    got2, got1, gotq, goto, gotv, mine, slots, mine2, slots2, send, recv = refs[26:]
    c, dp, z = coords()
    t = jnp.where(c == 0, z, S - 1 - z)
    sibling = (1 - c, dp, z)
    copies = Copies(send, recv)
    greet(near_peers(c, dp, z, DP, S))
    other = 1 - c
    swaps = [
        copies.go(r2.at[other], got2, sibling),
        copies.go(r1.at[other], got1, sibling),
        copies.go(rq.at[other], gotq, sibling),
        copies.go(ro.at[other], goto, sibling),
        copies.go(gv.at[other], gotv, sibling),
    ]

    def over_devices(value, here, slots_):
        for step, bit in enumerate(dp_bits(DP)):
            here[...] = value
            copy = copies.go(here, slots_.at[step], (c, dp ^ bit, z))
            arrive([copy])
            copies.settle([copy])
            value = value + slots_[step]
        here[...] = value
        first = len(dp_bits(DP))
        some = [
            copies.go(here, slots_.at[first + k - 1], (c, dp, z ^ k)) for k in range(1, S)
        ]
        arrive(some)
        for k in range(1, S):
            value = value + slots_[first + k - 1]
        copies.settle(some)
        return value

    masters = [wq, wo, w1, w2]
    weight_terms = [total_of(w[0] * w[0]) for w in masters]
    place_at = (dp * S + z) * n
    pos = lax.broadcasted_iota(jnp.int32, (1, n), 1) + place_at
    inside = [
        (pos >= at) & (pos < at + size) for at, size in PARTS.values()
    ]
    vec_weights = [
        jnp.sum(jnp.where(here, vec[...] * vec[...], 0.0), axis=1, keepdims=True)
        for here in inside
    ]

    arrive(swaps)
    wide = half_lanes(c, D // 2), half_lanes(1 - c, D // 2)
    g2[:, wide[0]] = r2[c]
    g2[:, wide[1]] = got2[...]
    go[:, wide[0]] = ro[c]
    go[:, wide[1]] = goto[...]
    g1[:, half_lanes(c, FF // 2)] = r1[c]
    g1[:, half_lanes(1 - c, FF // 2)] = got1[...]
    for k in range(GROUP):
        value = rq[c, t ^ k] + gotq[t ^ 3 ^ k]
        for i in range(3):
            gq[:, i * D + k * GW : i * D + (k + 1) * GW] = value[:, i * GW : (i + 1) * GW]
    grads = [gq, go, g1, g2]

    row_news = []
    col_parts = []
    for i, (_, width, _) in enumerate(MATS):
        squares = grads[i][...] * grads[i][...]
        old = upright(rows_fc2[...] if i == 3 else rows_small[0, i : i + 1, :])
        row_news.append(
            DECAY * old + (1.0 - DECAY) * (jnp.sum(squares, axis=1, keepdims=True) / width)
        )
        col_parts.append(jnp.sum(squares, axis=0, keepdims=True))
        if i == 3:
            rowf[...] = level(row_news[3])
        else:
            rowv[0, i : i + 1, :] = level(row_news[i])
    row_terms = [jnp.sum(row_new, axis=0, keepdims=True) for row_new in row_news]
    value = jnp.concatenate(
        col_parts + [gv[c] + gotv[...], lanes_of(weight_terms + row_terms + vec_weights)],
        axis=1,
    )
    value = over_devices(value, mine, slots)
    numbers = value[:, COLS + NV :]

    def number(i):
        return numbers[:, i : i + 1]

    base = pl.multiple_of(place_at // 128 * 128, 128)
    reach = -(-(n + 127) // 128) * 128
    mine[:, COLS : COLS + NV] = value[:, COLS : COLS + NV]
    window = mine[:, pl.ds(COLS + base, reach)]
    skew = place_at - base
    vec_grad = jnp.zeros((1, n), F32)
    for at in sorted({(i * n) % 128 for i in range(DP * S)}):
        vec_grad = vec_grad + jnp.where(skew == at, window[:, at : at + n], 0.0)
    vsq_new = DECAY * vsq[...] + (1.0 - DECAY) * vec_grad * vec_grad
    vec_update = vec_grad * lax.rsqrt(vsq_new)

    terms = []
    offset = 0
    for i, (_, width, count) in enumerate(MATS):
        col_new = (
            DECAY * columns[:, offset : offset + width]
            + (1.0 - DECAY) * value[:, offset : offset + width] / count
        )
        coln[:, offset : offset + width] = col_new
        by_col = lax.rsqrt(col_new)
        bcol[:, offset : offset + width] = by_col
        offset += width
        by_row = lax.rsqrt(row_news[i] / (number(4 + i) / count))
        if i == 3:
            acol2[...] = by_row
        else:
            acol[:, i : i + 1] = by_row
        update = grads[i][...] * by_row * by_col
        terms.append(total_of(update * update))
    terms += [
        jnp.sum(jnp.where(here, vec_update * vec_update, 0.0), axis=1, keepdims=True)
        for here in inside
    ]
    second = over_devices(lanes_of(terms), mine2, slots2)
    factors = []
    for i, (_, width, count) in enumerate(MATS):
        size = width * count
        rms_update = jnp.sqrt(second[:, i : i + 1] / size)
        rms_master = jnp.sqrt(number(i) / size)
        factors.append(LEARN_RATE * rms_master / jnp.maximum(1.0, rms_update / CLIP_LEVEL))
    scal[...] = lanes_of(factors)
    by_place = jnp.zeros((1, n), F32)
    for j, (here, (_, size)) in enumerate(zip(inside, PARTS.values())):
        rms_update = jnp.sqrt(second[:, 4 + j : 5 + j] / size)
        rms_master = jnp.sqrt(number(8 + j) / size)
        factor = LEARN_RATE * rms_master / jnp.maximum(1.0, rms_update / CLIP_LEVEL)
        by_place = by_place + jnp.where(here, factor, 0.0)
    vout[0] = vec_grad
    vout[1] = vec[...] - by_place * vec_update
    vout[2] = vsq_new
    copies.finish()


def step_kernel(*refs):
    gq, go, g1, g2, acol, acol2, bcol, scal, rowv, rowf, coln, vout, wq, wo, w1, w2 = refs[:16]
    outs = refs[16:]
    grads, masters = [gq, go, g1, g2], [wq, wo, w1, w2]
    offset = 0
    for i, (_, width, _) in enumerate(MATS):
        grad = grads[i][...]
        outs[i][0] = grad
        by_row = acol2[...] if i == 3 else acol[:, i : i + 1]
        update = grad * by_row * bcol[:, offset : offset + width]
        outs[5 + i][0] = masters[i][0] - scal[:, i : i + 1] * update
        offset += width
    outs[4][...] = vout[0]
    outs[9][...] = vout[1]
    outs[10][...] = vout[2]
    outs[11][...] = rowv[...]
    outs[12][...] = rowf[...]
    outs[13][...] = coln[...]


def step_all(sums, masters, vec, vsq, rows_small, rows_fc2, columns, DP, S):
    R = masters[0].shape[1]
    n = vec.shape[1]
    vmem = pl.BlockSpec(memory_space=pltpu.VMEM)
    rounds = len(dp_bits(DP)) + S - 1
    wide = COLS + NV + 128
    shapes = [
        (R, 3 * D),
        (R, D),
        (R, FF),
        (4 * R, D),
        (R, 4),
        (4 * R, 1),
        (1, COLS),
        (1, 128),
        (1, 3, R),
        (1, 4 * R),
        (1, COLS),
        (3, 1, n),
    ]
    found = pl.pallas_call(
        functools.partial(sums_kernel, DP, S, R, n),
        out_shape=tuple(jax.ShapeDtypeStruct(shape, F32) for shape in shapes),
        in_specs=[vmem] * 14,
        out_specs=(vmem,) * len(shapes),
        scratch_shapes=[
            pltpu.VMEM((4 * R, D // 2), F32),
            pltpu.VMEM((R, FF // 2), F32),
            pltpu.VMEM((S, R, 3 * GW), F32),
            pltpu.VMEM((R, D // 2), F32),
            pltpu.VMEM((1, NV), F32),
            pltpu.VMEM((1, wide), F32),
            pltpu.VMEM((rounds, 1, wide), F32),
            pltpu.VMEM((1, 128), F32),
            pltpu.VMEM((rounds, 1, 128), F32),
            pltpu.SemaphoreType.DMA((5 + 2 * rounds,)),
            pltpu.SemaphoreType.DMA((5 + 2 * rounds,)),
        ],
        compiler_params=pltpu.CompilerParams(
            collective_id=2, has_side_effects=True, vmem_limit_bytes=48 << 20
        ),
        name="step_sums",
    )(*sums, *masters, vec, vsq, rows_small, rows_fc2, columns)
    outs = (
        [(1,) + shape for shape in shapes[:4]]
        + [(1, n)]
        + [(1,) + shape for shape in shapes[:4]]
        + [(1, n), (1, n), (1, 3, R), (1, 4 * R), (1, COLS)]
    )
    return pl.pallas_call(
        step_kernel,
        out_shape=tuple(jax.ShapeDtypeStruct(shape, F32) for shape in outs),
        in_specs=[vmem] * 16,
        out_specs=(vmem,) * len(outs),
        compiler_params=pltpu.CompilerParams(vmem_limit_bytes=48 << 20),
        name="step",
    )(*found, *masters)


def local(DP, S, *args):
    (
        block_input,
        cotangent,
        doc_lengths,
        w_qkv,
        w_out,
        w_fc1,
        w_fc2,
        vectors,
        vector_sq,
        rows_small,
        rows_fc2,
        columns,
    ) = args
    c, dp, z = coords()
    first = c == 0
    chunk = block_input.shape[1]
    length = chunk * S
    R = w_qkv.shape[1]
    row = z // (S // 2)
    t = jnp.where(first, z, S - 1 - z)

    by_head = jnp.concatenate(
        [
            part
            for k in range(GROUP)
            for part in [w_qkv[0][:, i * D + k * GW : i * D + (k + 1) * GW] for i in range(3)]
            + [w_out[0][:, k * GW : (k + 1) * GW]]
        ],
        axis=1,
    ).astype(BF)
    shards = [by_head, w_fc1[0].astype(BF), w_fc2[0].astype(BF).reshape(4, R, D)]
    shard_size = vectors.shape[1]
    place_at = (dp * S + z) * shard_size
    wide = window_rows(shard_size, DP * S)
    vwin = lax.dynamic_update_slice(
        jnp.zeros((wide * 128,), F32), vectors[0], (lax.rem(place_at, 128),)
    ).reshape(wide, 128)
    done = forward_all(
        block_input.astype(BF),
        block_input,
        cotangent.astype(BF),
        cotangent,
        doc_lengths,
        shards,
        vwin,
        DP,
        S,
    )
    kept_all = done[6:]
    weights = []
    for layer in range(2):
        qkvo, w1, w2 = done[3 * layer : 3 * layer + 3]
        weights += [qkvo.reshape(D, 4 * D), w1.reshape(D, FF), w2.reshape(4, D, D)]
    saved = list(kept_all)
    saved[1] = saved[1].reshape(2, length, D)
    back = backward_all(weights, saved, doc_lengths, DP, S, R)
    activations, input_grads = back[3][None], back[4][None]
    stepped = step_all(
        back[5:],
        (w_qkv, w_out, w_fc1, w_fc2),
        vectors,
        vector_sq,
        rows_small,
        rows_fc2,
        columns,
        DP,
        S,
    )
    return (activations, input_grads) + tuple(stepped)


def solution(mesh):
    placed = (
        P("dp", "seq", None),
        P("dp", "seq", None),
        P("dp", None),
        P("section", ("dp", "seq"), None),
        P("section", ("dp", "seq"), None),
        P("section", ("dp", "seq"), None),
        P("section", ("dp", "seq"), None),
        P("section", ("dp", "seq")),
        P("section", ("dp", "seq")),
        P("section", None, ("dp", "seq")),
        P("section", ("dp", "seq")),
        P("section", None),
    )
    return jax.shard_map(
        functools.partial(local, mesh.shape["dp"], mesh.shape["seq"]),
        mesh=mesh,
        in_specs=placed,
        out_specs=(
            P("section", "dp", "seq", None),
            P("section", "dp", "seq", None),
            P("section", ("dp", "seq"), None),
            P("section", ("dp", "seq"), None),
            P("section", ("dp", "seq"), None),
            P("section", ("dp", "seq"), None),
            P("section", ("dp", "seq")),
            P("section", ("dp", "seq"), None),
            P("section", ("dp", "seq"), None),
            P("section", ("dp", "seq"), None),
            P("section", ("dp", "seq"), None),
            P("section", ("dp", "seq")),
            P("section", ("dp", "seq")),
            P("section", None, ("dp", "seq")),
            P("section", ("dp", "seq")),
            P("section", None),
        ),
        check_vma=False,
    )
```

```python
import functools

import jax
import jax.numpy as jnp
import numpy as np
from jax import lax
from jax.experimental import pallas as pl
from jax.experimental.pallas import tpu as pltpu
from jax.sharding import PartitionSpec as P

D = 768
FF = 3072
HEADS = 12
HEAD_DIM = 64
STEP = 10
NDOC = 4
NV = 10 * D + 3 * FF
GROUP = 4
GW = D // GROUP
CHUNK_HEADS = HEADS // GROUP

EPSILON = 1e-05
LEARN_RATE = 0.5
CLIP_LEVEL = 1.0
NEG_LARGE = -1e30
MESH = pl.DeviceIdType.MESH
BF = jnp.bfloat16
F32 = jnp.float32


def dp_bits(count):
    return [1 << i for i in range(count.bit_length() - 1)]


def bit_orders(count):
    bits = dp_bits(count)
    half = len(bits) // 2
    return (bits, bits[half:] + bits[:half])


def subsets(bits):
    found = [0]
    for bit in bits:
        found = found + [m | bit for m in found]
    return sorted(found)


class Copies:
    def __init__(self, send, recv):
        self.send, self.recv, self.used, self.started = send, recv, 0, []

    def go(self, src, dst, device):
        at = self.used
        self.used += 1
        copy = pltpu.make_async_remote_copy(
            src_ref=src,
            dst_ref=dst,
            send_sem=self.send.at[at],
            recv_sem=self.recv.at[at],
            device_id=device,
            device_id_type=MESH,
        )
        copy.start()
        self.started.append(copy)
        return copy

    def settle(self, some):
        for copy in some:
            copy.wait_send()
        gone = [id(copy) for copy in some]
        self.started = [copy for copy in self.started if id(copy) not in gone]

    def finish(self):
        self.settle(self.started)


def greet(peers):
    barrier = pltpu.get_barrier_semaphore()
    for peer in peers:
        pl.semaphore_signal(barrier, inc=1, device_id=peer, device_id_type=MESH)
    pl.semaphore_wait(barrier, len(peers))


def coords():
    return lax.axis_index("section"), lax.axis_index("dp"), lax.axis_index("seq")


def near_peers(c, dp, z, DP, S):
    return (
        [(1 - c, dp, z)]
        + [(c, dp, z ^ k) for k in range(1, S)]
        + [(c, dp ^ b, z) for b in dp_bits(DP)]
    )


def half_lanes(c, width):
    return pl.ds(pl.multiple_of(c * width, 128), width)


def sub_lanes(c, width, a):
    return pl.ds(pl.multiple_of(c * width + a * (width // 2), 128), width // 2)


class Locals:
    def __init__(self, sems):
        self.sems, self.used, self.open = sems, 0, []

    def go(self, src, dst):
        copy = pltpu.make_async_copy(src, dst, self.sems.at[self.used])
        self.used += 1
        copy.start()
        return copy

    def keep(self, src, dst):
        self.open.append(self.go(src, dst))

    def finish(self):
        for copy in self.open:
            copy.wait()


def arrive(some):
    for copy in some:
        copy.wait_recv()


def norm(values, gain, bias):
    average = jnp.mean(values, axis=1, keepdims=True)
    centred = values - average
    variance = jnp.mean(centred * centred, axis=1, keepdims=True)
    return centred * lax.rsqrt(variance + EPSILON) * gain + bias


def dot(left, right):
    return lax.dot_general(left, right, (((1,), (0,)), ((), ())), preferred_element_type=F32)


def dot_nt(left, right):
    return lax.dot_general(left, right, (((1,), (1,)), ((), ())), preferred_element_type=F32)


def dot_tn(left, right):
    return lax.dot_general(left, right, (((0,), (0,)), ((), ())), preferred_element_type=F32)


def pick(row_vector, t, width):
    total = jnp.where(t == 0, row_vector[:, 0:width], 0.0)
    for k in range(1, GROUP):
        total = total + jnp.where(t == k, row_vector[:, k * width : (k + 1) * width], 0.0)
    return total


def doc_start(lens, row, at, rows):
    pos = lax.broadcasted_iota(jnp.int32, (rows, 1), 0) + at
    bound = jnp.int32(0)
    start = jnp.zeros((rows, 1), jnp.int32)
    for j in range(NDOC):
        size = lens[row, j]
        bound = bound + size
        start = start + jnp.where(pos >= bound, size, 0)
    return start


PARTS = dict(
    g1=(0, D),
    b1=(D, D),
    bq=(2 * D, D),
    bv=(3 * D, D),
    gs1=(4 * D, D),
    bs1=(5 * D, D),
    bo=(6 * D, D),
    g2=(7 * D, D),
    b2=(8 * D, D),
    bo2=(9 * D, D),
    bf1=(10 * D, FF),
    gs2=(10 * D + FF, FF),
    bs2=(10 * D + 2 * FF, FF),
)


def window_reach(size):
    return -(-(size + 127) // 128) * 128


ORDER = (
    [("z", 1), ("y", 0), ("v", 0), ("1", 0), ("x",), ("z", 2), ("v", 1), ("y", 1), ("2", 0)]
    + [("1", 1), ("v", 2), ("V",), ("y", 2), ("e", 0), ("z", 3), ("2", 1), ("h",), ("1", 2)]
    + [("y", 3), ("z", 4), ("z", 5), ("X",), ("t",), ("c", 0, 0), ("1", 3), ("2", 2)]
    + [("y", 4), ("y", 5), ("e", 1), ("c", 0, 1), ("1", 4), ("c", 1, 0)]
    + [("2", 3), ("e", 2), ("c", 1, 1), ("2", 4), ("1", 5), ("e", 3), ("c", 2, 0), ("c", 3, 0)]
    + [("e", 4), ("c", 3, 1), ("2", 5), ("c", 4, 0), ("c", 4, 1), ("e", 5), ("c", 5, 0)]
)

QW = 640


def forward_kernel(DP, S, R, *refs):
    (xf, cotf, lens, w_qkv, w_out, w_fc1, w_fc2, vec_own) = refs[:8]
    outs = refs[8:16]
    s_x, s_h, s_qkv, s_o, s_lse, s_att, s_a, s_mid, s_n2, s_pre, s_u, s_y, s_vec = refs[16:29]
    s_dy, s_yb = refs[29:31]
    (shq, both_o, both_1, both_2, give_o, give_1, give_2, xb, xr, x_own) = refs[31:41]
    (hrow, qkv, o, lse, att4, att, a, mid, n2, pre, u, y) = refs[41:53]
    (gbuf, wh, wo, w1, w2, vwin, vall, vrow, cotb, cotr, dy, yb) = refs[53:65]
    flats = refs[65:-3]
    send, recv, local = refs[-3:]
    c, dp, z = coords()
    t = jnp.where(c == 0, z, S - 1 - z)
    row = z // (S // 2)
    chunk = xf.shape[1]
    n = vec_own.shape[1]
    order_a, order_b = bit_orders(DP)
    steps = len(order_a)
    copies = Copies(send, recv)
    locs = Locals(local)
    sibling, partner, diagonal = (1 - c, dp, z), (c, dp, z ^ 1), (1 - c, dp, z ^ 1)
    every = slice(None)
    greet(near_peers(c, dp, z, DP, S) + [diagonal])

    for k in range(GROUP):
        for i in range(3):
            shq[c, k, :, i * GW : (i + 1) * GW] = w_qkv[
                0, :, i * D + k * GW : i * D + (k + 1) * GW
            ].astype(BF)
    both_o[c] = w_out[0, :, half_lanes(c, D // 2)].astype(BF)
    give_o[...] = w_out[0, :, half_lanes(1 - c, D // 2)].astype(BF)
    give_a = [
        copies.go(shq.at[c], shq.at[c], sibling),
        copies.go(give_o, both_o.at[c], sibling),
    ]
    both_1[c] = w_fc1[0, :, half_lanes(c, FF // 2)].astype(BF)
    give_1[...] = w_fc1[0, :, half_lanes(1 - c, FF // 2)].astype(BF)
    both_2[c] = w_fc2[0, pl.ds(2 * c, 2)].astype(BF)
    give_2[...] = w_fc2[0, pl.ds(2 * (1 - c), 2)].astype(BF)
    give_b = [
        copies.go(give_1, both_1.at[c], sibling),
        copies.go(give_2, both_2.at[c], sibling),
    ]
    xb[0] = xf[row].astype(BF)
    xb[1] = xf[1 - row].astype(BF)

    half = S // 2

    def pieces(g):
        layer, kind = divmod(g, 3)
        o_q, o_o, o_1, o_2 = outs[4 * layer : 4 * layer + 4]
        if kind == 0:
            return [
                (lambda k: shq.at[layer, t ^ k], lambda lead: o_q.at[lead], False),
                (
                    lambda k: both_o.at[layer],
                    lambda lead: o_o.at[lead + (every, half_lanes(c, D // 2))],
                    True,
                ),
            ]
        if kind == 1:
            return [
                (
                    lambda k: both_1.at[layer],
                    lambda lead: o_1.at[lead + (every, half_lanes(c, FF // 2))],
                    True,
                )
            ]
        return [
            (lambda k: both_2.at[layer], lambda lead: o_2.at[lead + (pl.ds(2 * c, 2),)], True)
        ]

    def sides():
        return ((pl.ds(0, half), order_a), (pl.ds(half, half), order_b))

    cross, own_place, flight = {}, {}, {}
    forwarded = [[] for _ in range(6)]

    def across(g):
        own_place[g] = [locs.go(src(0), place((dp, z))) for src, place, _ in pieces(g)]
        cross[g] = [
            copies.go(src(k), place((dp, z)), (c, dp, z ^ k))
            for src, place, shared in pieces(g)
            for k in ([2] if shared else [3, 2, 1])
        ]

    def across_on(g):
        arrive(cross[g][-1:])
        cross[g] = cross[g][:-1]
        for src, place, shared in pieces(g):
            if shared:
                cross[g].append(copies.go(src(0), place((dp, z)), (c, dp, z ^ 1)))
                there = place((dp, z ^ 2))
                cross[g].append(copies.go(there, there, (c, dp, z ^ 1)))

    def beside(g, step):
        flight[g] = [
            copies.go(place((dp ^ m, part)), place((dp ^ m, part)), (c, dp ^ order[step], z))
            for _, place, _ in pieces(g)
            for part, order in sides()
            for m in subsets(order[:step])
        ]

    def over(g, step):
        for _, place, shared in pieces(g):
            if shared and step < 0:
                spot = place((dp, every))
                forwarded[g].append(copies.go(spot, spot, sibling))
            elif shared:
                for part, order in sides():
                    for m in subsets(order[:step]):
                        spot = place((dp ^ m ^ order[step], part))
                        forwarded[g].append(copies.go(spot, spot, sibling))

    def enter(g):
        if g < 6:
            for copy in own_place[g]:
                copy.wait()
            arrive(cross[g])
            beside(g, 0)
            over(g, -1)

    def middle(g):
        if g < 6:
            for step in range(1, steps):
                arrive(flight[g])
                beside(g, step)
                over(g, step - 1)

    arrive(give_a)
    across(0)
    arrive(give_b)
    x_far = pltpu.make_async_remote_copy(
        src_ref=xb.at[1],
        dst_ref=xr.at[z],
        send_sem=send.at[copies.used],
        recv_sem=recv.at[copies.used],
        device_id=(c, dp, S - 1 - z),
        device_id_type=MESH,
    )
    x_back = pltpu.make_async_remote_copy(
        src_ref=xr.at[S - 1 - z],
        dst_ref=xr.at[S - 1 - z],
        send_sem=send.at[copies.used + 1],
        recv_sem=recv.at[copies.used + 1],
        device_id=sibling,
        device_id_type=MESH,
    )
    copies.used += 2
    place_at = (dp * S + z) * n
    skew = lax.rem(place_at, 128)
    reach = vwin.shape[1]
    vwin[...] = jnp.zeros_like(vwin)
    for at in sorted({(i * n) % 128 for i in range(DP * S)}):
        vwin[:, at : at + n] = jnp.where(skew == at, vec_own[...], vwin[:, at : at + n])
    vec_copies = [
        copies.go(vwin, vall.at[c, dp, z], (c, dp, z ^ k)) for k in range(1, S)
    ]
    vall[c, dp, z] = vwin[...]
    xr[z] = xb[0]
    cotb[...] = cotf[1 - row].astype(BF)

    def vec(layer, name):
        at, size = PARTS[name]
        return vrow[layer, :, at : at + size]

    moving = {}

    def vectors_on(step):
        arrive(moving["vec"] if step else vec_copies)
        while 1 < step < steps:
            vectors_step(step)
            arrive(moving["vec"])
            step += 1
        vectors_step(step)

    def vectors_step(step):
        if step < steps:
            moving["vec"] = [
                copies.go(vall.at[c, dp ^ m], vall.at[c, dp ^ m], (c, dp ^ order_a[step], z))
                for m in subsets(order_a[:step])
            ]
        else:
            moving["vec"] = [copies.go(vall.at[c], vall.at[c], sibling)]

    def vectors_done():
        arrive(moving["vec"])
        for layer in range(2):
            vrow[layer] = jnp.zeros((1, vrow.shape[2]), F32)
            for i in range(DP * S):
                first = i * n // 128 * 128
                vrow[layer, :, first : first + reach] += vall[layer, i // S, i % S]
            vrow[layer] = vrow[layer].astype(BF).astype(F32)
            locs.keep(vrow.at[layer, :, 0:NV], s_vec.at[layer])

    def x_out():
        @pl.when(c == 1)
        def _():
            x_far.start()

    def x_on():
        @pl.when(c == 1)
        def _():
            x_far.wait()
            x_back.start()

        slot = jnp.where(c == 0, z, S - 1 - z)
        moving["x"] = copies.go(xr.at[slot], xr.at[slot], partner)

    def x_done():
        arrive([moving["x"]])
        slot = jnp.where(c == 0, z ^ 1, z ^ 2)
        moving["x"] = copies.go(xr.at[slot], xr.at[slot], sibling)

        @pl.when(c == 1)
        def _():
            x_back.wait_send()

        @pl.when(c == 0)
        def _():
            x_back.wait_recv()

        arrive([moving["x"]])
        x_own[...] = jnp.where(c == 0, xf[row], xr[S - 1 - z].astype(F32))
        locs.keep(x_own, s_x.at[0])

    def to_flat(stage, flat_ref, leads, base=0):
        if flat_ref is None:
            return
        for i, lead in enumerate(leads):
            flat_ref[base + i * R : base + (i + 1) * R, :] = stage[lead]

    shards_at = [(d, e) for d in range(DP) for e in range(S)]
    aligned = R % 16 == 0
    f_wh, f_wo, f_w1, f_w2 = (None,) * 4 if aligned else flats

    def load_a(layer):
        some = [locs.go(outs[4 * layer], wh), locs.go(outs[4 * layer + 1], wo)]
        for copy in some:
            copy.wait()
        to_flat(wh, f_wh, shards_at)
        to_flat(wo, f_wo, shards_at)

    def load_big(source, stage, flat_ref, tail):
        if aligned:
            locs.go(source, stage).wait()
            return
        some = stage.shape[0]
        leads = [(d, e) + j for d in range(some) for e in range(S) for j in tail]
        for q in range(DP // some):
            locs.go(source.at[q * some : (q + 1) * some], stage).wait()
            to_flat(stage, flat_ref, leads, q * len(leads) * R)

    def load_w1(layer):
        load_big(outs[4 * layer + 2], w1, f_w1, [()])

    def load_w2(layer):
        load_big(outs[4 * layer + 3], w2, f_w2, [(j,) for j in range(4)])

    def heads_w():
        return wh[...].reshape(D, QW) if aligned else f_wh[...]

    def out_w():
        return wo[...].reshape(D, D) if aligned else f_wo[...]

    def w1_piece(j):
        lanes = slice(j * D, (j + 1) * D)
        return w1[:, :, :, lanes].reshape(D, D) if aligned else f_w1[:, lanes]

    def w2_piece(j):
        if not aligned:
            return f_w2[j * D : (j + 1) * D, :]
        some = DP // 4
        return w2[j * some : (j + 1) * some].reshape(D, D)

    def project(layer):
        biases = (pick(vec(layer, "bq"), t, GW), None, pick(vec(layer, "bv"), t, GW))
        for b in range(GROUP):
            if layer == 0:
                values = jnp.where(z == b, xf[row], xr[b].astype(F32))
                hrow[0, b] = norm(values, vec(0, "g1"), vec(0, "b1")).astype(BF)
            full = dot(hrow[layer, b], heads_w())
            for i in range(3):
                piece = full[:, i * GW : (i + 1) * GW]
                if biases[i] is not None:
                    piece = piece + biases[i]
                qkv[layer, b * chunk : (b + 1) * chunk, i * GW : (i + 1) * GW] = piece.astype(BF)

    def attention(layer):
        for b in range(GROUP):
            rows = slice(b * chunk, (b + 1) * chunk)
            upto = (b + 1) * chunk
            start = doc_start(lens, row, b * chunk, chunk)
            key = lax.broadcasted_iota(jnp.int32, (chunk, upto), 1)
            query = lax.broadcasted_iota(jnp.int32, (chunk, upto), 0) + b * chunk
            ok = (key >= start) & (key <= query)
            for h in range(CHUNK_HEADS):
                at = h * HEAD_DIM
                q = qkv[layer, rows, at : at + HEAD_DIM]
                k = qkv[layer, 0:upto, GW + at : GW + at + HEAD_DIM]
                v = qkv[layer, 0:upto, 2 * GW + at : 2 * GW + at + HEAD_DIM]
                s = jnp.where(ok, dot_nt(q, k) * HEAD_DIM ** (-0.5), NEG_LARGE)
                top = jnp.max(s, axis=1, keepdims=True)
                e = jnp.exp(s - top)
                total = jnp.sum(e, axis=1, keepdims=True)
                o[layer, b, :, at : at + HEAD_DIM] = (dot(e.astype(BF), v) / total).astype(BF)
                lse[layer, rows, h : h + 1] = top + jnp.log(total)

    waiting = {}

    def share(layer):
        waiting["o"] = [
            copies.go(o.at[layer, t ^ 1], att4.at[layer, t], partner),
            copies.go(o.at[layer, t ^ 3], att4.at[layer, t], sibling),
            copies.go(o.at[layer, t ^ 2], att4.at[layer, t], diagonal),
        ]
        att4[layer, t] = o[layer, t]
        locs.keep(qkv.at[layer], s_qkv.at[layer])
        locs.keep(o.at[layer], s_o.at[layer])
        locs.keep(lse.at[layer], s_lse.at[layer])
        locs.keep(hrow.at[layer], s_h.at[layer])

    def branch(layer):
        x = x_own if layer == 0 else y.at[0]
        arrive(waiting["o"])
        for k in range(GROUP):
            att[layer, :, k * GW : (k + 1) * GW] = att4[layer, k]
        a[layer] = norm(
            att[layer].astype(F32), vec(layer, "gs1"), vec(layer, "bs1")
        ).astype(BF)
        mid[layer] = x[...] + dot(a[layer], out_w()) + vec(layer, "bo")
        n2[layer] = norm(mid[layer], vec(layer, "g2"), vec(layer, "b2")).astype(BF)
        locs.keep(att.at[layer], s_att.at[layer])
        locs.keep(a.at[layer], s_a.at[layer])
        locs.keep(mid.at[layer], s_mid.at[layer])
        locs.keep(n2.at[layer], s_n2.at[layer])

    def inner(layer):
        bf1, gs2, bs2 = vec(layer, "bf1"), vec(layer, "gs2"), vec(layer, "bs2")
        total = jnp.zeros((chunk, 1), F32)
        for j in range(FF // D):
            lanes = slice(j * D, (j + 1) * D)
            f = dot(n2[layer], w1_piece(j)) + bf1[:, lanes]
            pre[layer, :, lanes] = f
            g = 0.5 * f * (1.0 + lax.erf(f * np.float32(np.sqrt(0.5))))
            gbuf[:, lanes] = g
            total = total + jnp.sum(g, axis=1, keepdims=True)
        average = total / FF
        square = jnp.zeros((chunk, 1), F32)
        for j in range(FF // D):
            centred = gbuf[:, j * D : (j + 1) * D] - average
            square = square + jnp.sum(centred * centred, axis=1, keepdims=True)
        scale = lax.rsqrt(square / FF + EPSILON)
        for j in range(FF // D):
            lanes = slice(j * D, (j + 1) * D)
            u[layer, :, lanes] = (
                (gbuf[:, lanes] - average) * scale * gs2[:, lanes] + bs2[:, lanes]
            ).astype(BF)
        locs.keep(pre.at[layer], s_pre.at[layer])
        locs.keep(u.at[layer], s_u.at[layer])

    def outer(layer):
        total = mid[layer] + vec(layer, "bo2")
        for j in range(FF // D):
            total = total + dot(u[layer, :, j * D : (j + 1) * D], w2_piece(j))
        y[layer] = total
        yb[layer] = total.astype(BF)
        locs.keep(yb.at[layer], s_yb.at[layer])
        locs.keep(y.at[layer], s_y.at[layer])

    def pass_on():
        hrow[1, t] = norm(y[0], vec(1, "g1"), vec(1, "b1")).astype(BF)
        waiting["h"] = [
            copies.go(hrow.at[1, t], hrow.at[1, t], partner),
            copies.go(hrow.at[1, t], hrow.at[1, t], sibling),
        ]
        locs.keep(y.at[0], s_x.at[1])

    def row_in():
        arrive(waiting["h"])
        arrive([copies.go(hrow.at[1, t ^ 1], hrow.at[1, t ^ 1], sibling)])

    cot_copy = pltpu.make_async_remote_copy(
        src_ref=cotb,
        dst_ref=cotr,
        send_sem=send.at[copies.used],
        recv_sem=recv.at[copies.used],
        device_id=(c, dp, S - 1 - z),
        device_id_type=MESH,
    )
    copies.used += 1

    def cotangent_out():
        @pl.when(c == 1)
        def _():
            cot_copy.start()

    def cotangent_in():
        @pl.when(c == 1)
        def _():
            cot_copy.wait()
            dy[...] = cotr[...].astype(F32)

        @pl.when(c == 0)
        def _():
            dy[...] = cotf[row]

        locs.keep(dy, s_dy)

    def end(g):
        arrive(flight[g])
        over(g, steps - 1)

    def compute(g, part):
        layer, kind = divmod(g, 3)
        if part == 0:
            arrive(forwarded[g])
        if kind == 0 and part == 0:
            load_a(layer)
            if layer == 1:
                row_in()
            project(layer)
        elif kind == 0:
            attention(layer)
            share(layer)
        elif kind == 1 and part == 0:
            branch(layer)
        elif kind == 1:
            load_w1(layer)
            inner(layer)
        else:
            load_w2(layer)
            outer(layer)
            if layer == 0:
                pass_on()
            else:
                cotangent_in()

    for name, *at in ORDER:
        {
            "z": across,
            "y": across_on,
            "v": vectors_on,
            "V": vectors_done,
            "x": x_out,
            "h": x_on,
            "X": x_done,
            "1": enter,
            "2": middle,
            "e": end,
            "c": compute,
            "t": cotangent_out,
        }[name](*at)
    copies.finish()
    locs.finish()


def forward_all(xf, cotf, lens, masters, vec_own, DP, S):
    R = masters[0].shape[1]
    n = vec_own.shape[1]
    chunk = xf.shape[1]
    length = chunk * S
    gathered = [
        jax.ShapeDtypeStruct((DP, S, R, QW), BF),
        jax.ShapeDtypeStruct((DP, S, R, D), BF),
        jax.ShapeDtypeStruct((DP, S, R, FF), BF),
        jax.ShapeDtypeStruct((DP, S, 4, R, D), BF),
    ] * 2
    kept = [
        ((2, chunk, D), F32),
        ((2, GROUP, chunk, D), BF),
        ((2, length, 3 * GW), BF),
        ((2, GROUP, chunk, GW), BF),
        ((2, length, CHUNK_HEADS), F32),
        ((2, chunk, D), BF),
        ((2, chunk, D), BF),
        ((2, chunk, D), F32),
        ((2, chunk, D), BF),
        ((2, chunk, FF), F32),
        ((2, chunk, FF), BF),
        ((2, chunk, D), F32),
        ((2, 1, NV), F32),
        ((chunk, D), F32),
        ((2, chunk, D), BF),
    ]
    flats = (
        []
        if R % 16 == 0
        else [
            pltpu.VMEM((D, QW), BF),
            pltpu.VMEM((D, D), BF),
            pltpu.VMEM((D, FF), BF),
            pltpu.VMEM((FF, D), BF),
        ]
    )
    staged = DP if R % 16 == 0 else DP // 4
    reach = window_reach(n)
    across = 8 * 3
    beside = 8 * 2 * (DP - 1)
    over = 6 * (1 + 2 * (DP - 1))
    amount = 4 + across + beside + over + (S - 1) + (DP - 1) + 1 + 4 + 2 * 3 + 3 + 1
    anywhere = pl.BlockSpec(memory_space=pl.ANY)
    vmem = pl.BlockSpec(memory_space=pltpu.VMEM)
    return pl.pallas_call(
        functools.partial(forward_kernel, DP, S, R),
        out_shape=tuple(gathered)
        + tuple(jax.ShapeDtypeStruct(shape, kind) for shape, kind in kept),
        in_specs=[vmem] * 2 + [pl.BlockSpec(memory_space=pltpu.SMEM)] + [vmem] * 5,
        out_specs=(anywhere,) * (8 + len(kept)),
        scratch_shapes=[
            pltpu.VMEM((2, GROUP, R, QW), BF),
            pltpu.VMEM((2, R, D // 2), BF),
            pltpu.VMEM((2, R, FF // 2), BF),
            pltpu.VMEM((2, 2, R, D), BF),
            pltpu.VMEM((R, D // 2), BF),
            pltpu.VMEM((R, FF // 2), BF),
            pltpu.VMEM((2, R, D), BF),
            pltpu.VMEM((2, chunk, D), BF),
            pltpu.VMEM((GROUP, chunk, D), BF),
            pltpu.VMEM((chunk, D), F32),
            pltpu.VMEM((2, GROUP, chunk, D), BF),
            pltpu.VMEM((2, length, 3 * GW), BF),
            pltpu.VMEM((2, GROUP, chunk, GW), BF),
            pltpu.VMEM((2, length, CHUNK_HEADS), F32),
            pltpu.VMEM((2, GROUP, chunk, GW), BF),
            pltpu.VMEM((2, chunk, D), BF),
            pltpu.VMEM((2, chunk, D), BF),
            pltpu.VMEM((2, chunk, D), F32),
            pltpu.VMEM((2, chunk, D), BF),
            pltpu.VMEM((2, chunk, FF), F32),
            pltpu.VMEM((2, chunk, FF), BF),
            pltpu.VMEM((2, chunk, D), F32),
            pltpu.VMEM((chunk, FF), F32),
            pltpu.VMEM((DP, S, R, QW), BF),
            pltpu.VMEM((DP, S, R, D), BF),
            pltpu.VMEM((staged, S, R, FF), BF),
            pltpu.VMEM((staged, S, 4, R, D), BF),
            pltpu.VMEM((1, reach), F32),
            pltpu.VMEM((2, DP, S, 1, reach), F32),
            pltpu.VMEM((2, 1, NV + reach), F32),
            pltpu.VMEM((chunk, D), BF),
            pltpu.VMEM((chunk, D), BF),
            pltpu.VMEM((chunk, D), F32),
            pltpu.VMEM((2, chunk, D), BF),
        ]
        + flats
        + [
            pltpu.SemaphoreType.DMA((amount,)),
            pltpu.SemaphoreType.DMA((amount,)),
            pltpu.SemaphoreType.DMA((80,)),
        ],
        compiler_params=pltpu.CompilerParams(
            collective_id=0, has_side_effects=True, vmem_limit_bytes=62 << 20
        ),
        name="forward",
    )(xf, cotf, lens, *masters, vec_own)


def norm_back(values, gain, grads):
    average = jnp.mean(values, axis=1, keepdims=True)
    centred = values - average
    scale = lax.rsqrt(jnp.mean(centred * centred, axis=1, keepdims=True) + EPSILON)
    unit = centred * scale
    by_gain = jnp.sum(grads * unit, axis=0, keepdims=True)
    by_bias = jnp.sum(grads, axis=0, keepdims=True)
    by_unit = grads * gain
    first = jnp.mean(by_unit, axis=1, keepdims=True)
    second = jnp.mean(by_unit * unit, axis=1, keepdims=True)
    return scale * (by_unit - first - unit * second), by_gain, by_bias


def back_order():
    first = ["A", "B", "C", "D", ("p", 0), "E", "F", "G", ("m", 0), "H", ("p", 1), "I", ("p", 2)]
    first += [("J", 0), ("J", 1), ("a", 0), ("J", 2), "K", ("b", 0), "L", "M", ("m", 1)]
    first += [("p", 3), ("m", 2), "N"]
    then = ["A", (1, "c", 0), (1, "a", 1), "B", "C", (1, "a", 2), "D", ("p", 0), (1, "m", 3)]
    then += ["E", (1, "b", 1), (1, "b", 2), "F", (1, "a", 3), ("m", 0), "G", (1, "c", 1)]
    then += [(1, "c", 2), "H", ("p", 1), "I", ("p", 2), ("J", 0), ("a", 0), ("J", 1), ("m", 1)]
    then += [(1, "c", 3), ("J", 2), "K", ("b", 0), "L", "M", ("p", 3), ("m", 2), "N", ("dx",)]
    then += [("a", 1), ("a", 2), ("m", 3), ("c", 0), ("b", 1), ("b", 2), ("a", 3), ("c", 1)]
    then += [("c", 2), ("rows",), ("c", 3)]
    found = [("act",)]
    for layer, some in ((1, first), (0, then)):
        if layer == 0:
            found.append(("one",))
        for item in some:
            if isinstance(item, str):
                found.append((item, layer))
            elif isinstance(item[0], int):
                found.append((item[1], item[0]) + item[2:])
            elif item[0] in ("dx", "rows"):
                found.append(item)
            else:
                found.append((item[0], layer) + item[1:])
    return found


BACK_ORDER = back_order()


def backward_kernel(DP, S, R, *refs):
    wts = refs[:8]
    s_x, s_h, s_qkv, s_o, s_lse, s_att, s_a, s_mid, s_n2, s_pre, s_u, s_y, s_vec = refs[8:21]
    s_dy, s_yb, lens = refs[21:24]
    x_u, x_n2, x_a, act_cross, act_along, r2, r1, rq, ro, gv, dxb, dx_cross, dx_along, dyb = refs[24:38]
    (ub, nb, ab, preb, midb, attb, xb, hb, qkvb, ob, lseb) = refs[38:49]
    (wbig, wob, whb, vrow, dx1b, dub, dfb, sums) = refs[49:57]
    (dyc, dy_sib, df_sib, db_c, db_sib, do_out, do_in, dqkv, dk_acc, dv_acc) = refs[57:67]
    (dh_out, dh_in, dh2_out, dh2_in, ys) = refs[67:72]
    keeps = refs[72:76]
    slot_refs = refs[76:-3]
    send, recv, local = refs[-3:]
    c, dp, z = coords()
    t = jnp.where(c == 0, z, S - 1 - z)
    row = z // (S // 2)
    chunk = s_mid.shape[1]
    order_a, order_b = bit_orders(DP)
    steps = len(order_a)
    copies = Copies(send, recv)
    locs = Locals(local)
    sibling, partner, diagonal = (1 - c, dp, z), (c, dp, z ^ 1), (1 - c, dp, z ^ 1)
    crossing = (1 - c, dp, jnp.where(c == 0, z, S - 1 - z))
    greet(near_peers(c, dp, z, DP, S) + [diagonal, (1 - c, dp, S - 1 - z)])
    hold = {}

    def fetch(name, src, dst):
        hold[name] = locs.go(src, dst)

    def need(*names):
        for name in names:
            hold.pop(name).wait()

    sib = {}
    for layer in (1, 0):
        sib[layer, "u"] = copies.go(s_u.at[layer], x_u.at[layer], sibling)
        sib[layer, "n2"] = copies.go(s_n2.at[layer], x_n2.at[layer], sibling)
        sib[layer, "a"] = copies.go(s_a.at[layer], x_a.at[layer], sibling)

    half = S // 2
    groups = [[0], [1], [2], [3]]
    slots = {}
    at = 0
    for i in range(4):
        for step in range(steps + 2):
            for layer in range(2) if step < steps else [step - steps]:
                slots[layer, i, min(step, steps)] = slot_refs[at]
            at += 1
    results = [r2, r1, ro, rq]
    flights = {}
    sending = {}

    def sides():
        return ((0, order_a), (1, order_b))

    def beside(layer, g, step):
        found = []
        for i in groups[g]:
            for part, order in sides():
                bit = order[step]
                remain = subsets(order[step + 1 :])
                for at_, m in enumerate(remain):
                    found.append(
                        copies.go(
                            keeps[i].at[dp ^ m ^ bit, pl.ds(part * half, half)],
                            slots[layer, i, step].at[part * len(remain) + at_],
                            (c, dp ^ bit, z),
                        )
                    )
        flights[layer, g] = found
        sending.setdefault((layer, g), []).extend(found)

    def merge(layer, g, step):
        arrive(flights[layer, g])
        for i in groups[g]:
            for part, order in sides():
                remain = subsets(order[step + 1 :])
                for at_, m in enumerate(remain):
                    for e in range(half):
                        got = slots[layer, i, step][part * len(remain) + at_, e]
                        place = (dp ^ m, part * half + e)
                        keeps[i][place] = keeps[i][place] + got

    def across(layer, g):
        found = []
        for i in groups[g]:
            got = slots[layer, i, steps]
            if i == 3:
                for k in range(1, S):
                    found.append(
                        copies.go(keeps[i].at[dp, z ^ k], got.at[k - 1], (c, dp, z ^ k))
                    )
                continue
            for k in range(2):
                found.append(
                    copies.go(keeps[i].at[dp, z ^ 1 ^ (2 * k)], got.at[k], (c, dp, z ^ 1))
                )
        flights[layer, g] = found
        sending[layer, g].extend(found)

    def across_on(layer, g):
        if g == 3:
            return
        arrive(flights[layer, g])
        found = []
        for i in groups[g]:
            got = slots[layer, i, steps]
            keeps[i][dp, z ^ 2] = keeps[i][dp, z ^ 2] + got[1]
            found.append(copies.go(keeps[i].at[dp, z ^ 2], got.at[2], (c, dp, z ^ 2)))
        flights[layer, g] = found
        sending[layer, g].extend(found)

    def close(layer, g):
        arrive(flights[layer, g])
        for i in groups[g]:
            got = slots[layer, i, steps]
            own = keeps[i][dp, z].astype(F32)
            if i == 3:
                rq[layer, 0] = own
                for k in range(1, S):
                    rq[layer, k] = got[k - 1].astype(F32)
            else:
                results[i][layer] = own + got[0].astype(F32) + got[2].astype(F32)
        copies.settle(sending.pop((layer, g)))

    def store(i, first, rows, value, lanes=slice(None)):
        value = value.astype(BF)
        size = keeps[i].shape[2]
        if size % 16 == 0:
            d, e = divmod(first // size, S)
            some = rows // size
            if some < S:
                keeps[i][d, e : e + some, :, lanes] = value.reshape(some, size, value.shape[1])
            else:
                keeps[i][d : d + some // S, :, :, lanes] = value.reshape(
                    some // S, S, size, value.shape[1]
                )
            return
        for n in range(rows // size):
            d, e = divmod(first // size + n, S)
            keeps[i][d, e, :, lanes] = value[n * size : (n + 1) * size]

    w_in = {0: wts[:4], 1: wts[4:]}

    def fetch_w2(layer):
        fetch("w2", w_in[layer][3], wbig)

    def fetch_w1(layer):
        for j in range(4):
            fetch(("w1", j), w_in[layer][2].at[:, j * D : (j + 1) * D], wbig.at[j])

    def fetch_u(layer, part):
        lanes = slice(part * (FF // 2), (part + 1) * (FF // 2))
        if part == 0:
            arrive([sib[layer, "u"]])
        fetch("u", s_u.at[layer, :, lanes], ub.at[0])
        fetch("u_sib", x_u.at[layer, :, lanes], ub.at[1])

    def fetch_pre(layer):
        fetch("pre", s_pre.at[layer], preb)

    def fetch_n2(layer):
        arrive([sib[layer, "n2"]])
        fetch("n2", s_n2.at[layer], nb.at[0])
        fetch("n2_sib", x_n2.at[layer], nb.at[1])

    def fetch_a(layer):
        arrive([sib[layer, "a"]])
        fetch("a", s_a.at[layer], ab.at[0])
        fetch("a_sib", x_a.at[layer], ab.at[1])

    def fetch_mid(layer):
        fetch("mid", s_mid.at[layer], midb)

    def fetch_att(layer):
        fetch("att", s_att.at[layer], attb)
        fetch("wo", w_in[layer][1], wob)

    def fetch_heads(layer):
        fetch("qkv", s_qkv.at[layer], qkvb)
        fetch("o", s_o.at[layer], ob)
        fetch("lse", s_lse.at[layer], lseb)

    def fetch_h(layer):
        fetch("h", s_h.at[layer], hb)
        fetch("wh", w_in[layer][0], whb)
        fetch("x", s_x.at[layer], xb)

    def vec(layer, name):
        at_, size = PARTS[name]
        return vrow[layer, :, at_ : at_ + size]

    def put(layer, name, value, offset=0):
        at_ = PARTS[name][0] + offset
        gv[layer, :, at_ : at_ + value.shape[1]] = value

    def columns_of(value):
        return jnp.sum(value.astype(F32), axis=0, keepdims=True)

    def mine(ref, width, core):
        return ref[:, pl.ds(pl.multiple_of(core * width, 128), width)]

    def attention_back(layer, h):
        scale = HEAD_DIM ** (-0.5)
        low = h * HEAD_DIM
        lanes = slice(low, low + HEAD_DIM)
        klanes = slice(GW + low, GW + low + HEAD_DIM)
        vlanes = slice(2 * GW + low, 2 * GW + low + HEAD_DIM)
        for b in reversed(range(GROUP)):
            rows = slice(b * chunk, (b + 1) * chunk)
            upto = (b + 1) * chunk
            start = doc_start(lens, row, b * chunk, chunk)
            key = lax.broadcasted_iota(jnp.int32, (chunk, upto), 1)
            query = lax.broadcasted_iota(jnp.int32, (chunk, upto), 0) + b * chunk
            ok = (key >= start) & (key <= query)
            q = qkvb[rows, lanes]
            k = qkvb[0:upto, klanes]
            v = qkvb[0:upto, vlanes]
            do = do_in[layer, b, :, lanes]
            delta = jnp.sum(
                do.astype(F32) * ob[b, :, lanes].astype(F32), axis=1, keepdims=True
            )
            s = jnp.where(ok, dot_nt(q, k) * scale, NEG_LARGE)
            p = jnp.exp(s - lseb[rows, h : h + 1])
            ds = (p * (dot_nt(do, v) - delta)).astype(BF)
            dqkv[rows, lanes] = (dot(ds, k) * scale).astype(BF)
            dk, dv = dot_tn(ds, q), dot_tn(p.astype(BF), do)
            if b == GROUP - 1:
                dk_acc[...] = dk
                dv_acc[...] = dv
            else:
                dk_acc[0:upto, :] += dk
                dv_acc[0:upto, :] += dv
        dqkv[:, klanes] = (dk_acc[...] * scale).astype(BF)
        dqkv[:, vlanes] = dv_acc[...].astype(BF)

    def inner_back(layer, part):
        block = 32
        if part == 0:
            sums[...] = jnp.zeros_like(sums)
        gs2 = vec(layer, "gs2")

        def fold(value):
            return jnp.sum(value.reshape(block // 8, 8, FF), axis=0)

        def one(i, carry):
            rows = pl.ds(pl.multiple_of(i * block + part * (chunk // 2), block), block)
            f = preb[rows, :]
            bell = 0.5 * (1.0 + lax.erf(f * np.float32(np.sqrt(0.5))))
            g = f * bell
            average = jnp.mean(g, axis=1, keepdims=True)
            centred = g - average
            scale = lax.rsqrt(jnp.mean(centred * centred, axis=1, keepdims=True) + EPSILON)
            unit = centred * scale
            du = dub[pl.ds(pl.multiple_of(i * block, block), block), :]
            sums[0] += fold(du * unit)
            sums[1] += fold(du)
            by_unit = du * gs2
            first = jnp.mean(by_unit, axis=1, keepdims=True)
            second = jnp.mean(by_unit * unit, axis=1, keepdims=True)
            dg = scale * (by_unit - first - unit * second)
            slope = bell + f * jnp.exp(-0.5 * f * f) * np.float32(1.0 / np.sqrt(2.0 * np.pi))
            df = (dg * slope).astype(BF)
            dfb[rows, :] = df
            sums[2] += fold(df.astype(F32))
            return carry

        lax.fori_loop(0, chunk // 2 // block, one, 0)
        if part == 0:
            return
        put(layer, "gs2", jnp.sum(sums[0], axis=0, keepdims=True))
        put(layer, "bs2", jnp.sum(sums[1], axis=0, keepdims=True))
        put(layer, "bf1", jnp.sum(sums[2], axis=0, keepdims=True))

    went = {}

    def inner_grads(layer, part):
        rows = slice(part * (chunk // 2), (part + 1) * (chunk // 2))
        for j in range(4):
            dub[:, j * D : (j + 1) * D] = dot_nt(dyc[rows, :], wbig[j])

    def part_a(layer):
        dyc[...] = dyb[...].astype(BF)
        went["dy"] = copies.go(
            dyc.at[:, half_lanes(1 - c, D // 2)], dy_sib.at[layer], sibling
        )
        put(layer, "bo2", columns_of(dyc[...]))
        need("w2")
        inner_grads(layer, 0)

    def fc2_grads(layer, part):
        need("u", "u_sib")
        for j in range(4):
            lanes = slice(j * (D // 2), (j + 1) * (D // 2))
            value = dot_tn(ub[0, :, lanes], mine(dyc, D // 2, c)) + dot_tn(
                ub[1, :, lanes], dy_sib[layer]
            )
            store(0, part * (FF // 2) + j * (D // 2), D // 2, value)

    def part_b(layer):
        arrive([went["dy"]])
        fc2_grads(layer, 0)
        fetch_u(layer, 1)

    def part_c(layer):
        need("pre")
        inner_back(layer, 0)

    def part_d(layer):
        fc2_grads(layer, 1)
        if layer == 1:
            fetch_u(0, 0)

    def part_e(layer):
        inner_grads(layer, 1)
        fetch_w1(layer)
        inner_back(layer, 1)
        went["df"] = copies.go(
            dfb.at[:, half_lanes(1 - c, FF // 2)], df_sib.at[layer], sibling
        )
        if layer == 1:
            fetch_pre(0)

    def part_f(layer):
        total = jnp.zeros((chunk, D), F32)
        for j in range(4):
            need(("w1", j))
            total = total + dot_nt(dfb[:, j * D : (j + 1) * D], wbig[j])
        if layer == 1:
            fetch_w2(0)
        need("mid")
        part, by_gain, by_bias = norm_back(midb[...], vec(layer, "g2"), total)
        put(layer, "g2", by_gain)
        put(layer, "b2", by_bias)
        dx1b[...] = dyb[...] + part
        db_c[...] = dx1b[...].astype(BF)
        went["db"] = copies.go(
            db_c.at[:, half_lanes(1 - c, D // 2)], db_sib.at[layer], sibling
        )
        put(layer, "bo", columns_of(db_c[...]))
        if layer == 1:
            fetch_mid(0)

    def part_g(layer):
        need("att", "wo")
        da = dot_nt(db_c[...], wob[...])
        part, by_gain, by_bias = norm_back(attb[...].astype(F32), vec(layer, "gs1"), da)
        put(layer, "gs1", by_gain)
        put(layer, "bs1", by_bias)
        do = part.astype(BF)
        for k in range(GROUP):
            do_out[k] = do[:, k * GW : (k + 1) * GW]
        went["do"] = [
            copies.go(do_out.at[t ^ 1], do_in.at[layer, t], partner),
            copies.go(do_out.at[t ^ 3], do_in.at[layer, t], sibling),
            copies.go(do_out.at[t ^ 2], do_in.at[layer, t], diagonal),
        ]
        do_in[layer, t] = do_out[t]
        if layer == 1:
            fetch_att(0)

    def part_h(layer):
        need("n2", "n2_sib")
        arrive([went["df"]])
        for j in range(2):
            lanes = slice(j * (D // 2), (j + 1) * (D // 2))
            for k in range(2):
                there = pl.ds(pl.multiple_of(c * (FF // 2) + k * D, 128), D)
                value = dot_tn(nb[0, :, lanes], dfb[:, there]) + dot_tn(
                    nb[1, :, lanes], df_sib[layer, :, k * D : (k + 1) * D]
                )
                store(1, j * (D // 2), D // 2, value, slice(k * D, (k + 1) * D))
        if layer == 1:
            fetch_n2(0)

    def part_i(layer):
        need("a", "a_sib")
        arrive([went["db"]])
        for j in range(2):
            lanes = slice(j * (D // 2), (j + 1) * (D // 2))
            value = dot_tn(ab[0, :, lanes], mine(db_c, D // 2, c)) + dot_tn(
                ab[1, :, lanes], db_sib[layer]
            )
            store(2, j * (D // 2), D // 2, value)
        if layer == 1:
            fetch_a(0)

    def part_j(layer, h):
        if h == 0:
            need("qkv", "o", "lse")
            arrive(went["do"])
            copies.settle(went["do"] + [went["dy"], went["df"], went["db"]])
        attention_back(layer, h)
        if layer == 1 and h == CHUNK_HEADS - 1:
            fetch_heads(0)

    def partial(k):
        rows = pl.ds(pl.multiple_of((t ^ k) * chunk, chunk), chunk)
        return dot_nt(dqkv[rows, :], whb[:, 0 : 3 * GW])

    def part_k(layer):
        need("wh")
        dh_out[0] = partial(3).astype(BF)
        dh_out[1] = partial(2).astype(BF)
        went["dh"] = copies.go(dh_out, dh_in.at[layer], sibling)

    def part_l(layer):
        arrive([went["dh"]])
        dh2_out[...] = (partial(1) + dh_in[layer, 1].astype(F32)).astype(BF)
        went["dh2"] = copies.go(dh2_out, dh2_in.at[layer], partner)

    def part_m(layer):
        need("h")
        for j in range(2):
            lanes = slice(j * (D // 2), (j + 1) * (D // 2))
            value = dot_tn(hb[:, lanes], dqkv[...])
            store(3, j * (D // 2), D // 2, value)
        sums_q = columns_of(dqkv[...])
        for k in range(GROUP):
            here = t == k
            put(layer, "bq", jnp.where(here, sums_q[:, 0:GW], 0.0), k * GW)
            put(layer, "bv", jnp.where(here, sums_q[:, 2 * GW : 3 * GW], 0.0), k * GW)

    def part_n(layer):
        need("x")
        dh = partial(0) + dh_in[layer, 0].astype(F32)
        arrive([went["dh2"]])
        dh = dh + dh2_in[layer].astype(F32)
        part, by_gain, by_bias = norm_back(xb[...], vec(layer, "g1"), dh)
        put(layer, "g1", by_gain)
        put(layer, "b1", by_bias)
        dyb[...] = dx1b[...] + part
        copies.settle([went["dh"], went["dh2"]])
        dxb[layer] = dyb[...].astype(BF)
        if layer == 1:
            fetch_h(0)

    def once(src, dst, device):
        at_ = copies.used
        copies.used += 1
        return pltpu.make_async_remote_copy(
            src_ref=src,
            dst_ref=dst,
            send_sem=send.at[at_],
            recv_sem=recv.at[at_],
            device_id=device,
            device_id_type=MESH,
        )

    act_one = once(s_yb.at[1], act_along, (c, dp, S - 1 - z))
    dx_one = once(dxb.at[1], dx_along, (c, dp, S - 1 - z))
    rows_sent = {}

    def act_out():
        rows_sent["act"] = copies.go(s_yb.at[1 - c], act_cross, crossing)

        @pl.when(c == 1)
        def _():
            act_one.start()

    def dx_one_out():
        @pl.when(c == 1)
        def _():
            dx_one.start()

    def dx_out():
        ys[...] = jnp.where(c == 0, dxb[1], dxb[0])
        rows_sent["dx"] = copies.go(ys, dx_cross, crossing)

    def rows_in():
        arrive([rows_sent["act"], rows_sent["dx"]])

        @pl.when(c == 1)
        def _():
            act_one.wait()
            dx_one.wait()

    fetch("dy", s_dy, dyb)
    fetch("vec", s_vec, vrow)
    fetch_w2(1)
    fetch_u(1, 0)
    fetch_pre(1)
    fetch_mid(1)
    fetch_att(1)
    fetch_n2(1)
    fetch_a(1)
    fetch_heads(1)
    fetch_h(1)
    need("dy", "vec")

    def middle(layer, g):
        for step in range(steps - 1):
            merge(layer, g, step)
            beside(layer, g, step + 1)

    def final(layer, g):
        merge(layer, g, steps - 1)
        across(layer, g)

    for name, *at_ in BACK_ORDER:
        {
            "A": part_a,
            "B": part_b,
            "C": part_c,
            "D": part_d,
            "E": part_e,
            "F": part_f,
            "G": part_g,
            "H": part_h,
            "I": part_i,
            "J": part_j,
            "K": part_k,
            "L": part_l,
            "M": part_m,
            "N": part_n,
            "p": lambda layer, g: beside(layer, g, 0),
            "m": middle,
            "a": final,
            "b": across_on,
            "c": close,
            "act": act_out,
            "one": dx_one_out,
            "dx": dx_out,
            "rows": rows_in,
        }[name](*at_)
    copies.finish()
    locs.finish()


def backward_all(weights, saved, lens, DP, S, R):
    chunk = saved[7].shape[1]
    length = chunk * S
    steps = len(dp_bits(DP))
    tails = [(4 * R, D // 2), (R, FF // 2), (R, D // 2), (R, 3 * GW)]
    slots = []
    for tail in tails:
        for step in range(steps):
            slots.append(pltpu.VMEM((2 * (DP >> (step + 1)), S // 2) + tail, BF))
        slots.extend([pltpu.VMEM((S - 1,) + tail, BF)] * 2)
    anywhere = pl.BlockSpec(memory_space=pl.ANY)
    vmem = pl.BlockSpec(memory_space=pltpu.VMEM)
    outs = [
        ((2, chunk, FF), BF, anywhere),
        ((2, chunk, D), BF, anywhere),
        ((2, chunk, D), BF, anywhere),
        ((chunk, D), BF, anywhere),
        ((chunk, D), BF, anywhere),
        ((2,) + tails[0], F32, vmem),
        ((2,) + tails[1], F32, vmem),
        ((2, S) + tails[3], F32, vmem),
        ((2,) + tails[2], F32, vmem),
        ((2, 1, NV), F32, vmem),
        ((2, chunk, D), BF, vmem),
        ((chunk, D), BF, anywhere),
        ((chunk, D), BF, anywhere),
        ((chunk, D), F32, vmem),
    ]
    amount = 6 + 2 * (4 * (2 * (DP - 1) + S - 1) + 3 + 3 + 2) + 4
    return pl.pallas_call(
        functools.partial(backward_kernel, DP, S, R),
        out_shape=tuple(jax.ShapeDtypeStruct(shape, kind) for shape, kind, _ in outs),
        in_specs=[anywhere] * (8 + len(saved)) + [pl.BlockSpec(memory_space=pltpu.SMEM)],
        out_specs=tuple(spec for _, _, spec in outs),
        scratch_shapes=[
            pltpu.VMEM((2, chunk, FF // 2), BF),
            pltpu.VMEM((2, chunk, D), BF),
            pltpu.VMEM((2, chunk, D), BF),
            pltpu.VMEM((chunk, FF), F32),
            pltpu.VMEM((chunk, D), F32),
            pltpu.VMEM((chunk, D), BF),
            pltpu.VMEM((chunk, D), F32),
            pltpu.VMEM((length, D), BF),
            pltpu.VMEM((length, 3 * GW), BF),
            pltpu.VMEM((GROUP, chunk, GW), BF),
            pltpu.VMEM((length, CHUNK_HEADS), F32),
            pltpu.VMEM((4, D, D), BF),
            pltpu.VMEM((D, D), BF),
            pltpu.VMEM((D, QW), BF),
            pltpu.VMEM((2, 1, NV), F32),
            pltpu.VMEM((chunk, D), F32),
            pltpu.VMEM((chunk // 2, FF), F32),
            pltpu.VMEM((chunk, FF), BF),
            pltpu.VMEM((3, 8, FF), F32),
            pltpu.VMEM((chunk, D), BF),
            pltpu.VMEM((2, chunk, D // 2), BF),
            pltpu.VMEM((2, chunk, FF // 2), BF),
            pltpu.VMEM((chunk, D), BF),
            pltpu.VMEM((2, chunk, D // 2), BF),
            pltpu.VMEM((GROUP, chunk, GW), BF),
            pltpu.VMEM((2, GROUP, chunk, GW), BF),
            pltpu.VMEM((length, 3 * GW), BF),
            pltpu.VMEM((length, HEAD_DIM), F32),
            pltpu.VMEM((length, HEAD_DIM), F32),
            pltpu.VMEM((2, chunk, D), BF),
            pltpu.VMEM((2, 2, chunk, D), BF),
            pltpu.VMEM((chunk, D), BF),
            pltpu.VMEM((2, chunk, D), BF),
            pltpu.VMEM((chunk, D), BF),
        ]
        + [pltpu.VMEM((DP, S) + tail, BF) for tail in tails]
        + slots
        + [
            pltpu.SemaphoreType.DMA((amount,)),
            pltpu.SemaphoreType.DMA((amount,)),
            pltpu.SemaphoreType.DMA((80,)),
        ],
        compiler_params=pltpu.CompilerParams(
            collective_id=1, has_side_effects=True, vmem_limit_bytes=63 << 20
        ),
        name="backward",
    )(*weights, *saved, lens)


MATS = [("q", 3 * D, D), ("o", D, D), ("1", FF, D), ("2", D, FF)]
COLS = 3 * D + D + FF + D
DECAY = 1.0 - STEP ** (-0.8)


def total_of(value):
    return jnp.sum(jnp.sum(value, axis=1, keepdims=True), axis=0, keepdims=True)


def lanes_of(values, width=128):
    lane = lax.broadcasted_iota(jnp.int32, (1, width), 1)
    row = jnp.zeros((1, width), F32)
    for i, value in enumerate(values):
        row = row + jnp.where(lane == i, value, 0.0)
    return row


def square_mask(size):
    shape = (size, size)
    return lax.broadcasted_iota(jnp.int32, shape, 0) == lax.broadcasted_iota(jnp.int32, shape, 1)


def upright(row_vector):
    size = row_vector.shape[1]
    return jnp.sum(jnp.where(square_mask(size), row_vector, 0.0), axis=1, keepdims=True)


def level(column):
    size = column.shape[0]
    return jnp.sum(jnp.where(square_mask(size), column, 0.0), axis=0, keepdims=True)


def sums_kernel(DP, S, R, n, *refs):
    r2, r1, rq, ro, gv, wq, wo, w1, w2, vec, vsq, rows_small, rows_fc2, columns = refs[:14]
    gq, go, g1, g2, acol, acol2, bcol, scal, rowv, rowf, coln, vout = refs[14:26]
    got2, got1, gotq, goto, gotv, mine, slots, mine2, slots2, send, recv = refs[26:]
    c, dp, z = coords()
    t = jnp.where(c == 0, z, S - 1 - z)
    sibling = (1 - c, dp, z)
    copies = Copies(send, recv)
    greet(near_peers(c, dp, z, DP, S))
    other = 1 - c
    swaps = [
        copies.go(r2.at[other], got2, sibling),
        copies.go(r1.at[other], got1, sibling),
        copies.go(rq.at[other], gotq, sibling),
        copies.go(ro.at[other], goto, sibling),
        copies.go(gv.at[other], gotv, sibling),
    ]

    def over_devices(value, here, slots_):
        for step, bit in enumerate(dp_bits(DP)):
            here[...] = value
            copy = copies.go(here, slots_.at[step], (c, dp ^ bit, z))
            arrive([copy])
            copies.settle([copy])
            value = value + slots_[step]
        here[...] = value
        first = len(dp_bits(DP))
        some = [
            copies.go(here, slots_.at[first + k - 1], (c, dp, z ^ k)) for k in range(1, S)
        ]
        arrive(some)
        for k in range(1, S):
            value = value + slots_[first + k - 1]
        copies.settle(some)
        return value

    masters = [wq, wo, w1, w2]
    weight_terms = [total_of(w[0] * w[0]) for w in masters]
    place_at = (dp * S + z) * n
    pos = lax.broadcasted_iota(jnp.int32, (1, n), 1) + place_at
    inside = [
        (pos >= at) & (pos < at + size) for at, size in PARTS.values()
    ]
    vec_weights = [
        jnp.sum(jnp.where(here, vec[...] * vec[...], 0.0), axis=1, keepdims=True)
        for here in inside
    ]

    arrive(swaps)
    wide = half_lanes(c, D // 2), half_lanes(1 - c, D // 2)
    g2[:, wide[0]] = r2[c]
    g2[:, wide[1]] = got2[...]
    go[:, wide[0]] = ro[c]
    go[:, wide[1]] = goto[...]
    g1[:, half_lanes(c, FF // 2)] = r1[c]
    g1[:, half_lanes(1 - c, FF // 2)] = got1[...]
    for k in range(GROUP):
        value = rq[c, t ^ k] + gotq[t ^ 3 ^ k]
        for i in range(3):
            gq[:, i * D + k * GW : i * D + (k + 1) * GW] = value[:, i * GW : (i + 1) * GW]
    grads = [gq, go, g1, g2]

    row_news = []
    col_parts = []
    for i, (_, width, _) in enumerate(MATS):
        squares = grads[i][...] * grads[i][...]
        old = upright(rows_fc2[...] if i == 3 else rows_small[0, i : i + 1, :])
        row_news.append(
            DECAY * old + (1.0 - DECAY) * (jnp.sum(squares, axis=1, keepdims=True) / width)
        )
        col_parts.append(jnp.sum(squares, axis=0, keepdims=True))
        if i == 3:
            rowf[...] = level(row_news[3])
        else:
            rowv[0, i : i + 1, :] = level(row_news[i])
    row_terms = [jnp.sum(row_new, axis=0, keepdims=True) for row_new in row_news]
    value = jnp.concatenate(
        col_parts + [gv[c] + gotv[...], lanes_of(weight_terms + row_terms + vec_weights)],
        axis=1,
    )
    value = over_devices(value, mine, slots)
    numbers = value[:, COLS + NV :]

    def number(i):
        return numbers[:, i : i + 1]

    base = pl.multiple_of(place_at // 128 * 128, 128)
    reach = -(-(n + 127) // 128) * 128
    mine[:, COLS : COLS + NV] = value[:, COLS : COLS + NV]
    window = mine[:, pl.ds(COLS + base, reach)]
    skew = place_at - base
    vec_grad = jnp.zeros((1, n), F32)
    for at in sorted({(i * n) % 128 for i in range(DP * S)}):
        vec_grad = vec_grad + jnp.where(skew == at, window[:, at : at + n], 0.0)
    vsq_new = DECAY * vsq[...] + (1.0 - DECAY) * vec_grad * vec_grad
    vec_update = vec_grad * lax.rsqrt(vsq_new)

    terms = []
    offset = 0
    for i, (_, width, count) in enumerate(MATS):
        col_new = (
            DECAY * columns[:, offset : offset + width]
            + (1.0 - DECAY) * value[:, offset : offset + width] / count
        )
        coln[:, offset : offset + width] = col_new
        by_col = lax.rsqrt(col_new)
        bcol[:, offset : offset + width] = by_col
        offset += width
        by_row = lax.rsqrt(row_news[i] / (number(4 + i) / count))
        if i == 3:
            acol2[...] = by_row
        else:
            acol[:, i : i + 1] = by_row
        update = grads[i][...] * by_row * by_col
        terms.append(total_of(update * update))
    terms += [
        jnp.sum(jnp.where(here, vec_update * vec_update, 0.0), axis=1, keepdims=True)
        for here in inside
    ]
    second = over_devices(lanes_of(terms), mine2, slots2)
    factors = []
    for i, (_, width, count) in enumerate(MATS):
        size = width * count
        rms_update = jnp.sqrt(second[:, i : i + 1] / size)
        rms_master = jnp.sqrt(number(i) / size)
        factors.append(LEARN_RATE * rms_master / jnp.maximum(1.0, rms_update / CLIP_LEVEL))
    scal[...] = lanes_of(factors)
    by_place = jnp.zeros((1, n), F32)
    for j, (here, (_, size)) in enumerate(zip(inside, PARTS.values())):
        rms_update = jnp.sqrt(second[:, 4 + j : 5 + j] / size)
        rms_master = jnp.sqrt(number(8 + j) / size)
        factor = LEARN_RATE * rms_master / jnp.maximum(1.0, rms_update / CLIP_LEVEL)
        by_place = by_place + jnp.where(here, factor, 0.0)
    vout[0] = vec_grad
    vout[1] = vec[...] - by_place * vec_update
    vout[2] = vsq_new
    copies.finish()


def step_kernel(S, *refs):
    gq, go, g1, g2, acol, acol2, bcol, scal, rowv, rowf, coln, vout, wq, wo, w1, w2 = refs[:16]
    y, act_cross, act_along, dx, dx_cross, dx_along = refs[16:22]
    outs = refs[22:]
    c, z = lax.axis_index("section"), lax.axis_index("seq")
    row = z // (S // 2)
    for out, own, cross, along in (
        (outs[14], y[0], act_cross, act_along),
        (outs[15], dx[...], dx_cross, dx_along),
    ):
        crossed = cross[...].astype(F32)
        out[0, row] = jnp.where(c == 0, own, crossed)
        out[0, 1 - row] = jnp.where(c == 0, crossed, along[...].astype(F32))
    grads, masters = [gq, go, g1, g2], [wq, wo, w1, w2]
    offset = 0
    for i, (_, width, _) in enumerate(MATS):
        grad = grads[i][...]
        outs[i][0] = grad
        by_row = acol2[...] if i == 3 else acol[:, i : i + 1]
        update = grad * by_row * bcol[:, offset : offset + width]
        outs[5 + i][0] = masters[i][0] - scal[:, i : i + 1] * update
        offset += width
    outs[4][...] = vout[0]
    outs[9][...] = vout[1]
    outs[10][...] = vout[2]
    outs[11][...] = rowv[...]
    outs[12][...] = rowf[...]
    outs[13][...] = coln[...]


def step_all(sums, masters, vec, vsq, rows_small, rows_fc2, columns, rows, DP, S):
    R = masters[0].shape[1]
    n = vec.shape[1]
    vmem = pl.BlockSpec(memory_space=pltpu.VMEM)
    rounds = len(dp_bits(DP)) + S - 1
    wide = COLS + NV + 128
    shapes = [
        (R, 3 * D),
        (R, D),
        (R, FF),
        (4 * R, D),
        (R, 4),
        (4 * R, 1),
        (1, COLS),
        (1, 128),
        (1, 3, R),
        (1, 4 * R),
        (1, COLS),
        (3, 1, n),
    ]
    found = pl.pallas_call(
        functools.partial(sums_kernel, DP, S, R, n),
        out_shape=tuple(jax.ShapeDtypeStruct(shape, F32) for shape in shapes),
        in_specs=[vmem] * 14,
        out_specs=(vmem,) * len(shapes),
        scratch_shapes=[
            pltpu.VMEM((4 * R, D // 2), F32),
            pltpu.VMEM((R, FF // 2), F32),
            pltpu.VMEM((S, R, 3 * GW), F32),
            pltpu.VMEM((R, D // 2), F32),
            pltpu.VMEM((1, NV), F32),
            pltpu.VMEM((1, wide), F32),
            pltpu.VMEM((rounds, 1, wide), F32),
            pltpu.VMEM((1, 128), F32),
            pltpu.VMEM((rounds, 1, 128), F32),
            pltpu.SemaphoreType.DMA((5 + 2 * rounds,)),
            pltpu.SemaphoreType.DMA((5 + 2 * rounds,)),
        ],
        compiler_params=pltpu.CompilerParams(
            collective_id=2, has_side_effects=True, vmem_limit_bytes=48 << 20
        ),
        name="step_sums",
    )(*sums, *masters, vec, vsq, rows_small, rows_fc2, columns)
    outs = (
        [(1,) + shape for shape in shapes[:4]]
        + [(1, n)]
        + [(1,) + shape for shape in shapes[:4]]
        + [(1, n), (1, n), (1, 3, R), (1, 4 * R), (1, COLS)]
        + [(1,) + rows[0].shape] * 2
    )
    return pl.pallas_call(
        functools.partial(step_kernel, S),
        out_shape=tuple(jax.ShapeDtypeStruct(shape, F32) for shape in outs),
        in_specs=[vmem] * 22,
        out_specs=(vmem,) * len(outs),
        compiler_params=pltpu.CompilerParams(vmem_limit_bytes=48 << 20),
        name="step",
    )(*found, *masters, *rows)


def local(DP, S, *args):
    (
        block_input,
        cotangent,
        doc_lengths,
        w_qkv,
        w_out,
        w_fc1,
        w_fc2,
        vectors,
        vector_sq,
        rows_small,
        rows_fc2,
        columns,
    ) = args
    chunk = block_input.shape[1]
    length = chunk * S
    R = w_qkv.shape[1]
    masters = (w_qkv, w_out, w_fc1, w_fc2.reshape(1, 4, R, D))
    done = forward_all(block_input, cotangent, doc_lengths, masters, vectors, DP, S)
    kept_all = done[8:]
    weights = []
    for layer in range(2):
        wq, wo, w1, w2 = done[4 * layer : 4 * layer + 4]
        weights += [wq.reshape(D, QW), wo.reshape(D, D), w1.reshape(D, FF), w2.reshape(4, D, D)]
    saved = list(kept_all)
    saved[1] = saved[1].reshape(2, length, D)
    back = backward_all(weights, saved, doc_lengths, DP, S, R)
    stepped = step_all(
        back[5:10],
        (w_qkv, w_out, w_fc1, w_fc2),
        vectors,
        vector_sq,
        rows_small,
        rows_fc2,
        columns,
        (kept_all[11], back[3], back[4], back[13], back[11], back[12]),
        DP,
        S,
    )
    return (stepped[14], stepped[15]) + tuple(stepped[:14])


def solution(mesh):
    placed = (
        P("dp", "seq", None),
        P("dp", "seq", None),
        P("dp", None),
        P("section", ("dp", "seq"), None),
        P("section", ("dp", "seq"), None),
        P("section", ("dp", "seq"), None),
        P("section", ("dp", "seq"), None),
        P("section", ("dp", "seq")),
        P("section", ("dp", "seq")),
        P("section", None, ("dp", "seq")),
        P("section", ("dp", "seq")),
        P("section", None),
    )
    return jax.shard_map(
        functools.partial(local, mesh.shape["dp"], mesh.shape["seq"]),
        mesh=mesh,
        in_specs=placed,
        out_specs=(
            P("section", "dp", "seq", None),
            P("section", "dp", "seq", None),
            P("section", ("dp", "seq"), None),
            P("section", ("dp", "seq"), None),
            P("section", ("dp", "seq"), None),
            P("section", ("dp", "seq"), None),
            P("section", ("dp", "seq")),
            P("section", ("dp", "seq"), None),
            P("section", ("dp", "seq"), None),
            P("section", ("dp", "seq"), None),
            P("section", ("dp", "seq"), None),
            P("section", ("dp", "seq")),
            P("section", ("dp", "seq")),
            P("section", None, ("dp", "seq")),
            P("section", ("dp", "seq")),
            P("section", None),
        ),
        check_vma=False,
    )
```
